32 devices in a mesh: sec: 4 (over y, core), blk: 8 (over z, x).
Axes of the slice: x: 2, y: 2, z: 4, core: 2. Of those that a mesh axis runs over, the one named last changes fastest.
Arguments:
- fluid_temp: float32 [8, 256, 1024], P(None, 'sec', 'blk'), may hold values from -6 to 6
- stream_velocity: float32 [8, 256, 1024], P(None, 'sec', 'blk'), may hold values from 0.2 to 1
- pitch_velocity: float32 [8, 256, 1024], P(None, 'sec', 'blk'), may hold values from -0.5 to 0.5
- film_coeff: float32 [256, 1024], P('sec', 'blk'), may hold values from 0.1 to 0.3
- solid_temp: float32 [4, 32, 1024], P('sec', None, 'blk'), may hold values from -6 to 6
- conductivity: float32 [4, 32, 1024], P('sec', None, 'blk'), may hold values from 0.5 to 2
- face_owner: int32 [4, 8, 64, 1], P('sec', 'blk'), may hold values from 0 to 7; in each aligned block of 64 rows (0 to 63, 64 to 127, ..., all dimensions but the last counted through in order) at most 8 rows name the same one
Outputs:
- fluid_out: float32 [8, 256, 1024], P(None, 'sec', 'blk')
- solid_out: float32 [4, 32, 1024], P('sec', None, 'blk')
The draws below stay inside these ranges and needn't reach their ends.
Inputs may be any that keep to these rules, and one draw needn't show every extreme that they name: `face_owner`: the 64 wall blocks of one device name any one owner at most 8 times; some device names some owner exactly 8 times.
All inputs are finite; a program needn't handle non-finite values.
Results may differ from the reference program's by a relative error of at most 0.0001.
Values sent between devices are 32-bit elements; how exact they have to be, the bound alone decides.
No kernel may reach another device: no remote copies, remote signals or barrier semaphores. Data moves between devices by JAX's collectives and lax.ppermute only.
A program may use at most 64 MiB of HBM per device.

```python
import math
import jax
import jax.numpy as jnp
import numpy as np
from jax import lax

FZ = 8
FP = 64
FS = 128
SD = 32
SUB = 4
CAP = 8
NP = 256
NSTR = 1024
N_SEC = 4
N_BLK = 8


def level_of(rng, dims, cuts, least, high):
    level, own = 1.0, jax.random.fold_in(rng, 6)
    for position, blocks in cuts:
        heights = jnp.exp(jax.random.uniform(jax.random.fold_in(own, position), (blocks,), jnp.float32, least / len(cuts), high / len(cuts)))
        level = level * jnp.repeat(heights, dims[position] // blocks).reshape([-1 if axis == position else 1 for axis in range(len(dims))])
    return level


def shared_out(own_key, own, number, rows, number_of, top, limit, slope):
    order = jax.random.permutation(own_key, number_of)
    packed, ordinary = load_shares(number_of, rows * top, limit, slope, True), load_shares(number_of, rows * top, limit, slope, False)
    places = jnp.arange(number_of)

    def named(tallies, offset_by):
        used = int((tallies > 0).sum())
        fixed = max(1, used // 4)
        shifted = fixed + (places - fixed + offset_by * (used - fixed)) % max(1, number_of - fixed)
        return jnp.zeros((number_of,), jnp.int32).at[order[jnp.where(places < fixed, places, shifted)]].set(jnp.asarray(tallies, jnp.int32))

    tallies = jnp.where(number % 4 == 0, named(packed, number // 4), named(ordinary, number - number // 4 - 1))
    mixed = jax.random.permutation(jax.random.fold_in(own, 3), number_of)
    source_of, sink = mixed[0:number_of // 2 * 2:2], mixed[1:number_of // 2 * 2:2]
    room = jnp.minimum(tallies[source_of] - 1, limit - tallies[sink]) // 2
    room = jnp.where((source_of == order[0]) | (sink == order[0]) | (tallies[sink] == 0), 0, jnp.maximum(room, 0))
    shifted = jax.random.randint(jax.random.fold_in(own, 4), (number_of // 2,), 0, 1 << 20) % (room + 1)
    tallies = tallies.at[source_of].add(-shifted).at[sink].add(shifted)
    labels = jnp.searchsorted(jnp.cumsum(tallies), jnp.arange(rows * top), side="right").astype(jnp.int32)
    grid = labels.reshape(top, rows).T
    grid = grid[jax.random.permutation(jax.random.fold_in(own, 1), rows)]
    offset_by = jax.random.randint(jax.random.fold_in(own, 2), (rows, 1), 0, top)
    return jnp.take_along_axis(grid, (jnp.arange(top)[None, :] + offset_by) % top, axis=1)


def load_shares(number_of, total, bound, slope, full):
    portions = [(1 << 20) // math.isqrt(rank ** slope) + 1 for rank in range(1, number_of + 1)]
    largest = bound if full else min(bound, max(-(-total // number_of), total * portions[0] // sum(portions)))
    least = 1 if total - largest >= number_of - 1 else 0
    given, spare = [largest] + [least] * (number_of - 1), total - largest - least * (number_of - 1)
    while spare > 0:
        movable = [i for i in range(1, number_of) if given[i] < largest] or [i for i in range(1, number_of) if given[i] < bound]
        whole, budget = sum([portions[i] for i in movable]), spare
        for i in movable:
            extra = min(bound - given[i], max(1, budget * portions[i] // whole), spare)
            given[i] = given[i] + extra
            spare = spare - extra
    return np.array(given)


def centred(key, shape, scale, most, shards=(), held_as=jnp.bfloat16):
    entries = jax.random.normal(key, shape, jnp.float32) * scale
    if len(shards) > 0:
        entries = level_of(key, shape, shards, -0.22, 0.18) * entries
    return jnp.clip(entries, min=-most, max=most).astype(held_as)


def setup_inputs(seed: int = 0) -> dict:
    streams_of = jax.random.split(jax.random.key(seed), 8)
    fluid_temp = centred(streams_of[0], (FZ, NP, NSTR), 1.0, 6.0, ((1, 4), (2, 8)), jnp.float32)
    stream_velocity = jnp.clip(0.2 + 0.8 * jax.random.uniform(streams_of[1], (FZ, NP, NSTR), jnp.float32) ** level_of(streams_of[1], (FZ, NP, NSTR), ((1, 4), (2, 8)), -0.2, 0.2), 0.2, 1.0)
    pitch_velocity = jnp.clip(jax.random.uniform(streams_of[2], (FZ, NP, NSTR), jnp.float32, -0.5, 0.5) * level_of(streams_of[2], (FZ, NP, NSTR), ((1, 4), (2, 8)), -0.4, 0.0), -0.5, 0.5)
    film_coeff = jnp.clip(jnp.exp(math.log(0.3) - 1.0986123 * jax.random.uniform(streams_of[3], (NP, NSTR), jnp.float32) ** level_of(streams_of[3], (NP, NSTR), ((0, 4), (1, 8)), -0.2, 0.2)), 0.1, 0.3)
    solid_temp = centred(streams_of[4], (N_SEC, SD, NSTR), 1.0, 6.0, ((0, 4), (2, 8)), jnp.float32)
    conductivity = jnp.clip(jnp.exp(math.log(2.0) - 1.3862944 * jax.random.uniform(streams_of[5], (N_SEC, SD, NSTR), jnp.float32) ** level_of(streams_of[5], (N_SEC, SD, NSTR), ((0, 4), (2, 8)), -0.2, 0.2)), 0.5, 2.0)
    face_owner_keys = jax.random.split(jax.random.fold_in(streams_of[6], 1), N_SEC * N_BLK * FP // FP)
    face_owner_turns = jax.random.permutation(jax.random.fold_in(streams_of[6], 3), N_SEC * N_BLK * FP // FP)
    face_owner = jax.vmap(lambda own, number: shared_out(jax.random.fold_in(streams_of[6], 2), own, number, FP, N_BLK, 1, CAP, 2))(face_owner_keys, face_owner_turns).reshape((N_SEC, N_BLK, FP, 1))
    return {"fluid_temp": fluid_temp, "stream_velocity": stream_velocity, "pitch_velocity": pitch_velocity, "film_coeff": film_coeff, "solid_temp": solid_temp, "conductivity": conductivity, "face_owner": face_owner}


ADVECT = 0.4
SPREAD = 0.04
WALL = 0.4
SOLID_STEP = 0.04
COOLING = 0.5
COOLANT = -1.0


def fluid_update(fluid, stream_velocity, pitch_velocity, wall_flux, pitch_extended, stream_extended):
    pitch_prev = pitch_extended[:, :-2]
    pitch_next = pitch_extended[:, 2:]
    stream_prev = stream_extended[:, :, :-2]
    stream_next = stream_extended[:, :, 2:]
    span_prev = jnp.concatenate([fluid[:1], fluid[:-1]], 0)
    span_next = jnp.concatenate([fluid[1:], fluid[-1:]], 0)
    spread = SPREAD * (pitch_prev + pitch_next + stream_prev + stream_next + span_prev + span_next - 6.0 * fluid)
    carried = (-ADVECT * stream_velocity * (fluid - stream_prev)
               - ADVECT * jnp.maximum(pitch_velocity, 0.0) * (fluid - pitch_prev)
               + ADVECT * jnp.maximum(-pitch_velocity, 0.0) * (pitch_next - fluid))
    updated = fluid + spread + carried
    return updated.at[0].add(-WALL * wall_flux)


def solid_update(solid, conduct, inflow, solid_extended, conduct_extended):
    stream_prev = solid_extended[..., :-2]
    stream_next = solid_extended[..., 2:]
    conduct_prev = conduct_extended[..., :-2]
    conduct_next = conduct_extended[..., 2:]
    depth_prev = jnp.concatenate([solid[:, :1], solid[:, :-1]], 1)
    depth_next = jnp.concatenate([solid[:, 1:], solid[:, -1:]], 1)
    kdepth_prev = jnp.concatenate([conduct[:, :1], conduct[:, :-1]], 1)
    kdepth_next = jnp.concatenate([conduct[:, 1:], conduct[:, -1:]], 1)
    flow = (0.5 * (conduct + conduct_prev) * (stream_prev - solid)
            + 0.5 * (conduct + conduct_next) * (stream_next - solid)
            + 0.5 * (conduct + kdepth_prev) * (depth_prev - solid)
            + 0.5 * (conduct + kdepth_next) * (depth_next - solid))
    updated = solid + SOLID_STEP * flow
    updated = updated.at[:, 0].add(SOLID_STEP * inflow)
    updated = updated.at[:, -1].add(SOLID_STEP * COOLING * (COOLANT - solid[:, -1]))
    return updated


def reference(fluid_temp, stream_velocity, pitch_velocity, film_coeff, solid_temp, conductivity, face_owner):
    owners = face_owner[..., 0]
    onehot = (owners[..., None] == jnp.arange(N_BLK, dtype=jnp.int32)).astype(jnp.float32)
    film = film_coeff.reshape(N_SEC, FP, N_BLK, FS).transpose(0, 2, 1, 3)
    fluid = fluid_temp
    solid = solid_temp
    for subiter in range(SUB):
        wall_rows = solid[:, 0, :].reshape(N_SEC, N_BLK, FS)
        wall_temp = jnp.einsum("sbpo,sof->sbpf", onehot, wall_rows, precision=lax.Precision.HIGHEST)
        layer = fluid[0].reshape(N_SEC, FP, N_BLK, FS).transpose(0, 2, 1, 3)
        flux = film * (layer - wall_temp)
        inflow = jnp.einsum("sbpo,sbpf->sof", onehot, flux, precision=lax.Precision.HIGHEST).reshape(N_SEC, NSTR)
        wall_flux = flux.transpose(0, 2, 1, 3).reshape(NP, NSTR)
        pitch_extended = jnp.concatenate([fluid[:, -1:], fluid, fluid[:, :1]], 1)
        stream_extended = jnp.pad(fluid, ((0, 0), (0, 0), (1, 1)))
        conduct = conductivity * (1.0 + 0.25 * jnp.tanh(solid))
        solid_extended = jnp.pad(solid, ((0, 0), (0, 0), (1, 1)))
        conduct_extended = jnp.pad(conduct, ((0, 0), (0, 0), (1, 1)))
        fluid = fluid_update(fluid, stream_velocity, pitch_velocity, wall_flux, pitch_extended, stream_extended)
        solid = solid_update(solid, conduct, inflow, solid_extended, conduct_extended)
    return (fluid, solid)
```

```python
import jax
import jax.numpy as jnp
from jax import lax
from jax.experimental import pallas as pl
from jax.experimental.pallas import tpu as pltpu
from jax.sharding import PartitionSpec as P

SUB = 4


ADVECT = 0.4
SPREAD = 0.04
WALL = 0.4
SOLID_STEP = 0.04
COOLING = 0.5
COOLANT = -1.0

F32 = jnp.float32
NB = 8
FZ = 8
FP = 64
FS = 128
SD = 32
R0 = 48
R1 = 40


def lanes(rows):
    return lax.broadcasted_iota(jnp.int32, (rows, FS), 1)


def subs(rows):
    return lax.broadcasted_iota(jnp.int32, (rows, FS), 0)


def turn(x, shift, axis=1):
    return pltpu.roll(x, shift % x.shape[axis], axis)


def by_owner(owner, values):
    sub = subs(NB)
    outs = [jnp.zeros((NB, FS), F32) for _ in values]
    for o in range(NB):
        mine = owner == o
        for i, value in enumerate(values):
            total = jnp.sum(jnp.where(mine, value, 0.0), axis=0, keepdims=True)
            outs[i] = jnp.where(sub == o, total, outs[i])
    return outs


def pick(owner, table):
    out = jnp.zeros(owner.shape, F32)
    for o in range(NB):
        out = jnp.where(owner == o, table[o : o + 1], out)
    return out


def pick_lane(owner_row, table, lane):
    column = jnp.broadcast_to(table[:, lane : lane + 1], (NB, FS))
    named = jnp.broadcast_to(owner_row, (NB, FS)) == subs(NB).astype(F32)
    return jnp.sum(jnp.where(named, column, 0.0), axis=0, keepdims=True)


def stencil(x, low, high, left, right, below, above, sv, pv):
    spread = SPREAD * (low + high + left + right + below + above - 6.0 * x)
    carried = (
        -ADVECT * sv * (x - left)
        - ADVECT * jnp.maximum(pv, 0.0) * (x - low)
        + ADVECT * jnp.maximum(-pv, 0.0) * (high - x)
    )
    return x + spread + carried


def span(x):
    sub = subs(FZ)
    below = jnp.where(sub == 0, x, turn(x, 1, 0))
    above = jnp.where(sub == FZ - 1, x, turn(x, FZ - 1, 0))
    return below, above


def halo_column(x, corners, left, right, sv, pv, film, wall, keep):
    lane = lanes(FZ)
    low = jnp.where(lane == 0, turn(corners, 32), turn(x, 1))
    high = jnp.where(lane == FP - 1, turn(corners, FP - 1 - 97), turn(x, -1))
    below, above = span(x)
    new = stencil(x, low, high, left, right, below, above, sv, pv)
    new = new - jnp.where(subs(FZ) == 0, WALL * film * (x - wall), 0.0)
    return new * keep


def halo_row(x, low, high, left_corner, right_corner, sv, pv, film, wall):
    lane = lanes(FZ)
    left = jnp.where(lane == 0, left_corner, turn(x, 1))
    right = jnp.where(lane == FS - 1, right_corner, turn(x, -1))
    below, above = span(x)
    new = stencil(x, low, high, left, right, below, above, sv, pv)
    return new - jnp.where(subs(FZ) == 0, WALL * film * (x - wall), 0.0)


def advance(src, dst, low_row, high_row, columns, base, sv, pv, film, wall):
    lane = lanes(FP)
    sub = subs(FP)
    for z in range(FZ):
        x = src[z]
        low = jnp.where(sub == 0, low_row[z : z + 1], turn(x, 1, 0))
        high = jnp.where(sub == FP - 1, high_row[z : z + 1], turn(x, -1, 0))
        edge = turn(columns, -(base + 2 * z + 1))
        left = jnp.where(lane == 0, edge, turn(x, 1))
        right = jnp.where(lane == FS - 1, edge, turn(x, -1))
        new = stencil(
            x, low, high, left, right, src[max(z - 1, 0)], src[min(z + 1, FZ - 1)], sv[z], pv[z]
        )
        if z == 0:
            new = new - WALL * film * (x - wall)
        dst[z] = new


def strip_row(here, k_here, under, k_under):
    sub, lane = subs(NB), lanes(NB)

    def prev(x):
        moved = turn(x, 1)
        carried = jnp.where(sub == 0, 0.0, turn(moved, 1, 0))
        return jnp.where(lane == 0, carried, moved)

    def following(x):
        moved = turn(x, -1)
        carried = jnp.where(sub == NB - 1, 0.0, turn(moved, -1, 0))
        return jnp.where(lane == FS - 1, carried, moved)

    flow = (
        0.5 * (k_here + prev(k_here)) * (prev(here) - here)
        + 0.5 * (k_here + following(k_here)) * (following(here) - here)
        + 0.5 * (k_here + k_under) * (under - here)
    )
    return here + SOLID_STEP * flow


def conduct_of(conductivity, solid):
    return conductivity * (1.0 + 0.25 * jnp.tanh(solid))


def metal_step(own, halo, c_own, c_halo, keep):
    k_own, k_halo = conduct_of(c_own, own), conduct_of(c_halo, halo)
    lane, sub = lanes(SD), subs(SD)

    def depth(x):
        up = jnp.where(sub == 0, x, turn(x, 1, 0))
        down = jnp.where(sub == SD - 1, x, turn(x, -1, 0))
        return up, down

    def stream(x, other):
        prev = jnp.where(lane == 0, turn(other, 1), turn(x, 1))
        following = jnp.where(lane == FS - 1, turn(other, -1), turn(x, -1))
        return prev, following

    def update(x, k, other, k_other):
        flow = jnp.zeros_like(x)
        for (a, ka) in zip(stream(x, other) + depth(x), stream(k, k_other) + depth(k)):
            flow = flow + 0.5 * (k + ka) * (a - x)
        new = x + SOLID_STEP * flow
        return new + jnp.where(sub == SD - 1, SOLID_STEP * COOLING * (COOLANT - x), 0.0)

    return update(own, k_own, halo, k_halo), update(halo, k_halo, own, k_own) * keep


def add_inflow(own, halo, inflow, me, keep):
    sub, lane = subs(SD), lanes(SD)
    row = subs(NB)
    mine = jnp.sum(jnp.where(row == me, inflow, 0.0), axis=0, keepdims=True)
    before = jnp.sum(jnp.where(row == me - 1, inflow, 0.0), axis=0, keepdims=True)
    after = jnp.sum(jnp.where(row == me + 1, inflow, 0.0), axis=0, keepdims=True)
    beside = jnp.where(lane >= FS // 2, before, after)
    own = own + jnp.where(sub == 0, SOLID_STEP * mine, 0.0)
    halo = halo + jnp.where(sub == 0, SOLID_STEP * beside, 0.0) * keep
    return own, halo


def column_blocks(mt):
    right = mt[pl.ds(1, FZ, stride=4), :], mt[pl.ds(0, FZ, stride=4), :]
    left = mt[pl.ds(2, FZ, stride=4), :], mt[pl.ds(3, FZ, stride=4), :]
    return right, left


def with_corners(block, low, high, lane_from):
    lane = lanes(FZ)
    block = jnp.where(lane == 96, turn(low, 96 - lane_from), block)
    return jnp.where(lane == 97, turn(high, 97 - lane_from), block)


def gather_columns(fluid, lane):
    acc = jnp.zeros((FP, FS), F32)
    for z in range(FZ):
        acc = jnp.where(lane // 4 == z, turn(fluid[z], 4 * z + 2), acc)
    return acc


def first_kernel(fluid, sv, pv, film, solid, cond, owner, mt, sums):
    lane = lanes(FP)
    named = jnp.broadcast_to(owner[...], (FP, FS))
    top = gather_columns(fluid, lane)
    bottom = jnp.zeros((FP, FS), F32)
    pair = (lane - 32) // 2
    for z in range(FZ):
        here = (pair == z) & (lane >= 32)
        top = jnp.where(here, turn(pv[z], 33 + 2 * z), top)
        bottom = jnp.where(here, turn(sv[z], 33 + 2 * z), bottom)
    top = jnp.where(lane // 2 == 24, turn(film[...], 49), top)
    top = jnp.where(lane == 50, named.astype(F32), top)
    metal = bottom[:SD]
    thin = lanes(SD)
    s, c = solid[...], cond[...]
    for k in range(4):
        metal = jnp.where(thin == 4 * k + 1, turn(s, 3 * k + 5), metal)
        metal = jnp.where(thin == 4 * k + 2, turn(s, 3 * k + 2), metal)
        metal = jnp.where(thin == 4 * k + 17, turn(c, 3 * k + 21), metal)
        metal = jnp.where(thin == 4 * k + 18, turn(c, 3 * k + 18), metal)
    whole = jnp.concatenate([top, metal, bottom[SD:]], axis=0)
    mt[...] = whole.T
    sums[0:8, :], sums[8:16, :] = by_owner(named, [film[...] * fluid[0], film[...]])


def pack_kernel(mt, sums, solid, cond, lo, hi, out):
    me = lax.axis_index("blk")
    lane, sub = lanes(FZ), subs(FZ)
    (r0, r1), (l0, l1) = column_blocks(mt)
    r2, l2 = mt[pl.ds(32, FZ, stride=2), :], mt[pl.ds(33, FZ, stride=2), :]
    low, high = lo[8:16, :], hi[8:16, :]
    r0 = with_corners(r0, low, high, FS - 1)
    l0 = with_corners(l0, low, high, 0)
    owner = turn(mt[50:51, :], 64)

    def with_walls(block, film):
        extra = jnp.where(sub == 0, turn(film, 64), jnp.where(sub == 1, owner, 0.0))
        return jnp.where(lane >= 64, extra, block)

    r1, l1 = with_walls(r1, mt[48:49, :]), with_walls(l1, mt[49:50, :])
    head = jnp.concatenate(
        [solid[0:2, :], cond[0:2, :], lo[33:34, :], hi[33:34, :], lo[34:35, :], hi[34:35, :]], axis=0
    )
    for peer in range(NB):
        out[peer, 0:8, :] = head
        out[peer, 8:24, :] = sums[...]
        ahead = (me + 1 == peer).astype(F32)
        behind = (me - 1 == peer).astype(F32)
        for i, (r, l) in enumerate(((r0, l0), (r1, l1), (r2, l2))):
            out[peer, 24 + 8 * i : 32 + 8 * i, :] = r * ahead + l * behind


def neighbours(recv, me, count):
    before = jnp.maximum(me - 1, 0)
    after = jnp.minimum(me + 1, NB - 1)
    keep_l = (me > 0).astype(F32)
    keep_r = (me < NB - 1).astype(F32)
    start = 24
    left = [recv[before, start + 8 * i : start + 8 * i + 8, :] * keep_l for i in range(count)]
    right = [recv[after, start + 8 * i : start + 8 * i + 8, :] * keep_r for i in range(count)]
    return left, right, keep_l, keep_r


def edge_terms(blocks):
    sv = turn(blocks[2], 64)
    film, owner = turn(blocks[1][0:1], 64), turn(blocks[1][1:2], 64)
    return sv, blocks[2], film, owner


def second_kernel(
    recv, mt, fluid, sv, pv, film, solid, cond, owner, lo, hi, fluid2, up, down, metal, tm, fluid1
):
    me = lax.axis_index("blk")
    left, right, keep_l, keep_r = neighbours(recv, me, 3)
    sv_l, pv_l, film_l, own_l = edge_terms(left)
    sv_r, pv_r, film_r, own_r = edge_terms(right)
    wall0, under0 = recv[:, 0, :], recv[:, 1, :]
    c0, c1 = recv[:, 2, :], recv[:, 3, :]
    a0, h = recv[0, 8:16, :], recv[0, 16:24, :]
    for j in range(1, NB):
        a0, h = a0 + recv[j, 8:16, :], h + recv[j, 16:24, :]
    inflow0 = a0 - h * wall0
    wall1 = strip_row(wall0, conduct_of(c0, wall0), under0, conduct_of(c1, under0))
    wall1 = wall1 + SOLID_STEP * inflow0

    own_cols, _ = None, None
    mine_right, mine_left = mt[pl.ds(1, FZ, stride=4), :], mt[pl.ds(2, FZ, stride=4), :]
    new_l = halo_column(
        left[0], left[0], left[1], mine_left, sv_l, pv_l, film_l,
        pick_lane(own_l, wall0, FS - 1), keep_l,
    )
    new_r = halo_column(
        right[0], right[0], mine_right, right[1], sv_r, pv_r, film_r,
        pick_lane(own_r, wall0, 0), keep_r,
    )
    tm[...] = jnp.zeros((FS, FS), F32)
    tm[pl.ds(0, FZ, stride=2), :] = right[0]
    tm[pl.ds(1, FZ, stride=2), :] = left[0]
    tm[16:24, :] = left[0]
    tm[24:32, :] = right[0]
    tm[pl.ds(32, FZ, stride=2), :] = new_r
    tm[pl.ds(33, FZ, stride=2), :] = new_l
    turned = tm[...].T
    columns = turned[:FP]
    deep = turned[64 : 64 + SD]
    thin = lanes(SD)
    halo = jnp.where(thin >= 124, turn(deep, 108), jnp.where(thin < 4, turn(deep, 104), 0.0))
    c_halo = jnp.where(thin >= 124, turn(deep, 104), jnp.where(thin < 4, turn(deep, 100), 0.0))
    keep = jnp.where(thin >= 64, keep_l, keep_r)

    low, high = lo[8:16, :], hi[8:16, :]
    first, last = fluid[:, 0, :], fluid[:, FP - 1, :]
    wall_lo = pick(lo[34:35, :], recv[:, 4, :])
    wall_hi = pick(hi[34:35, :], recv[:, 5, :])
    new_low = halo_row(
        low, lo[0:8, :], first, turn(left[0], 32), turn(right[0], 31),
        lo[16:24, :], lo[24:32, :], lo[32:33, :], wall_lo,
    )
    new_high = halo_row(
        high, last, hi[0:8, :], turn(left[0], 31), turn(right[0], 30),
        hi[16:24, :], hi[24:32, :], hi[32:33, :], wall_hi,
    )
    named = jnp.broadcast_to(owner[...], (FP, FS))
    walls0, walls1 = pick(named, wall0), pick(named, wall1)
    advance(fluid, fluid1, low, high, columns, 0, sv, pv, film[...], walls0)
    advance(fluid1, fluid2, new_low, new_high, columns, 32, sv, pv, film[...], walls1)
    (flux,) = by_owner(named, [film[...] * (fluid1[0] - walls1)])

    own, halo = metal_step(solid[...], halo, cond[...], c_halo, keep)
    own, halo = add_inflow(own, halo, inflow0, me, keep)
    own, halo = metal_step(own, halo, cond[...], c_halo, keep)
    metal[0:SD, :] = own
    metal[SD : 2 * SD, :] = halo
    metal[2 * SD : 3 * SD, :] = c_halo
    up[0:8, :], up[8:16, :] = fluid2[:, FP - 2, :], fluid2[:, FP - 1, :]
    down[0:8, :], down[8:16, :] = fluid2[:, 1, :], fluid2[:, 0, :]
    for ref in (up, down):
        ref[16:24, :] = flux
        ref[24:32, :] = own[0:8]


def sums_kernel(recv, fluid2, sv, pv, film, owner, mt, sums):
    me = lax.axis_index("blk")
    left, right, keep_l, keep_r = neighbours(recv, me, 3)
    _, _, film_l, own_l = edge_terms(left)
    sv_r, _, film_r, own_r = edge_terms(right)
    lane, sub = lanes(FP), subs(FP)
    named = jnp.broadcast_to(owner[...], (FP, FS))
    x, f = fluid2[0], film[...]
    low = jnp.where(sub == 0, 0.0, turn(x, 1, 0))
    high = jnp.where(sub == FP - 1, 0.0, turn(x, -1, 0))
    before = jnp.where(lane == 0, 0.0, turn(x, 1))
    after = jnp.where(lane == FS - 1, 0.0, turn(x, -1))
    moved = stencil(x, low, high, before, after, x, fluid2[1], sv[0], pv[0]) - WALL * f * x
    a2, b3, h2 = by_owner(named, [f * x, f * moved, f * f])
    whole = jnp.concatenate([gather_columns(fluid2, lane), jnp.zeros((FP, FS), F32)], axis=0)
    mt[0:FS, :] = whole.T
    thin = subs(NB)
    inside = lanes(NB) < FP
    right_term = film_r * (SPREAD + ADVECT * sv_r[0:1]) * mt[1:2, :] * keep_r
    left_term = film_l * SPREAD * mt[2:3, :] * keep_l

    def shared(own_row, term):
        hit = (jnp.broadcast_to(own_row, (NB, FS)) == thin.astype(F32)) & inside
        return jnp.sum(jnp.where(hit, term, 0.0), axis=1, keepdims=True)

    b3 = b3 + jnp.where(lanes(NB) == 0, shared(own_r, right_term), 0.0)
    b3 = b3 + jnp.where(lanes(NB) == FS - 1, shared(own_l, left_term), 0.0)
    top, end = f[0:1], f[FP - 1 : FP]
    up = top * (SPREAD + ADVECT * jnp.maximum(pv[0, 0:1, :], 0.0))
    down = end * (SPREAD + ADVECT * jnp.maximum(-pv[0, FP - 1 : FP, :], 0.0))
    mt[FS : FS + 8, :] = jnp.concatenate(
        [up, down, named[0:1].astype(F32), named[FP - 1 : FP].astype(F32), jnp.zeros((4, FS), F32)],
        axis=0,
    )
    sums[0:8, :], sums[8:16, :], sums[16:24, :] = a2, b3, h2


def send_kernel(recv, mt, sums, up, metal, lo, hi, out):
    me = lax.axis_index("blk")
    sub = subs(NB)
    rows = sub.astype(F32)
    (r0, r1), (l0, l1) = column_blocks(mt)
    low, high = lo[8:16, :], hi[8:16, :]
    r0 = with_corners(r0, low, high, FS - 1)
    l0 = with_corners(l0, low, high, 0)
    b3 = sums[8:16, :]
    b3 = b3 + jnp.where(rows == mt[FS + 2 : FS + 3, :], mt[FS : FS + 1, :] * low[0:1], 0.0)
    b3 = b3 + jnp.where(rows == mt[FS + 3 : FS + 4, :], mt[FS + 1 : FS + 2, :] * high[0:1], 0.0)
    relay_lo = pick(recv[:, 6, :], lo[16:24, :])
    relay_hi = pick(recv[:, 7, :], hi[16:24, :])
    h2 = sums[16:24, :]
    for peer in range(NB):
        out[peer, 0:8, :] = jnp.concatenate(
            [
                metal[0:2, :],
                lo[24:25, :],
                hi[24:25, :],
                b3[peer : peer + 1],
                h2[peer : peer + 1],
                relay_lo[peer : peer + 1],
                relay_hi[peer : peer + 1],
            ],
            axis=0,
        )
        out[peer, 8:16, :] = up[16:24, :]
        out[peer, 16:24, :] = sums[0:8, :]
        ahead = (me + 1 == peer).astype(F32)
        behind = (me - 1 == peer).astype(F32)
        out[peer, 24:32, :] = r0 * ahead + l0 * behind
        out[peer, 32:40, :] = r1 * ahead + l1 * behind


def last_kernel(
    recv1, recv, mt, fluid2, sv, pv, film, cond, owner, lo, hi, lo1, hi1, metal, fluid_out, solid_out,
    tm, fluid3,
):
    me = lax.axis_index("blk")
    stat_l, stat_r, keep_l, keep_r = neighbours(recv, me, 3)
    left, right, _, _ = neighbours(recv1, me, 2)
    sv_l, pv_l, film_l, own_l = edge_terms(stat_l)
    sv_r, pv_r, film_r, own_r = edge_terms(stat_r)
    c0, c1 = recv[:, 2, :], recv[:, 3, :]
    h = recv[0, 16:24, :]
    tail, inflow1, a2 = recv1[0, 0:8, :], recv1[0, 8:16, :], recv1[0, 16:24, :]
    for j in range(1, NB):
        h = h + recv[j, 16:24, :]
        tail = tail + recv1[j, 0:8, :]
        inflow1 = inflow1 + recv1[j, 8:16, :]
        a2 = a2 + recv1[j, 16:24, :]
    wall2 = recv1[:, 0, :] + SOLID_STEP * inflow1
    under2 = recv1[:, 1, :]
    inflow2 = a2 - h * wall2
    wall3 = strip_row(wall2, conduct_of(c0, wall2), under2, conduct_of(c1, under2))
    wall3 = wall3 + SOLID_STEP * inflow2
    inflow3 = tail[4:5] + WALL * tail[5:6] * wall2 - h * wall3
    wall_lo = pick(lo[34:35, :], recv1[:, 2, :]) + SOLID_STEP * tail[6:7]
    wall_hi = pick(hi[34:35, :], recv1[:, 3, :]) + SOLID_STEP * tail[7:8]

    mine_right, mine_left = mt[pl.ds(1, FZ, stride=4), :], mt[pl.ds(2, FZ, stride=4), :]
    new_l = halo_column(
        left[0], left[0], left[1], mine_left, sv_l, pv_l, film_l,
        pick_lane(own_l, wall2, FS - 1), keep_l,
    )
    new_r = halo_column(
        right[0], right[0], mine_right, right[1], sv_r, pv_r, film_r,
        pick_lane(own_r, wall2, 0), keep_r,
    )
    tm[...] = jnp.zeros((FS, FS), F32)
    tm[pl.ds(0, FZ, stride=2), :] = right[0]
    tm[pl.ds(1, FZ, stride=2), :] = left[0]
    tm[pl.ds(32, FZ, stride=2), :] = new_r
    tm[pl.ds(33, FZ, stride=2), :] = new_l
    columns = tm[...].T[:FP]
    low, high = lo1[8:16, :], hi1[8:16, :]
    first, last = fluid2[:, 0, :], fluid2[:, FP - 1, :]
    new_low = halo_row(
        low, lo1[0:8, :], first, turn(left[0], 32), turn(right[0], 31),
        lo[16:24, :], lo[24:32, :], lo[32:33, :], wall_lo,
    )
    new_high = halo_row(
        high, last, hi1[0:8, :], turn(left[0], 31), turn(right[0], 30),
        hi[16:24, :], hi[24:32, :], hi[32:33, :], wall_hi,
    )
    named = jnp.broadcast_to(owner[...], (FP, FS))
    advance(fluid2, fluid3, low, high, columns, 0, sv, pv, film[...], pick(named, wall2))
    advance(fluid3, fluid_out, new_low, new_high, columns, 32, sv, pv, film[...], pick(named, wall3))

    thin = lanes(SD)
    keep = jnp.where(thin >= 64, keep_l, keep_r)
    own, halo, c_halo = metal[0:SD, :], metal[SD : 2 * SD, :], metal[2 * SD : 3 * SD, :]
    own, halo = add_inflow(own, halo, inflow1, me, keep)
    own, halo = metal_step(own, halo, cond[...], c_halo, keep)
    own, halo = add_inflow(own, halo, inflow2, me, keep)
    own, halo = metal_step(own, halo, cond[...], c_halo, keep)
    own, _ = add_inflow(own, halo, inflow3, me, keep)
    solid_out[...] = own


def shape(*dims):
    return jax.ShapeDtypeStruct(dims, F32)


VMEM = pl.BlockSpec(memory_space=pltpu.VMEM)


def call(kernel, outs, args, name, scratch=()):
    return pl.pallas_call(
        kernel,
        out_shape=outs,
        in_specs=[VMEM] * len(args),
        out_specs=jax.tree.map(lambda _: VMEM, outs),
        scratch_shapes=scratch,
        name=name,
        compiler_params=pltpu.CompilerParams(vmem_limit_bytes=32 * 1024 * 1024),
    )(*args)


def both_ways(up, down):
    count = lax.axis_size("sec")
    forward = [(i, (i + 1) % count) for i in range(count)]
    backward = [(target, source) for source, target in forward]
    return lax.ppermute(up, "sec", forward), lax.ppermute(down, "sec", backward)


def swap(message):
    return lax.all_to_all(message, "blk", split_axis=0, concat_axis=0, tiled=True)


def two_exchanges(fluid, sv, pv, film, solid, cond, face_owner):
    owner = face_owner.reshape(FP, 1)
    solid, cond = solid.reshape(SD, FS), cond.reshape(SD, FS)

    def rows(outer, inner):
        name = jnp.broadcast_to(owner[outer : outer + 1].astype(F32), (1, FS))
        return jnp.concatenate(
            [
                fluid[:, inner],
                fluid[:, outer],
                sv[:, outer],
                pv[:, outer],
                film[outer : outer + 1],
                solid[0:1],
                name,
                jnp.zeros((5, FS), F32),
            ],
            axis=0,
        )

    lo, hi = both_ways(rows(FP - 1, FP - 2), rows(0, 1))
    mt, sums = call(
        first_kernel,
        (shape(FS, FS), shape(16, FS)),
        (fluid, sv, pv, film, solid, cond, owner),
        "columns",
    )
    recv = swap(call(pack_kernel, shape(NB, R0, FS), (mt, sums, solid, cond, lo, hi), "pack"))
    work = [pltpu.VMEM((FS, FS), F32), pltpu.VMEM((FZ, FP, FS), F32)]
    fluid2, up, down, metal = call(
        second_kernel,
        (shape(FZ, FP, FS), shape(32, FS), shape(32, FS), shape(3 * SD, FS)),
        (recv, mt, fluid, sv, pv, film, solid, cond, owner, lo, hi),
        "steps",
        work,
    )
    lo1, hi1 = both_ways(up, down)
    mt1, sums1 = call(
        sums_kernel,
        (shape(FS + 8, FS), shape(24, FS)),
        (recv, fluid2, sv, pv, film, owner),
        "sums",
    )
    recv1 = swap(
        call(send_kernel, shape(NB, R1, FS), (recv, mt1, sums1, up, metal, lo1, hi1), "pack")
    )
    fluid, solid = call(
        last_kernel,
        (shape(FZ, FP, FS), shape(SD, FS)),
        (recv1, recv, mt1, fluid2, sv, pv, film, cond, owner, lo, hi, lo1, hi1, metal),
        "steps",
        work,
    )
    return fluid, solid.reshape(1, SD, FS)


def padded(block, sides, width, periodic):
    for axis, dim in sides:
        count = lax.axis_size(axis)
        forward = [(i, i + 1) for i in range(count - 1)]
        if periodic:
            forward.append((count - 1, 0))
        backward = [(target, source) for source, target in forward]
        low = lax.ppermute(
            lax.slice_in_dim(block, block.shape[dim] - width, None, axis=dim), axis, forward
        )
        high = lax.ppermute(lax.slice_in_dim(block, 0, width, axis=dim), axis, backward)
        block = jnp.concatenate([low, block, high], axis=dim)
    return block


def fluid_update(
    fluid, stream_velocity, pitch_velocity, wall_flux, pitch_extended, stream_extended
):
    pitch_prev = pitch_extended[:, :-2]
    pitch_next = pitch_extended[:, 2:]
    stream_prev = stream_extended[:, :, :-2]
    stream_next = stream_extended[:, :, 2:]
    span_prev = jnp.concatenate([fluid[:1], fluid[:-1]], 0)
    span_next = jnp.concatenate([fluid[1:], fluid[-1:]], 0)
    spread = SPREAD * (
        pitch_prev + pitch_next + stream_prev + stream_next + span_prev + span_next - 6.0 * fluid
    )
    carried = (
        -ADVECT * stream_velocity * (fluid - stream_prev)
        - ADVECT * jnp.maximum(pitch_velocity, 0.0) * (fluid - pitch_prev)
        + ADVECT * jnp.maximum(-pitch_velocity, 0.0) * (pitch_next - fluid)
    )
    updated = fluid + spread + carried
    return updated.at[0].add(-WALL * wall_flux)


def solid_update(solid, conduct, inflow, solid_extended, conduct_extended):
    stream_prev = solid_extended[..., :-2]
    stream_next = solid_extended[..., 2:]
    conduct_prev = conduct_extended[..., :-2]
    conduct_next = conduct_extended[..., 2:]
    depth_prev = jnp.concatenate([solid[:, :1], solid[:, :-1]], 1)
    depth_next = jnp.concatenate([solid[:, 1:], solid[:, -1:]], 1)
    kdepth_prev = jnp.concatenate([conduct[:, :1], conduct[:, :-1]], 1)
    kdepth_next = jnp.concatenate([conduct[:, 1:], conduct[:, -1:]], 1)
    flow = (
        0.5 * (conduct + conduct_prev) * (stream_prev - solid)
        + 0.5 * (conduct + conduct_next) * (stream_next - solid)
        + 0.5 * (conduct + kdepth_prev) * (depth_prev - solid)
        + 0.5 * (conduct + kdepth_next) * (depth_next - solid)
    )
    updated = solid + SOLID_STEP * flow
    updated = updated.at[:, 0].add(SOLID_STEP * inflow)
    updated = updated.at[:, -1].add(SOLID_STEP * COOLING * (COOLANT - solid[:, -1]))
    return updated


def local(
    fluid_temp, stream_velocity, pitch_velocity, film_coeff, solid_temp, conductivity, face_owner
):
    span_cells, pitch_cells, stream_cells = fluid_temp.shape
    depth_cells = solid_temp.shape[1]
    block_count = lax.axis_size("blk")
    capacity = max(2, (pitch_cells + block_count - 1) // block_count)
    owners = face_owner.reshape(-1)
    onehot = (owners[:, None] == jnp.arange(block_count, dtype=jnp.int32)[None, :]).astype(
        jnp.float32
    )
    same_owner = owners[:, None] == owners[None, :]
    earlier = lax.broadcasted_iota(jnp.int32, (pitch_cells, pitch_cells), 0) < lax.broadcasted_iota(
        jnp.int32, (pitch_cells, pitch_cells), 1
    )
    slot_rank = jnp.sum((same_owner & earlier).astype(jnp.int32), axis=0)
    slot_table = (slot_rank[None, :] == jnp.arange(capacity, dtype=jnp.int32)[:, None]).astype(
        jnp.float32
    )
    placing = onehot.T[:, None, :] * slot_table[None, :, :]
    fluid = fluid_temp
    solid = solid_temp
    gas_rows = span_cells * pitch_cells
    for subiter in range(SUB):
        wall_row = solid[0, 0:1, :]
        wall_temp = jnp.dot(
            onehot,
            lax.all_gather(wall_row, "blk", axis=0, tiled=True),
            precision=lax.Precision.HIGHEST,
            preferred_element_type=jnp.float32,
        )
        flux = film_coeff * (fluid[0] - wall_temp)
        outgoing = jnp.einsum("ocb,bf->ocf", placing, flux, precision=lax.Precision.HIGHEST)
        received = lax.all_to_all(outgoing, "blk", split_axis=0, concat_axis=0, tiled=True)
        inflow = jnp.sum(received, axis=(0, 1))
        conduct = conductivity * (1.0 + 0.25 * jnp.tanh(solid))
        stacked = jnp.concatenate([fluid.reshape(gas_rows, stream_cells), solid[0], conduct[0]], 0)
        stream_ext = padded(stacked, (("blk", 1),), 1, False)
        pitch_extended = padded(fluid, (("sec", 1),), 1, True)
        fluid_stream = stream_ext[:gas_rows].reshape(span_cells, pitch_cells, stream_cells + 2)
        solid_stream = stream_ext[gas_rows : gas_rows + depth_cells][None]
        conduct_stream = stream_ext[gas_rows + depth_cells :][None]
        fluid = fluid_update(
            fluid, stream_velocity, pitch_velocity, flux, pitch_extended, fluid_stream
        )
        solid = solid_update(solid, conduct, inflow[None, :], solid_stream, conduct_stream)
    return (fluid, solid)


def solution(mesh):
    placed = (
        P(None, "sec", "blk"),
        P(None, "sec", "blk"),
        P(None, "sec", "blk"),
        P("sec", "blk"),
        P("sec", None, "blk"),
        P("sec", None, "blk"),
        P("sec", "blk", None, None),
    )
    sizes = dict(mesh.shape)

    def chosen(*args):
        fits = args[0].shape == (FZ, FP, FS) and args[4].shape == (1, SD, FS)
        return two_exchanges(*args) if fits and sizes["blk"] == NB else local(*args)

    return jax.shard_map(
        chosen,
        mesh=mesh,
        in_specs=placed,
        out_specs=(P(None, "sec", "blk"), P("sec", None, "blk")),
        check_vma=False,
    )
```

```python
import jax
import jax.numpy as jnp
from jax import lax
from jax.experimental import pallas as pl
from jax.experimental.pallas import tpu as pltpu
from jax.sharding import PartitionSpec as P

SUB = 4


ADVECT = 0.4
SPREAD = 0.04
WALL = 0.4
SOLID_STEP = 0.04
COOLING = 0.5
COOLANT = -1.0

F32 = jnp.float32
NB = 8
FZ = 8
FP = 64
FS = 128
SD = 32
R0 = 48
R1 = 40


def lanes(rows):
    return lax.broadcasted_iota(jnp.int32, (rows, FS), 1)


def subs(rows):
    return lax.broadcasted_iota(jnp.int32, (rows, FS), 0)


def turn(x, shift, axis=1):
    return pltpu.roll(x, shift % x.shape[axis], axis)


def by_owner(owner, values):
    sub = subs(NB)
    outs = [jnp.zeros((NB, FS), F32) for _ in values]
    for o in range(NB):
        mine = owner == o
        for i, value in enumerate(values):
            total = jnp.sum(jnp.where(mine, value, 0.0), axis=0, keepdims=True)
            outs[i] = jnp.where(sub == o, total, outs[i])
    return outs


def pick(owner, table):
    out = jnp.zeros(owner.shape, F32)
    for o in range(NB):
        out = jnp.where(owner == o, table[o : o + 1], out)
    return out


def pick_lane(owner_row, table, lane):
    column = jnp.broadcast_to(table[:, lane : lane + 1], (NB, FS))
    named = jnp.broadcast_to(owner_row, (NB, FS)) == subs(NB).astype(F32)
    return jnp.sum(jnp.where(named, column, 0.0), axis=0, keepdims=True)


def stencil(x, low, high, left, right, below, above, sv, pv):
    spread = SPREAD * (low + high + left + right + below + above - 6.0 * x)
    carried = (
        -ADVECT * sv * (x - left)
        - ADVECT * jnp.maximum(pv, 0.0) * (x - low)
        + ADVECT * jnp.maximum(-pv, 0.0) * (high - x)
    )
    return x + spread + carried


def span(x):
    sub = subs(FZ)
    below = jnp.where(sub == 0, x, turn(x, 1, 0))
    above = jnp.where(sub == FZ - 1, x, turn(x, FZ - 1, 0))
    return below, above


def halo_column(x, corners, left, right, sv, pv, film, wall, keep):
    lane = lanes(FZ)
    low = jnp.where(lane == 0, turn(corners, 32), turn(x, 1))
    high = jnp.where(lane == FP - 1, turn(corners, FP - 1 - 97), turn(x, -1))
    below, above = span(x)
    new = stencil(x, low, high, left, right, below, above, sv, pv)
    new = new - jnp.where(subs(FZ) == 0, WALL * film * (x - wall), 0.0)
    return new * keep


def halo_row(x, low, high, left_corner, right_corner, sv, pv, film, wall):
    lane = lanes(FZ)
    left = jnp.where(lane == 0, left_corner, turn(x, 1))
    right = jnp.where(lane == FS - 1, right_corner, turn(x, -1))
    below, above = span(x)
    new = stencil(x, low, high, left, right, below, above, sv, pv)
    return new - jnp.where(subs(FZ) == 0, WALL * film * (x - wall), 0.0)


def advance(src, dst, low_row, high_row, columns, base, sv, pv, film, wall):
    lane = lanes(FP)
    sub = subs(FP)
    for z in range(FZ):
        x = src[z]
        low = jnp.where(sub == 0, low_row[z : z + 1], turn(x, 1, 0))
        high = jnp.where(sub == FP - 1, high_row[z : z + 1], turn(x, -1, 0))
        edge = turn(columns, -(base + 2 * z + 1))
        left = jnp.where(lane == 0, edge, turn(x, 1))
        right = jnp.where(lane == FS - 1, edge, turn(x, -1))
        new = stencil(
            x, low, high, left, right, src[max(z - 1, 0)], src[min(z + 1, FZ - 1)], sv[z], pv[z]
        )
        if z == 0:
            new = new - WALL * film * (x - wall)
        dst[z] = new


def strip_row(here, k_here, under, k_under):
    sub, lane = subs(NB), lanes(NB)

    def prev(x):
        moved = turn(x, 1)
        carried = jnp.where(sub == 0, 0.0, turn(moved, 1, 0))
        return jnp.where(lane == 0, carried, moved)

    def following(x):
        moved = turn(x, -1)
        carried = jnp.where(sub == NB - 1, 0.0, turn(moved, -1, 0))
        return jnp.where(lane == FS - 1, carried, moved)

    flow = (
        0.5 * (k_here + prev(k_here)) * (prev(here) - here)
        + 0.5 * (k_here + following(k_here)) * (following(here) - here)
        + 0.5 * (k_here + k_under) * (under - here)
    )
    return here + SOLID_STEP * flow


def conduct_of(conductivity, solid):
    return conductivity * (1.0 + 0.25 * jnp.tanh(solid))


def metal_step(own, halo, c_own, c_halo, keep):
    k_own, k_halo = conduct_of(c_own, own), conduct_of(c_halo, halo)
    lane, sub = lanes(SD), subs(SD)

    def depth(x):
        up = jnp.where(sub == 0, x, turn(x, 1, 0))
        down = jnp.where(sub == SD - 1, x, turn(x, -1, 0))
        return up, down

    def stream(x, other):
        prev = jnp.where(lane == 0, turn(other, 1), turn(x, 1))
        following = jnp.where(lane == FS - 1, turn(other, -1), turn(x, -1))
        return prev, following

    def update(x, k, other, k_other):
        flow = jnp.zeros_like(x)
        for (a, ka) in zip(stream(x, other) + depth(x), stream(k, k_other) + depth(k)):
            flow = flow + 0.5 * (k + ka) * (a - x)
        new = x + SOLID_STEP * flow
        return new + jnp.where(sub == SD - 1, SOLID_STEP * COOLING * (COOLANT - x), 0.0)

    return update(own, k_own, halo, k_halo), update(halo, k_halo, own, k_own) * keep


def add_inflow(own, halo, inflow, me, keep):
    sub, lane = subs(SD), lanes(SD)
    row = subs(NB)
    mine = jnp.sum(jnp.where(row == me, inflow, 0.0), axis=0, keepdims=True)
    before = jnp.sum(jnp.where(row == me - 1, inflow, 0.0), axis=0, keepdims=True)
    after = jnp.sum(jnp.where(row == me + 1, inflow, 0.0), axis=0, keepdims=True)
    beside = jnp.where(lane >= FS // 2, before, after)
    own = own + jnp.where(sub == 0, SOLID_STEP * mine, 0.0)
    halo = halo + jnp.where(sub == 0, SOLID_STEP * beside, 0.0) * keep
    return own, halo


def column_blocks(mt):
    right = mt[pl.ds(1, FZ, stride=4), :], mt[pl.ds(0, FZ, stride=4), :]
    left = mt[pl.ds(2, FZ, stride=4), :], mt[pl.ds(3, FZ, stride=4), :]
    return right, left


def with_corners(block, low, high, lane_from):
    lane = lanes(FZ)
    block = jnp.where(lane == 96, turn(low, 96 - lane_from), block)
    return jnp.where(lane == 97, turn(high, 97 - lane_from), block)


def gather_columns(fluid, lane):
    acc = jnp.zeros((FP, FS), F32)
    for z in range(FZ):
        acc = jnp.where(lane // 4 == z, turn(fluid[z], 4 * z + 2), acc)
    return acc


def fetch(copies, sems):
    started = [
        pltpu.make_async_copy(src, dst, sems.at[i]) for i, (src, dst) in enumerate(copies)
    ]
    for copy in started:
        copy.start()
    return started


def rows_kernel(fluid, sv, pv, film, solid, owner, first, second, tiles, flat, ids, sems):
    starts = (FP - 8, 0)
    copies = []
    for side, start in enumerate(starts):
        for i, ref in enumerate((fluid, sv, pv)):
            copies.append((ref.at[:, pl.ds(start, 8), :], tiles.at[3 * side + i]))
        copies.append((film.at[pl.ds(start, 8), :], flat.at[side]))
    copies += [(solid.at[pl.ds(0, 8), :], flat.at[2]), (owner, ids)]
    for copy in fetch(copies, sems):
        copy.wait()
    even = lax.axis_index("sec") % 2 == 0
    wall = flat[2, 0:1, :]

    def rows(side, outer, inner, row):
        name = jnp.broadcast_to(ids[:, row : row + 1].astype(F32), (1, FS))
        blank = jnp.zeros((5, FS), F32)
        return (
            tiles[3 * side, :, inner, :],
            tiles[3 * side, :, outer, :],
            tiles[3 * side + 1, :, outer, :],
            tiles[3 * side + 2, :, outer, :],
            jnp.concatenate([flat[side, outer : outer + 1, :], wall, name, blank], axis=0),
        )

    for i, (up, down) in enumerate(zip(rows(0, 7, 6, FP - 1), rows(1, 0, 1, 0))):
        first[8 * i : 8 * i + 8, :] = jnp.where(even, up, down)
        second[8 * i : 8 * i + 8, :] = jnp.where(even, down, up)


def first_kernel(
    fluid_in, sv_in, pv_in, film_in, solid_in, cond_in, owner,
    mt, sums, fluid, sv, pv, film, solid, cond, names, ids, sems,
):
    half = FZ // 2
    copies = [(owner, ids), (film_in, film), (solid_in, solid), (cond_in, cond)]
    for src, dst in ((fluid_in, fluid), (pv_in, pv), (sv_in, sv)):
        for part in range(2):
            copies.append((src.at[pl.ds(half * part, half)], dst.at[pl.ds(half * part, half)]))
    started = fetch(copies, sems)
    lane = lanes(FP)
    for copy in started[:4]:
        copy.wait()
    ids_row = jnp.concatenate([ids[...].astype(F32), jnp.zeros((1, FS - FP), F32)], axis=1)
    named = jnp.broadcast_to(ids_row, (FS, FS)).T[:FP]
    names[...] = named
    bottom = jnp.zeros((FP, FS), F32)
    pair = (lane - 32) // 2
    metal = jnp.zeros((SD, FS), F32)
    thin = lanes(SD)
    s, c = solid[...], cond[...]
    for k in range(4):
        metal = jnp.where(thin == 4 * k + 1, turn(s, 3 * k + 5), metal)
        metal = jnp.where(thin == 4 * k + 2, turn(s, 3 * k + 2), metal)
        metal = jnp.where(thin == 4 * k + 17, turn(c, 3 * k + 21), metal)
        metal = jnp.where(thin == 4 * k + 18, turn(c, 3 * k + 18), metal)
    started[4].wait()
    sums[0:8, :], sums[8:16, :] = by_owner(named, [film[...] * fluid[0], film[...]])
    started[5].wait()
    top = gather_columns(fluid, lane)
    for copy in started[6:]:
        copy.wait()
    for z in range(FZ):
        here = (pair == z) & (lane >= 32)
        top = jnp.where(here, turn(pv[z], 33 + 2 * z), top)
        bottom = jnp.where(here, turn(sv[z], 33 + 2 * z), bottom)
    top = jnp.where(lane // 2 == 24, turn(film[...], 49), top)
    top = jnp.where(lane == 50, named, top)
    metal = jnp.where(thin < 32, metal, bottom[:SD])
    whole = jnp.concatenate([top, metal, bottom[SD:]], axis=0)
    mt[...] = whole.T


def sort_rows(first, second, lo, hi):
    even = lax.axis_index("sec") % 2 == 0
    lo[...] = jnp.where(even, second[...], first[...])
    hi[...] = jnp.where(even, first[...], second[...])


def pack_kernel(mt, sums, solid, cond, first, second, out, lo, hi):
    sort_rows(first, second, lo, hi)
    me = lax.axis_index("blk")
    lane, sub = lanes(FZ), subs(FZ)
    (r0, r1), (l0, l1) = column_blocks(mt)
    r2, l2 = mt[pl.ds(32, FZ, stride=2), :], mt[pl.ds(33, FZ, stride=2), :]
    low, high = lo[8:16, :], hi[8:16, :]
    r0 = with_corners(r0, low, high, FS - 1)
    l0 = with_corners(l0, low, high, 0)
    owner = turn(mt[50:51, :], 64)

    def with_walls(block, film):
        extra = jnp.where(sub == 0, turn(film, 64), jnp.where(sub == 1, owner, 0.0))
        return jnp.where(lane >= 64, extra, block)

    r1, l1 = with_walls(r1, mt[48:49, :]), with_walls(l1, mt[49:50, :])
    head = jnp.concatenate(
        [solid[0:2, :], cond[0:2, :], lo[33:34, :], hi[33:34, :], lo[34:35, :], hi[34:35, :]], axis=0
    )
    for peer in range(NB):
        out[peer, 0:8, :] = head
        out[peer, 8:24, :] = sums[...]
        ahead = (me + 1 == peer).astype(F32)
        behind = (me - 1 == peer).astype(F32)
        for i, (r, l) in enumerate(((r0, l0), (r1, l1), (r2, l2))):
            out[peer, 24 + 8 * i : 32 + 8 * i, :] = r * ahead + l * behind


def neighbours(recv, me, count):
    before = jnp.maximum(me - 1, 0)
    after = jnp.minimum(me + 1, NB - 1)
    keep_l = (me > 0).astype(F32)
    keep_r = (me < NB - 1).astype(F32)
    start = 24
    left = [recv[before, start + 8 * i : start + 8 * i + 8, :] * keep_l for i in range(count)]
    right = [recv[after, start + 8 * i : start + 8 * i + 8, :] * keep_r for i in range(count)]
    return left, right, keep_l, keep_r


def edge_terms(blocks):
    sv = turn(blocks[2], 64)
    film, owner = turn(blocks[1][0:1], 64), turn(blocks[1][1:2], 64)
    return sv, blocks[2], film, owner


def second_kernel(
    recv, mt, fluid, sv, pv, film, solid, cond, owner, lo, hi,
    fluid2, first_out, second_out, metal, tm, fluid1,
):
    me = lax.axis_index("blk")
    left, right, keep_l, keep_r = neighbours(recv, me, 3)
    sv_l, pv_l, film_l, own_l = edge_terms(left)
    sv_r, pv_r, film_r, own_r = edge_terms(right)
    wall0, under0 = recv[:, 0, :], recv[:, 1, :]
    c0, c1 = recv[:, 2, :], recv[:, 3, :]
    a0, h = recv[0, 8:16, :], recv[0, 16:24, :]
    for j in range(1, NB):
        a0, h = a0 + recv[j, 8:16, :], h + recv[j, 16:24, :]
    inflow0 = a0 - h * wall0
    wall1 = strip_row(wall0, conduct_of(c0, wall0), under0, conduct_of(c1, under0))
    wall1 = wall1 + SOLID_STEP * inflow0

    mine_right, mine_left = mt[pl.ds(1, FZ, stride=4), :], mt[pl.ds(2, FZ, stride=4), :]
    new_l = halo_column(
        left[0], left[0], left[1], mine_left, sv_l, pv_l, film_l,
        pick_lane(own_l, wall0, FS - 1), keep_l,
    )
    new_r = halo_column(
        right[0], right[0], mine_right, right[1], sv_r, pv_r, film_r,
        pick_lane(own_r, wall0, 0), keep_r,
    )
    tm[...] = jnp.zeros((FS, FS), F32)
    tm[pl.ds(0, FZ, stride=2), :] = right[0]
    tm[pl.ds(1, FZ, stride=2), :] = left[0]
    tm[16:24, :] = left[0]
    tm[24:32, :] = right[0]
    tm[pl.ds(32, FZ, stride=2), :] = new_r
    tm[pl.ds(33, FZ, stride=2), :] = new_l
    turned = tm[...].T
    columns = turned[:FP]
    deep = turned[64 : 64 + SD]
    thin = lanes(SD)
    halo = jnp.where(thin >= 124, turn(deep, 108), jnp.where(thin < 4, turn(deep, 104), 0.0))
    c_halo = jnp.where(thin >= 124, turn(deep, 104), jnp.where(thin < 4, turn(deep, 100), 0.0))
    keep = jnp.where(thin >= 64, keep_l, keep_r)

    low, high = lo[8:16, :], hi[8:16, :]
    first, last = fluid[:, 0, :], fluid[:, FP - 1, :]
    wall_lo = pick(lo[34:35, :], recv[:, 4, :])
    wall_hi = pick(hi[34:35, :], recv[:, 5, :])
    new_low = halo_row(
        low, lo[0:8, :], first, turn(left[0], 32), turn(right[0], 31),
        lo[16:24, :], lo[24:32, :], lo[32:33, :], wall_lo,
    )
    new_high = halo_row(
        high, last, hi[0:8, :], turn(left[0], 31), turn(right[0], 30),
        hi[16:24, :], hi[24:32, :], hi[32:33, :], wall_hi,
    )
    named = owner[...]
    walls0, walls1 = pick(named, wall0), pick(named, wall1)
    advance(fluid, fluid1, low, high, columns, 0, sv, pv, film[...], walls0)
    advance(fluid1, fluid2, new_low, new_high, columns, 32, sv, pv, film[...], walls1)
    (flux,) = by_owner(named, [film[...] * (fluid1[0] - walls1)])

    own, halo = metal_step(solid[...], halo, cond[...], c_halo, keep)
    own, halo = add_inflow(own, halo, inflow0, me, keep)
    own, halo = metal_step(own, halo, cond[...], c_halo, keep)
    metal[0:SD, :] = own
    metal[SD : 2 * SD, :] = halo
    metal[2 * SD : 3 * SD, :] = c_halo
    even = lax.axis_index("sec") % 2 == 0
    for i, (inner, outer) in enumerate(((FP - 2, 1), (FP - 1, 0))):
        up, down = fluid2[:, inner, :], fluid2[:, outer, :]
        first_out[8 * i : 8 * i + 8, :] = jnp.where(even, up, down)
        second_out[8 * i : 8 * i + 8, :] = jnp.where(even, down, up)
    for ref in (first_out, second_out):
        ref[16:24, :] = flux
        ref[24:32, :] = own[0:8]


def sums_kernel(recv, fluid2, sv, pv, film, owner, mt, sums):
    me = lax.axis_index("blk")
    left, right, keep_l, keep_r = neighbours(recv, me, 3)
    _, _, film_l, own_l = edge_terms(left)
    sv_r, _, film_r, own_r = edge_terms(right)
    lane, sub = lanes(FP), subs(FP)
    named = owner[...]
    x, f = fluid2[0], film[...]
    low = jnp.where(sub == 0, 0.0, turn(x, 1, 0))
    high = jnp.where(sub == FP - 1, 0.0, turn(x, -1, 0))
    before = jnp.where(lane == 0, 0.0, turn(x, 1))
    after = jnp.where(lane == FS - 1, 0.0, turn(x, -1))
    moved = stencil(x, low, high, before, after, x, fluid2[1], sv[0], pv[0]) - WALL * f * x
    a2, b3, h2 = by_owner(named, [f * x, f * moved, f * f])
    whole = jnp.concatenate([gather_columns(fluid2, lane), jnp.zeros((FP, FS), F32)], axis=0)
    mt[0:FS, :] = whole.T
    thin = subs(NB)
    inside = lanes(NB) < FP
    right_term = film_r * (SPREAD + ADVECT * sv_r[0:1]) * mt[1:2, :] * keep_r
    left_term = film_l * SPREAD * mt[2:3, :] * keep_l

    def shared(own_row, term):
        hit = (jnp.broadcast_to(own_row, (NB, FS)) == thin.astype(F32)) & inside
        return jnp.sum(jnp.where(hit, term, 0.0), axis=1, keepdims=True)

    b3 = b3 + jnp.where(lanes(NB) == 0, shared(own_r, right_term), 0.0)
    b3 = b3 + jnp.where(lanes(NB) == FS - 1, shared(own_l, left_term), 0.0)
    top, end = f[0:1], f[FP - 1 : FP]
    up = top * (SPREAD + ADVECT * jnp.maximum(pv[0, 0:1, :], 0.0))
    down = end * (SPREAD + ADVECT * jnp.maximum(-pv[0, FP - 1 : FP, :], 0.0))
    mt[FS : FS + 8, :] = jnp.concatenate(
        [up, down, named[0:1], named[FP - 1 : FP], jnp.zeros((4, FS), F32)],
        axis=0,
    )
    sums[0:8, :], sums[8:16, :], sums[16:24, :] = a2, b3, h2


def send_kernel(recv, mt, sums, mine, metal, first, second, out, lo, hi):
    sort_rows(first, second, lo, hi)
    me = lax.axis_index("blk")
    sub = subs(NB)
    rows = sub.astype(F32)
    (r0, r1), (l0, l1) = column_blocks(mt)
    low, high = lo[8:16, :], hi[8:16, :]
    r0 = with_corners(r0, low, high, FS - 1)
    l0 = with_corners(l0, low, high, 0)
    b3 = sums[8:16, :]
    b3 = b3 + jnp.where(rows == mt[FS + 2 : FS + 3, :], mt[FS : FS + 1, :] * low[0:1], 0.0)
    b3 = b3 + jnp.where(rows == mt[FS + 3 : FS + 4, :], mt[FS + 1 : FS + 2, :] * high[0:1], 0.0)
    relay_lo = pick(recv[:, 6, :], lo[16:24, :])
    relay_hi = pick(recv[:, 7, :], hi[16:24, :])
    h2 = sums[16:24, :]
    for peer in range(NB):
        out[peer, 0:8, :] = jnp.concatenate(
            [
                metal[0:2, :],
                lo[24:25, :],
                hi[24:25, :],
                b3[peer : peer + 1],
                h2[peer : peer + 1],
                relay_lo[peer : peer + 1],
                relay_hi[peer : peer + 1],
            ],
            axis=0,
        )
        out[peer, 8:16, :] = mine[16:24, :]
        out[peer, 16:24, :] = sums[0:8, :]
        ahead = (me + 1 == peer).astype(F32)
        behind = (me - 1 == peer).astype(F32)
        out[peer, 24:32, :] = r0 * ahead + l0 * behind
        out[peer, 32:40, :] = r1 * ahead + l1 * behind


def last_kernel(
    recv1, recv, mt, fluid2, sv, pv, film, cond, owner, lo, hi, lo1, hi1, metal, fluid_out, solid_out,
    tm, fluid3,
):
    me = lax.axis_index("blk")
    stat_l, stat_r, keep_l, keep_r = neighbours(recv, me, 3)
    left, right, _, _ = neighbours(recv1, me, 2)
    sv_l, pv_l, film_l, own_l = edge_terms(stat_l)
    sv_r, pv_r, film_r, own_r = edge_terms(stat_r)
    c0, c1 = recv[:, 2, :], recv[:, 3, :]
    h = recv[0, 16:24, :]
    tail, inflow1, a2 = recv1[0, 0:8, :], recv1[0, 8:16, :], recv1[0, 16:24, :]
    for j in range(1, NB):
        h = h + recv[j, 16:24, :]
        tail = tail + recv1[j, 0:8, :]
        inflow1 = inflow1 + recv1[j, 8:16, :]
        a2 = a2 + recv1[j, 16:24, :]
    wall2 = recv1[:, 0, :] + SOLID_STEP * inflow1
    under2 = recv1[:, 1, :]
    inflow2 = a2 - h * wall2
    wall3 = strip_row(wall2, conduct_of(c0, wall2), under2, conduct_of(c1, under2))
    wall3 = wall3 + SOLID_STEP * inflow2
    inflow3 = tail[4:5] + WALL * tail[5:6] * wall2 - h * wall3
    wall_lo = pick(lo[34:35, :], recv1[:, 2, :]) + SOLID_STEP * tail[6:7]
    wall_hi = pick(hi[34:35, :], recv1[:, 3, :]) + SOLID_STEP * tail[7:8]

    mine_right, mine_left = mt[pl.ds(1, FZ, stride=4), :], mt[pl.ds(2, FZ, stride=4), :]
    new_l = halo_column(
        left[0], left[0], left[1], mine_left, sv_l, pv_l, film_l,
        pick_lane(own_l, wall2, FS - 1), keep_l,
    )
    new_r = halo_column(
        right[0], right[0], mine_right, right[1], sv_r, pv_r, film_r,
        pick_lane(own_r, wall2, 0), keep_r,
    )
    tm[...] = jnp.zeros((FS, FS), F32)
    tm[pl.ds(0, FZ, stride=2), :] = right[0]
    tm[pl.ds(1, FZ, stride=2), :] = left[0]
    tm[pl.ds(32, FZ, stride=2), :] = new_r
    tm[pl.ds(33, FZ, stride=2), :] = new_l
    columns = tm[...].T[:FP]
    low, high = lo1[8:16, :], hi1[8:16, :]
    first, last = fluid2[:, 0, :], fluid2[:, FP - 1, :]
    new_low = halo_row(
        low, lo1[0:8, :], first, turn(left[0], 32), turn(right[0], 31),
        lo[16:24, :], lo[24:32, :], lo[32:33, :], wall_lo,
    )
    new_high = halo_row(
        high, last, hi1[0:8, :], turn(left[0], 31), turn(right[0], 30),
        hi[16:24, :], hi[24:32, :], hi[32:33, :], wall_hi,
    )
    named = owner[...]
    advance(fluid2, fluid3, low, high, columns, 0, sv, pv, film[...], pick(named, wall2))
    advance(fluid3, fluid_out, new_low, new_high, columns, 32, sv, pv, film[...], pick(named, wall3))

    thin = lanes(SD)
    keep = jnp.where(thin >= 64, keep_l, keep_r)
    own, halo, c_halo = metal[0:SD, :], metal[SD : 2 * SD, :], metal[2 * SD : 3 * SD, :]
    own, halo = add_inflow(own, halo, inflow1, me, keep)
    own, halo = metal_step(own, halo, cond[...], c_halo, keep)
    own, halo = add_inflow(own, halo, inflow2, me, keep)
    own, halo = metal_step(own, halo, cond[...], c_halo, keep)
    own, _ = add_inflow(own, halo, inflow3, me, keep)
    solid_out[...] = own


def shape(*dims):
    return jax.ShapeDtypeStruct(dims, F32)


VMEM = pl.BlockSpec(memory_space=pltpu.VMEM)
GRANT = 54 * 1024 * 1024
HBM = pl.BlockSpec(memory_space=pltpu.HBM)


def call(kernel, outs, args, name, scratch=(), far=0, limit=32 * 1024 * 1024):
    return pl.pallas_call(
        kernel,
        out_shape=outs,
        in_specs=[HBM] * far + [VMEM] * (len(args) - far),
        out_specs=jax.tree.map(lambda _: VMEM, outs),
        scratch_shapes=scratch,
        name=name,
        compiler_params=pltpu.CompilerParams(vmem_limit_bytes=limit),
    )(*args)


def both_ways(first, second):
    count = lax.axis_size("sec")
    near = [(i, i ^ 1) for i in range(count)]
    far = [(i, (i + 1 if i % 2 else i - 1) % count) for i in range(count)]
    second = lax.ppermute(second, "sec", far)
    return lax.ppermute(first, "sec", near), second


def swap(message):
    return lax.all_to_all(message, "blk", split_axis=0, concat_axis=0, tiled=True)


def two_exchanges(fluid, sv, pv, film, solid, cond, face_owner):
    owner = face_owner.reshape(1, FP)
    solid, cond = solid.reshape(SD, FS), cond.reshape(SD, FS)

    field = shape(FZ, FP, FS)
    first, second = both_ways(
        *call(
            rows_kernel,
            (shape(40, FS), shape(40, FS)),
            (fluid, sv, pv, film, solid, owner),
            "rows",
            [
                pltpu.VMEM((6, FZ, 8, FS), F32),
                pltpu.VMEM((3, 8, FS), F32),
                pltpu.VMEM((1, FP), jnp.int32),
                pltpu.SemaphoreType.DMA((10,)),
            ],
            far=6,
            limit=GRANT - 56 * 1024,
        )
    )
    mt, sums, fluid, sv, pv, film, solid, cond, owner = call(
        first_kernel,
        (
            shape(FS, FS), shape(16, FS), field, field, field,
            shape(FP, FS), shape(SD, FS), shape(SD, FS), shape(FP, FS),
        ),
        (fluid, sv, pv, film, solid, cond, owner),
        "columns",
        [pltpu.VMEM((1, FP), jnp.int32), pltpu.SemaphoreType.DMA((10,))],
        far=7,
        limit=GRANT - 1104 * 1024,
    )
    message, lo, hi = call(
        pack_kernel,
        (shape(NB, R0, FS), shape(40, FS), shape(40, FS)),
        (mt, sums, solid, cond, first, second),
        "pack",
    )
    recv = swap(message)
    work = [pltpu.VMEM((FS, FS), F32), pltpu.VMEM((FZ, FP, FS), F32)]
    fluid2, first, second, metal = call(
        second_kernel,
        (field, shape(32, FS), shape(32, FS), shape(3 * SD, FS)),
        (recv, mt, fluid, sv, pv, film, solid, cond, owner, lo, hi),
        "steps",
        work,
    )
    first1, second1 = both_ways(first, second)
    mt1, sums1 = call(
        sums_kernel,
        (shape(FS + 8, FS), shape(24, FS)),
        (recv, fluid2, sv, pv, film, owner),
        "sums",
    )
    message, lo1, hi1 = call(
        send_kernel,
        (shape(NB, R1, FS), shape(32, FS), shape(32, FS)),
        (recv, mt1, sums1, first, metal, first1, second1),
        "pack",
    )
    recv1 = swap(message)
    fluid, solid = call(
        last_kernel,
        (field, shape(SD, FS)),
        (recv1, recv, mt1, fluid2, sv, pv, film, cond, owner, lo, hi, lo1, hi1, metal),
        "steps",
        work,
    )
    return fluid, solid.reshape(1, SD, FS)


def padded(block, sides, width, periodic):
    for axis, dim in sides:
        count = lax.axis_size(axis)
        forward = [(i, i + 1) for i in range(count - 1)]
        if periodic:
            forward.append((count - 1, 0))
        backward = [(target, source) for source, target in forward]
        low = lax.ppermute(
            lax.slice_in_dim(block, block.shape[dim] - width, None, axis=dim), axis, forward
        )
        high = lax.ppermute(lax.slice_in_dim(block, 0, width, axis=dim), axis, backward)
        block = jnp.concatenate([low, block, high], axis=dim)
    return block


def fluid_update(
    fluid, stream_velocity, pitch_velocity, wall_flux, pitch_extended, stream_extended
):
    pitch_prev = pitch_extended[:, :-2]
    pitch_next = pitch_extended[:, 2:]
    stream_prev = stream_extended[:, :, :-2]
    stream_next = stream_extended[:, :, 2:]
    span_prev = jnp.concatenate([fluid[:1], fluid[:-1]], 0)
    span_next = jnp.concatenate([fluid[1:], fluid[-1:]], 0)
    spread = SPREAD * (
        pitch_prev + pitch_next + stream_prev + stream_next + span_prev + span_next - 6.0 * fluid
    )
    carried = (
        -ADVECT * stream_velocity * (fluid - stream_prev)
        - ADVECT * jnp.maximum(pitch_velocity, 0.0) * (fluid - pitch_prev)
        + ADVECT * jnp.maximum(-pitch_velocity, 0.0) * (pitch_next - fluid)
    )
    updated = fluid + spread + carried
    return updated.at[0].add(-WALL * wall_flux)


def solid_update(solid, conduct, inflow, solid_extended, conduct_extended):
    stream_prev = solid_extended[..., :-2]
    stream_next = solid_extended[..., 2:]
    conduct_prev = conduct_extended[..., :-2]
    conduct_next = conduct_extended[..., 2:]
    depth_prev = jnp.concatenate([solid[:, :1], solid[:, :-1]], 1)
    depth_next = jnp.concatenate([solid[:, 1:], solid[:, -1:]], 1)
    kdepth_prev = jnp.concatenate([conduct[:, :1], conduct[:, :-1]], 1)
    kdepth_next = jnp.concatenate([conduct[:, 1:], conduct[:, -1:]], 1)
    flow = (
        0.5 * (conduct + conduct_prev) * (stream_prev - solid)
        + 0.5 * (conduct + conduct_next) * (stream_next - solid)
        + 0.5 * (conduct + kdepth_prev) * (depth_prev - solid)
        + 0.5 * (conduct + kdepth_next) * (depth_next - solid)
    )
    updated = solid + SOLID_STEP * flow
    updated = updated.at[:, 0].add(SOLID_STEP * inflow)
    updated = updated.at[:, -1].add(SOLID_STEP * COOLING * (COOLANT - solid[:, -1]))
    return updated


def local(
    fluid_temp, stream_velocity, pitch_velocity, film_coeff, solid_temp, conductivity, face_owner
):
    span_cells, pitch_cells, stream_cells = fluid_temp.shape
    depth_cells = solid_temp.shape[1]
    block_count = lax.axis_size("blk")
    capacity = max(2, (pitch_cells + block_count - 1) // block_count)
    owners = face_owner.reshape(-1)
    onehot = (owners[:, None] == jnp.arange(block_count, dtype=jnp.int32)[None, :]).astype(
        jnp.float32
    )
    same_owner = owners[:, None] == owners[None, :]
    earlier = lax.broadcasted_iota(jnp.int32, (pitch_cells, pitch_cells), 0) < lax.broadcasted_iota(
        jnp.int32, (pitch_cells, pitch_cells), 1
    )
    slot_rank = jnp.sum((same_owner & earlier).astype(jnp.int32), axis=0)
    slot_table = (slot_rank[None, :] == jnp.arange(capacity, dtype=jnp.int32)[:, None]).astype(
        jnp.float32
    )
    placing = onehot.T[:, None, :] * slot_table[None, :, :]
    fluid = fluid_temp
    solid = solid_temp
    gas_rows = span_cells * pitch_cells
    for subiter in range(SUB):
        wall_row = solid[0, 0:1, :]
        wall_temp = jnp.dot(
            onehot,
            lax.all_gather(wall_row, "blk", axis=0, tiled=True),
            precision=lax.Precision.HIGHEST,
            preferred_element_type=jnp.float32,
        )
        flux = film_coeff * (fluid[0] - wall_temp)
        outgoing = jnp.einsum("ocb,bf->ocf", placing, flux, precision=lax.Precision.HIGHEST)
        received = lax.all_to_all(outgoing, "blk", split_axis=0, concat_axis=0, tiled=True)
        inflow = jnp.sum(received, axis=(0, 1))
        conduct = conductivity * (1.0 + 0.25 * jnp.tanh(solid))
        stacked = jnp.concatenate([fluid.reshape(gas_rows, stream_cells), solid[0], conduct[0]], 0)
        stream_ext = padded(stacked, (("blk", 1),), 1, False)
        pitch_extended = padded(fluid, (("sec", 1),), 1, True)
        fluid_stream = stream_ext[:gas_rows].reshape(span_cells, pitch_cells, stream_cells + 2)
        solid_stream = stream_ext[gas_rows : gas_rows + depth_cells][None]
        conduct_stream = stream_ext[gas_rows + depth_cells :][None]
        fluid = fluid_update(
            fluid, stream_velocity, pitch_velocity, flux, pitch_extended, fluid_stream
        )
        solid = solid_update(solid, conduct, inflow[None, :], solid_stream, conduct_stream)
    return (fluid, solid)


def solution(mesh):
    placed = (
        P(None, "sec", "blk"),
        P(None, "sec", "blk"),
        P(None, "sec", "blk"),
        P("sec", "blk"),
        P("sec", None, "blk"),
        P("sec", None, "blk"),
        P("sec", "blk", None, None),
    )
    sizes = dict(mesh.shape)

    def chosen(*args):
        fits = args[0].shape == (FZ, FP, FS) and args[4].shape == (1, SD, FS)
        fits = fits and sizes["blk"] == NB and sizes["sec"] % 2 == 0
        return two_exchanges(*args) if fits else local(*args)

    return jax.shard_map(
        chosen,
        mesh=mesh,
        in_specs=placed,
        out_specs=(P(None, "sec", "blk"), P("sec", None, "blk")),
        check_vma=False,
    )
```

```python
import jax
import jax.numpy as jnp
from jax import lax
from jax.experimental import pallas as pl
from jax.experimental.pallas import tpu as pltpu
from jax.sharding import PartitionSpec as P

SUB = 4


ADVECT = 0.4
SPREAD = 0.04
WALL = 0.4
SOLID_STEP = 0.04
COOLING = 0.5
COOLANT = -1.0

F32 = jnp.float32
NB = 8
FZ = 8
FP = 64
FS = 128
SD = 32
R0 = 40
R1 = 32
ROWS = 48
OPEN_ROOM = 56 * 1024


def lanes(rows):
    return lax.broadcasted_iota(jnp.int32, (rows, FS), 1)


def subs(rows):
    return lax.broadcasted_iota(jnp.int32, (rows, FS), 0)


def turn(x, shift, axis=1):
    return pltpu.roll(x, shift % x.shape[axis], axis)


def by_owner(owner, values):
    sub = subs(NB)
    outs = [jnp.zeros((NB, FS), F32) for _ in values]
    for o in range(NB):
        mine = owner == o
        for i, value in enumerate(values):
            total = jnp.sum(jnp.where(mine, value, 0.0), axis=0, keepdims=True)
            outs[i] = jnp.where(sub == o, total, outs[i])
    return outs


def pick(owner, table):
    out = jnp.zeros(owner.shape, F32)
    for o in range(NB):
        out = jnp.where(owner == o, table[o : o + 1], out)
    return out


def pick_lane(owner_row, table, lane):
    column = jnp.broadcast_to(table[:, lane : lane + 1], (NB, FS))
    named = jnp.broadcast_to(owner_row, (NB, FS)) == subs(NB).astype(F32)
    return jnp.sum(jnp.where(named, column, 0.0), axis=0, keepdims=True)


def stencil(x, low, high, left, right, below, above, sv, pv):
    spread = SPREAD * (low + high + left + right + below + above - 6.0 * x)
    carried = (
        -ADVECT * sv * (x - left)
        - ADVECT * jnp.maximum(pv, 0.0) * (x - low)
        + ADVECT * jnp.maximum(-pv, 0.0) * (high - x)
    )
    return x + spread + carried


def span(x):
    sub = subs(FZ)
    below = jnp.where(sub == 0, x, turn(x, 1, 0))
    above = jnp.where(sub == FZ - 1, x, turn(x, FZ - 1, 0))
    return below, above


def halo_row(x, low, high, left_corner, right_corner, sv, pv, flux):
    lane = lanes(FZ)
    left = jnp.where(lane == 0, left_corner, turn(x, 1))
    right = jnp.where(lane == FS - 1, right_corner, turn(x, -1))
    below, above = span(x)
    new = stencil(x, low, high, left, right, below, above, sv, pv)
    return new - jnp.where(subs(FZ) == 0, WALL * flux, 0.0)


def edge_part(x, low_end, high_end, left, right, sv, pv, film):
    lane = lanes(FZ)
    low = jnp.where(lane == 0, low_end, turn(x, 1))
    high = jnp.where(lane == FP - 1, high_end, turn(x, -1))
    below, above = span(x)
    new = stencil(x, low, high, left, right, below, above, sv, pv)
    return new - jnp.where(subs(FZ) == 0, WALL * film * x, 0.0)


def set_row(x, row, at):
    if at == 0:
        return jnp.concatenate([jnp.where(subs(8) == 0, row, x[:8]), x[8:]], axis=0)
    return jnp.concatenate([x[:-8], jnp.where(subs(8) == 7, row, x[-8:])], axis=0)


def advance(src, dst, low_row, high_row, columns, base, sv, pv, film, wall):
    lane = lanes(FP)
    for z in range(FZ):
        x = src[z]
        low = set_row(turn(x, 1, 0), low_row[z : z + 1], 0)
        high = set_row(turn(x, -1, 0), high_row[z : z + 1], 1)
        edge = turn(columns, -(base + 2 * z + 1))
        left = jnp.where(lane == 0, edge, turn(x, 1))
        right = jnp.where(lane == FS - 1, edge, turn(x, -1))
        new = stencil(
            x, low, high, left, right, src[max(z - 1, 0)], src[min(z + 1, FZ - 1)], sv[z], pv[z]
        )
        if z == 0:
            new = new - WALL * film * (x - wall)
        dst[z] = new


def strip_row(here, k_here, under, k_under):
    sub, lane = subs(NB), lanes(NB)

    def prev(x):
        moved = turn(x, 1)
        carried = jnp.where(sub == 0, 0.0, turn(moved, 1, 0))
        return jnp.where(lane == 0, carried, moved)

    def following(x):
        moved = turn(x, -1)
        carried = jnp.where(sub == NB - 1, 0.0, turn(moved, -1, 0))
        return jnp.where(lane == FS - 1, carried, moved)

    flow = (
        0.5 * (k_here + prev(k_here)) * (prev(here) - here)
        + 0.5 * (k_here + following(k_here)) * (following(here) - here)
        + 0.5 * (k_here + k_under) * (under - here)
    )
    return here + SOLID_STEP * flow


def conduct_of(conductivity, solid):
    return conductivity * (1.0 + 0.25 * jnp.tanh(solid))


def metal_step(own, halo, c_own, c_halo, keep):
    depth_cells = own.shape[0]
    k_own, k_halo = conduct_of(c_own, own), conduct_of(c_halo, halo)
    lane, sub = lanes(depth_cells), subs(depth_cells)

    def depth(x):
        up = jnp.where(sub == 0, x, turn(x, 1, 0))
        down = jnp.where(sub == depth_cells - 1, x, turn(x, -1, 0))
        return up, down

    def stream(x, other):
        prev = jnp.where(lane == 0, turn(other, 1), turn(x, 1))
        following = jnp.where(lane == FS - 1, turn(other, -1), turn(x, -1))
        return prev, following

    def update(x, k, other, k_other):
        flow = jnp.zeros_like(x)
        for a, ka in zip(stream(x, other) + depth(x), stream(k, k_other) + depth(k)):
            flow = flow + 0.5 * (k + ka) * (a - x)
        new = x + SOLID_STEP * flow
        return new + jnp.where(sub == SD - 1, SOLID_STEP * COOLING * (COOLANT - x), 0.0)

    return update(own, k_own, halo, k_halo), update(halo, k_halo, own, k_own) * keep


def row_of(table, index):
    return jnp.sum(jnp.where(subs(NB) == index, table, 0.0), axis=0, keepdims=True)


def set_walls(own, halo, walls, me, keep):
    sub, lane = subs(own.shape[0]), lanes(own.shape[0])
    beside = jnp.where(lane >= FS // 2, row_of(walls, me - 1), row_of(walls, me + 1)) * keep
    return jnp.where(sub == 0, row_of(walls, me), own), jnp.where(sub == 0, beside, halo)


def metal_halo(turned, rows):
    deep = turned[FP : FP + rows]
    lane = lanes(rows)

    def placed(left, right):
        return jnp.where(
            lane >= 124, turn(deep, left), jnp.where(lane < 4, turn(deep, right), 0.0)
        )

    return placed(108, 104), placed(104, 100)


def keeps(me):
    return (me > 0).astype(F32), (me < NB - 1).astype(F32)


def block_of(recv, me, start):
    keep_l, keep_r = keeps(me)
    before, after = jnp.maximum(me - 1, 0), jnp.minimum(me + 1, NB - 1)
    part = slice(start, start + 8)
    return recv[before, part, :] * keep_l, recv[after, part, :] * keep_r


def column_blocks(mt):
    right = mt[pl.ds(1, FZ, stride=4), :], mt[pl.ds(0, FZ, stride=4), :]
    left = mt[pl.ds(2, FZ, stride=4), :], mt[pl.ds(3, FZ, stride=4), :]
    return right, left


def flows(mt):
    right, left = mt[pl.ds(32, FZ, stride=2), :], mt[pl.ds(33, FZ, stride=2), :]
    return (turn(right, 64), right, mt[48:49, :]), (turn(left, 64), left, mt[49:50, :])


def gather_columns(fluid, lane):
    acc = jnp.zeros((FP, FS), F32)
    for z in range(FZ):
        acc = jnp.where(lane // 4 == z, turn(fluid[z], 4 * z + 2), acc)
    return acc


def sorted_rows(first, second):
    even = lax.axis_index("sec") % 2 == 0
    return (
        lambda a, b: jnp.where(even, second[a:b, :], first[a:b, :]),
        lambda a, b: jnp.where(even, first[a:b, :], second[a:b, :]),
    )


def send_rows(first, second, start, up, down):
    even = lax.axis_index("sec") % 2 == 0
    part = slice(start, start + up.shape[0])
    first[part, :] = jnp.where(even, up, down)
    second[part, :] = jnp.where(even, down, up)


def up_factor(pv):
    return SPREAD + ADVECT * jnp.maximum(pv, 0.0)


def down_factor(pv):
    return SPREAD + ADVECT * jnp.maximum(-pv, 0.0)


def fetch(copies, sems):
    started = [
        pltpu.make_async_copy(src, dst, sems.at[i]) for i, (src, dst) in enumerate(copies)
    ]
    for copy in started:
        copy.start()
    return started


def open_kernel(
    fluid_in, sv_in, pv_in, film_in, solid_in, cond_in, owner,
    out, first, second, mt, names, fluid, sv, pv, film, solid, cond, ids, sems,
):
    me = lax.axis_index("blk")
    half = FZ // 2
    copies = [(owner, ids), (film_in, film), (solid_in, solid), (cond_in, cond)]
    for src, dst in ((fluid_in, fluid), (pv_in, pv), (sv_in, sv)):
        for part in range(2):
            copies.append((src.at[pl.ds(half * part, half)], dst.at[pl.ds(half * part, half)]))
    started = fetch(copies, sems)
    lane = lanes(FP)
    for copy in started[:4]:
        copy.wait()
    ids_row = jnp.concatenate([ids[...].astype(F32), jnp.zeros((1, FS - FP), F32)], axis=1)
    named = jnp.broadcast_to(ids_row, (FS, FS)).T[:FP]
    names[...] = named
    metal = jnp.zeros((SD, FS), F32)
    thin = lanes(SD)
    s, c = solid[...], cond[...]
    for k in range(4):
        metal = jnp.where(thin == 4 * k + 1, turn(s, 3 * k + 5), metal)
        metal = jnp.where(thin == 4 * k + 2, turn(s, 3 * k + 2), metal)
        metal = jnp.where(thin == 4 * k + 17, turn(c, 3 * k + 21), metal)
        metal = jnp.where(thin == 4 * k + 18, turn(c, 3 * k + 18), metal)
    started[4].wait()
    a0, h = by_owner(named, [film[...] * fluid[0], film[...]])
    started[5].wait()
    top = gather_columns(fluid, lane)
    send_rows(first, second, 0, fluid[:, FP - 1, :], fluid[:, 0, :])
    blank = jnp.zeros((7, FS), F32)
    send_rows(
        first, second, 40,
        jnp.concatenate([film[FP - 1 : FP, :], blank], axis=0),
        jnp.concatenate([film[0:1, :], blank], axis=0),
    )
    for copy in started[6:]:
        copy.wait()
    send_rows(first, second, 8, sv[:, FP - 2, :], sv[:, 1, :])
    send_rows(first, second, 16, sv[:, FP - 1, :], sv[:, 0, :])
    send_rows(first, second, 24, pv[:, FP - 2, :], pv[:, 1, :])
    send_rows(first, second, 32, pv[:, FP - 1, :], pv[:, 0, :])
    bottom = jnp.zeros((FP, FS), F32)
    pair = (lane - 32) // 2
    for z in range(FZ):
        here = (pair == z) & (lane >= 32)
        top = jnp.where(here, turn(pv[z], 33 + 2 * z), top)
        bottom = jnp.where(here, turn(sv[z], 33 + 2 * z), bottom)
    top = jnp.where(lane // 2 == 24, turn(film[...], 49), top)
    top = jnp.where(lane == 50, named, top)
    metal = jnp.where(thin < 32, metal, bottom[:SD])
    mt[...] = jnp.concatenate([top, metal, bottom[SD:]], axis=0).T

    (r0, r1), (l0, l1) = column_blocks(mt)
    (sv_r, pv_r, film_r), (sv_l, pv_l, film_l) = flows(mt)
    wide = lanes(FZ)
    right_part = edge_part(r0, 0.0, 0.0, r1, 0.0, sv_r, pv_r, film_r)
    left_part = edge_part(l0, 0.0, 0.0, 0.0, l1, sv_l, pv_l, film_l)
    right_part = jnp.where(wide < FP, right_part, SPREAD)
    left_part = jnp.where(wide < FP, left_part, turn(SPREAD + ADVECT * sv_l, 64))

    def with_factors(block, p):
        block = jnp.where(wide == 96, turn(up_factor(p), 96), block)
        return jnp.where(wide == 97, turn(down_factor(p), 97 - (FP - 1)), block)

    r0, l0 = with_factors(r0, pv_r), with_factors(l0, pv_l)
    owner_row = turn(mt[50:51, :], 64)
    inside = lanes(1) < FP
    right_row, left_row = (jnp.where(inside, f, owner_row) for f in (film_r, film_l))
    head = jnp.concatenate([s[0:2], c[0:2], named[FP - 1 : FP], named[0:1]], axis=0)
    for peer in range(NB):
        ahead = (me + 1 == peer).astype(F32)
        behind = (me - 1 == peer).astype(F32)
        special = right_row * ahead + left_row * behind
        out[peer, 0:8, :] = jnp.concatenate([head, special, special], axis=0)
        out[peer, 8:16, :] = a0
        out[peer, 16:24, :] = h
        same = (me == peer).astype(F32)
        out[peer, 24:32, :] = r0 * ahead + l0 * behind + r0 * same
        out[peer, 32:40, :] = right_part * ahead + left_part * behind + l0 * same


def halo_columns(known_l, known_r, factor_l, factor_r, rows, mine_right, mine_left, walls, me):
    keep_l, keep_r = keeps(me)
    (film_l, own_l), (film_r, own_r) = rows
    top = subs(FZ) == 0
    wall_l, wall_r = pick_lane(own_l, walls, FS - 1), pick_lane(own_r, walls, 0)
    new_l = known_l + factor_l * mine_left + jnp.where(top, WALL * film_l * wall_l, 0.0)
    new_r = known_r + factor_r * mine_right + jnp.where(top, WALL * film_r * wall_r, 0.0)
    return new_l * keep_l, new_r * keep_r


def edge_rows(recv, me):
    return [(block[6:7], turn(block[6:7], 64)) for block in block_of(recv, me, 0)]


def first_kernel(
    recv, fluid, sv, pv, film, solid, cond, owner, first, second,
    fluid1, first_out, second_out, turned, side, tm,
):
    me = lax.axis_index("blk")
    lo, hi = sorted_rows(first, second)
    left, right = block_of(recv, me, 24)
    part_l, part_r = block_of(recv, me, 32)
    wall0, under0 = recv[:, 0, :], recv[:, 1, :]
    c0, c1 = recv[:, 2, :], recv[:, 3, :]
    a0, h = recv[0, 8:16, :], recv[0, 16:24, :]
    for j in range(1, NB):
        a0, h = a0 + recv[j, 8:16, :], h + recv[j, 16:24, :]
    wall1 = strip_row(wall0, conduct_of(c0, wall0), under0, conduct_of(c1, under0))
    wall1 = wall1 + SOLID_STEP * (a0 - h * wall0)

    mine_right, mine_left = recv[me, 24:32, :], recv[me, 32:40, :]
    new_l, new_r = halo_columns(
        part_l, part_r, turn(part_l, 64), turn(part_r, 64), edge_rows(recv, me),
        mine_right, mine_left, wall0, me,
    )
    tm[...] = jnp.zeros((FS, FS), F32)
    tm[pl.ds(0, FZ, stride=2), :] = right
    tm[pl.ds(1, FZ, stride=2), :] = left
    tm[16:24, :] = left
    tm[24:32, :] = right
    tm[pl.ds(32, FZ, stride=2), :] = new_r
    tm[pl.ds(33, FZ, stride=2), :] = new_l
    turned[...] = tm[...].T
    named = owner[...]
    walls0, walls1 = pick(named, wall0), pick(named, wall1)
    advance(fluid, fluid1, lo(0, 8), hi(0, 8), turned[:FP, :], 0, sv, pv, film[...], walls0)
    flux = film[...] * (fluid1[0] - walls1)
    (shares,) = by_owner(named, [flux])

    keep_l, keep_r = keeps(me)
    keep = jnp.where(lanes(8) >= FS // 2, keep_l, keep_r)
    halo, c_halo = metal_halo(turned, 8)
    own, halo = metal_step(solid[0:8, :], halo, cond[0:8, :], c_halo, keep)
    own, halo = set_walls(own, halo, wall1, me, keep)
    own, _ = metal_step(own, halo, cond[0:8, :], c_halo, keep)
    shares = SOLID_STEP * shares + jnp.where(subs(NB) == me, own[0:1], 0.0)
    side[0:8, :], side[8:16, :], side[16:24, :] = wall1, shares, h

    lane = lanes(FZ)

    def corners(at, beside, factor):
        out = jnp.zeros((FZ, FS), F32)
        for i, (old, new) in enumerate(((left, new_l), (right, new_r))):
            for k, (source, lane_of) in enumerate(
                ((old, at), (new, at), (old, factor), (new, beside))
            ):
                out = jnp.where(lane == 4 * i + k, turn(source, 4 * i + k - lane_of), out)
        return out

    blank = jnp.zeros((6, FS), F32)
    for i in range(3):
        send_rows(first_out, second_out, 8 * i, fluid1[:, FP - 3 + i, :], fluid1[:, 2 - i, :])
    send_rows(first_out, second_out, 24, corners(FP - 1, FP - 2, 97), corners(0, 1, 96))
    send_rows(first_out, second_out, 32, pick(recv[:, 4, :], shares), pick(recv[:, 5, :], shares))
    send_rows(
        first_out, second_out, 40,
        jnp.concatenate([flux[FP - 2 : FP], blank], axis=0),
        jnp.concatenate([flux[1:2], flux[0:1], blank], axis=0),
    )


def sums_kernel(
    fluid1, turned, side, sv, pv, film, solid, cond, owner, fluid2, mt, sums, metal
):
    me = lax.axis_index("blk")
    lane, sub = lanes(FP), subs(FP)
    named, f = owner[...], film[...]
    wall1 = side[0:8, :]
    none = jnp.zeros((FZ, FS), F32)
    advance(fluid1, fluid2, none, none, turned[:FP, :], 32, sv, pv, f, pick(named, wall1))
    x = fluid2[0]
    low, high = turn(x, 1, 0), turn(x, -1, 0)
    before = jnp.where(lane == 0, 0.0, turn(x, 1))
    after = jnp.where(lane == FS - 1, 0.0, turn(x, -1))
    moved = stencil(x, low, high, before, after, x, fluid2[1], sv[0], pv[0]) - WALL * f * x
    within = jnp.where((sub == 0) | (sub == FP - 1), 0.0, f)
    deep = jnp.where((sub < 2) | (sub >= FP - 2), 0.0, f)
    sums[0:8, :], sums[8:16, :], sums[16:24, :] = by_owner(
        named, [within * x, deep * moved, f * f]
    )
    whole = jnp.concatenate([gather_columns(fluid2, lane), jnp.zeros((FP, FS), F32)], axis=0)
    mt[...] = whole.T
    keep_l, keep_r = keeps(me)
    keep = jnp.where(lanes(SD) >= FS // 2, keep_l, keep_r)
    halo, c_halo = metal_halo(turned, SD)
    own, halo = metal_step(solid[...], halo, cond[...], c_halo, keep)
    own, halo = set_walls(own, halo, wall1, me, keep)
    own, halo = metal_step(own, halo, cond[...], c_halo, keep)
    metal[0:SD, :], metal[SD : 2 * SD, :], metal[2 * SD : 3 * SD, :] = own, halo, c_halo


def pack_kernel(
    recv, mt_old, mt, sums, metal, side, fluid1, fluid2, sv, pv, film, owner,
    first, second, first1, second1, out, edge,
):
    me = lax.axis_index("blk")
    lane, sub = lanes(FZ), subs(FZ)
    keep_l, keep_r = keeps(me)
    lo, hi = sorted_rows(first, second)
    lo1, hi1 = sorted_rows(first1, second1)
    left, right = block_of(recv, me, 24)
    pv_first, pv_last = pv[:, 0, :], pv[:, FP - 1, :]

    def outside(rows, rows1, inner, near_l, near_r):
        far, mid, near = rows1(0, 8), rows1(8, 16), rows1(16, 24)
        corner = rows1(24, 32)

        def at(k, to):
            return turn(corner, to - k)

        def lane_at(x, of, to):
            return turn(x, to - of)

        old_l, old_r = at(0, 0), at(4, FS - 1)
        side_l = at(1, 0) + at(2, 0) * lane_at(left, near_l, 0)
        side_r = at(5, FS - 1) + at(6, FS - 1) * lane_at(right, near_r, FS - 1)
        return far, mid, near, (old_l, old_r), (side_l, side_r), (at(3, 0), at(7, FS - 1))

    def finish(rows, rows1, inner, own_partial, own_pv, factor, near_lane, factor_lane, upward):
        far, mid, near, old, beside, beside2 = outside(rows, rows1, inner, near_lane, near_lane)
        sv2, sv1, pv2, pv1 = rows(8, 16), rows(16, 24), rows(24, 32), rows(32, 40)
        flux = rows1(40, 42)
        order = (mid, inner) if upward else (inner, mid)
        new1 = halo_row(near, *order, *beside, sv1, pv1, flux[1:2])
        order = (far, near) if upward else (near, far)
        new2 = halo_row(mid, *order, *beside2, sv2, pv2, flux[0:1])
        through_l = turn(left, -factor_lane) * old[0]
        through_r = turn(right, FS - 1 - factor_lane) * old[1]
        own = own_partial + factor * near
        sv_here = sv[:, 0 if upward else FP - 1, :]
        own = own + jnp.where(lane == 0, (SPREAD + ADVECT * sv_here) * through_l, 0.0)
        own = own + jnp.where(lane == FS - 1, SPREAD * through_r, 0.0)
        return new1, new2, own

    low1, low2, x_first = finish(
        lo, lo1, fluid1[:, 0, :], fluid2[:, 0, :], pv_first, up_factor(pv_first), 0, 96, True
    )
    high1, high2, x_last = finish(
        hi, hi1, fluid1[:, FP - 1, :], fluid2[:, FP - 1, :], pv_last, down_factor(pv_last),
        FP - 1, 97, False,
    )

    (r0, r1), (l0, l1) = column_blocks(mt)

    def patched(block, column):
        block = jnp.where(lane == 0, turn(x_first, -column), block)
        return jnp.where(lane == FP - 1, turn(x_last, FP - 1 - column), block)

    r0, r1 = patched(r0, FS - 1), patched(r1, FS - 2)
    l0, l1 = patched(l0, 0), patched(l1, 1)
    (sv_r, pv_r, film_r), (sv_l, pv_l, film_l) = flows(mt_old)

    def ends(column):
        return turn(low1, -column), turn(high1, FP - 1 - column)

    right_part = edge_part(r0, *ends(FS - 1), r1, 0.0, sv_r, pv_r, film_r)
    left_part = edge_part(l0, *ends(0), 0.0, l1, sv_l, pv_l, film_l)

    def corner_row(column):
        rows = []
        for i, x in enumerate((low1, high1)):
            spread = jnp.broadcast_to(x[:, column : column + 1], (FZ, FS))
            rows.append(
                jnp.sum(jnp.where(lane == sub + 8 * i, spread, 0.0), axis=0, keepdims=True)
            )
        return rows[0] + rows[1]

    rows = (0, 1, FP - 2, FP - 1)

    def stack(parts):
        return jnp.concatenate(list(parts) + [jnp.zeros((4, FS), F32)], axis=0)

    layer = {r: fluid2[0, r : r + 1, :] for r in (1, 2, FP - 3, FP - 2)}
    layer[-1], layer[0], layer[FP - 1], layer[FP] = (
        low1[0:1], x_first[0:1], x_last[0:1], high1[0:1],
    )
    here = stack(layer[r] for r in rows)
    above = stack([x_first[1:2], fluid2[1, 1:2, :], fluid2[1, FP - 2 : FP - 1, :], x_last[1:2]])
    f4 = stack(film[r : r + 1, :] for r in rows)
    sv4 = stack(sv[0, r : r + 1, :] for r in rows)
    pv4 = stack(pv[0, r : r + 1, :] for r in rows)
    before = jnp.where(lane == 0, 0.0, turn(here, 1))
    after = jnp.where(lane == FS - 1, 0.0, turn(here, -1))
    moved = f4 * (
        stencil(
            here, stack(layer[r - 1] for r in rows), stack(layer[r + 1] for r in rows),
            before, after, here, above, sv4, pv4,
        )
        - WALL * f4 * here
    )
    direct = f4 * here
    a2, b3, h2 = sums[0:8, :], sums[8:16, :], sums[16:24, :]
    for i, r in enumerate(rows):
        hit = owner[r : r + 1, :] == sub.astype(F32)
        b3 = b3 + jnp.where(hit, moved[i : i + 1], 0.0)
        if r in (0, FP - 1):
            a2 = a2 + jnp.where(hit, direct[i : i + 1], 0.0)
    (film_bl, own_bl), (film_br, own_br) = edge_rows(recv, me)
    _, part_r = block_of(recv, me, 32)
    inside = lane < FP

    def shared(own_row, term):
        hit = (jnp.broadcast_to(own_row, (NB, FS)) == sub.astype(F32)) & inside
        return jnp.sum(jnp.where(hit, term, 0.0), axis=1, keepdims=True)

    right_term = film_br * turn(part_r, 64)[0:1] * r0[0:1] * keep_r
    left_term = film_bl * SPREAD * l0[0:1] * keep_l
    b3 = b3 + jnp.where(lane == 0, shared(own_br, right_term), 0.0)
    b3 = b3 + jnp.where(lane == FS - 1, shared(own_bl, left_term), 0.0)

    right_corner, left_corner = corner_row(FS - 1), corner_row(0)
    to_right = jnp.where(inside, r0, turn(right_part, 64))
    to_left = jnp.where(inside, l0, turn(left_part, 64))
    relay_lo, relay_hi = lo1(32, 40), hi1(32, 40)
    blank = jnp.zeros((2, FS), F32)
    for peer in range(NB):
        ahead = (me + 1 == peer).astype(F32)
        behind = (me - 1 == peer).astype(F32)
        out[peer, 0:8, :] = jnp.concatenate(
            [
                metal[1:2, :],
                b3[peer : peer + 1],
                h2[peer : peer + 1],
                relay_lo[peer : peer + 1],
                relay_hi[peer : peer + 1],
                right_corner * ahead + left_corner * behind,
                blank,
            ],
            axis=0,
        )
        out[peer, 8:16, :] = side[8:16, :]
        out[peer, 16:24, :] = a2
        out[peer, 24:32, :] = to_right * ahead + to_left * behind
    kept = (
        low1, low2, high1, high2, r0, l0, x_first, x_last,
        lo(16, 24), lo(32, 40), hi(16, 24), hi(32, 40), lo(40, 48), hi(40, 48),
    )
    for i, value in enumerate(kept):
        edge[8 * i : 8 * i + 8, :] = value


def last_kernel(
    recv1, recv, edge, side, metal, fluid2, sv, pv, film, cond, owner, fluid_out, solid_out,
    tm, fluid3,
):
    me = lax.axis_index("blk")
    lane, sub = lanes(FZ), subs(FZ)
    (
        low1, low2, high1, high2, mine_right, mine_left, x_first, x_last,
        sv_lo, pv_lo, sv_hi, pv_hi, film_lo, film_hi,
    ) = [edge[8 * i : 8 * i + 8, :] for i in range(14)]
    left, right = block_of(recv1, me, 24)
    corner_l, corner_r = (block[5:6] for block in block_of(recv1, me, 0))
    part_l, part_r = block_of(recv, me, 32)
    c0, c1, h = recv[:, 2, :], recv[:, 3, :], side[16:24, :]
    tail, wall2, a2 = recv1[0, 0:8, :], recv1[0, 8:16, :], recv1[0, 16:24, :]
    for j in range(1, NB):
        tail = tail + recv1[j, 0:8, :]
        wall2 = wall2 + recv1[j, 8:16, :]
        a2 = a2 + recv1[j, 16:24, :]
    under2 = recv1[:, 0, :]
    wall3 = strip_row(wall2, conduct_of(c0, wall2), under2, conduct_of(c1, under2))
    wall3 = wall3 + SOLID_STEP * (a2 - h * wall2)
    inflow3 = tail[1:2] + WALL * tail[2:3] * row_of(wall2, me) - row_of(h * wall3, me)

    new_l, new_r = halo_columns(
        turn(left, 64), turn(right, 64), turn(part_l, 64), turn(part_r, 64),
        edge_rows(recv, me), mine_right, mine_left, wall2, me,
    )
    tm[...] = jnp.zeros((FS, FS), F32)
    tm[pl.ds(0, FZ, stride=2), :] = right
    tm[pl.ds(1, FZ, stride=2), :] = left
    tm[pl.ds(32, FZ, stride=2), :] = new_r
    tm[pl.ds(33, FZ, stride=2), :] = new_l
    columns = tm[...].T[:FP]

    def corner(row, which):
        spread = jnp.broadcast_to(row, (FZ, FS))
        return jnp.sum(jnp.where(lane == sub + 8 * which, spread, 0.0), axis=1, keepdims=True)

    new_low = halo_row(
        low1, low2, x_first, corner(corner_l, 0), corner(corner_r, 0), sv_lo, pv_lo,
        film_lo[0:1] * (low1[0:1] - tail[3:4]),
    )
    new_high = halo_row(
        high1, x_last, high2, corner(corner_l, 1), corner(corner_r, 1), sv_hi, pv_hi,
        film_hi[0:1] * (high1[0:1] - tail[4:5]),
    )
    named, f = owner[...], film[...]
    source = [
        set_row(set_row(fluid2[z], x_first[z : z + 1], 0), x_last[z : z + 1], 1)
        for z in range(FZ)
    ]
    advance(source, fluid3, low1, high1, columns, 0, sv, pv, f, pick(named, wall2))
    advance(fluid3, fluid_out, new_low, new_high, columns, 32, sv, pv, f, pick(named, wall3))

    keep_l, keep_r = keeps(me)
    keep = jnp.where(lanes(SD) >= FS // 2, keep_l, keep_r)
    own, halo, c_halo = metal[0:SD, :], metal[SD : 2 * SD, :], metal[2 * SD : 3 * SD, :]
    own, halo = set_walls(own, halo, wall2, me, keep)
    own, halo = metal_step(own, halo, cond[...], c_halo, keep)
    own, halo = set_walls(own, halo, wall3, me, keep)
    own, _ = metal_step(own, halo, cond[...], c_halo, keep)
    solid_out[...] = own + jnp.where(subs(SD) == 0, SOLID_STEP * inflow3, 0.0)


def shape(*dims):
    return jax.ShapeDtypeStruct(dims, F32)


VMEM = pl.BlockSpec(memory_space=pltpu.VMEM)
GRANT = 54 * 1024 * 1024
HBM = pl.BlockSpec(memory_space=pltpu.HBM)


def call(kernel, outs, args, name, scratch=(), far=0, limit=32 * 1024 * 1024):
    return pl.pallas_call(
        kernel,
        out_shape=outs,
        in_specs=[HBM] * far + [VMEM] * (len(args) - far),
        out_specs=jax.tree.map(lambda _: VMEM, outs),
        scratch_shapes=scratch,
        name=name,
        compiler_params=pltpu.CompilerParams(vmem_limit_bytes=limit),
    )(*args)


def both_ways(first, second):
    count = lax.axis_size("sec")
    near = [(i, i ^ 1) for i in range(count)]
    far = [(i, (i + 1 if i % 2 else i - 1) % count) for i in range(count)]
    second = lax.ppermute(second, "sec", far)
    return lax.ppermute(first, "sec", near), second


def swap(message):
    return lax.all_to_all(message, "blk", split_axis=0, concat_axis=0, tiled=True)


def two_exchanges(fluid, sv, pv, film, solid, cond, face_owner):
    owner = face_owner.reshape(1, FP)
    solid, cond = solid.reshape(SD, FS), cond.reshape(SD, FS)
    field, rows = shape(FZ, FP, FS), shape(ROWS, FS)
    held = [pltpu.VMEM((FZ, FP, FS), F32)] * 3
    held += [pltpu.VMEM((n, FS), F32) for n in (FP, SD, SD)]
    message, first, second, mt, owner = call(
        open_kernel,
        (shape(NB, R0, FS), rows, rows, shape(FS, FS), shape(FP, FS)),
        (fluid, sv, pv, film, solid, cond, owner),
        "open",
        held + [pltpu.VMEM((1, FP), jnp.int32), pltpu.SemaphoreType.DMA((10,))],
        far=7,
        limit=GRANT - OPEN_ROOM,
    )
    first, second = both_ways(first, second)
    recv = swap(message)
    fluid1, first1, second1, turned, side = call(
        first_kernel,
        (field, rows, rows, shape(FS, FS), shape(24, FS)),
        (recv, fluid, sv, pv, film, solid, cond, owner, first, second),
        "first",
        [pltpu.VMEM((FS, FS), F32)],
    )
    first1, second1 = both_ways(first1, second1)
    fluid2, mt2, sums, metal = call(
        sums_kernel,
        (field, shape(FS, FS), shape(24, FS), shape(3 * SD, FS)),
        (fluid1, turned, side, sv, pv, film, solid, cond, owner),
        "sums",
    )
    message, edge = call(
        pack_kernel,
        (shape(NB, R1, FS), shape(14 * 8, FS)),
        (
            recv, mt, mt2, sums, metal, side, fluid1, fluid2, sv, pv, film, owner,
            first, second, first1, second1,
        ),
        "pack",
    )
    recv1 = swap(message)
    fluid, solid = call(
        last_kernel,
        (field, shape(SD, FS)),
        (recv1, recv, edge, side, metal, fluid2, sv, pv, film, cond, owner),
        "last",
        [pltpu.VMEM((FS, FS), F32), pltpu.VMEM((FZ, FP, FS), F32)],
    )
    return fluid, solid.reshape(1, SD, FS)


def padded(block, sides, width, periodic):
    for axis, dim in sides:
        count = lax.axis_size(axis)
        forward = [(i, i + 1) for i in range(count - 1)]
        if periodic:
            forward.append((count - 1, 0))
        backward = [(target, source) for source, target in forward]
        low = lax.ppermute(
            lax.slice_in_dim(block, block.shape[dim] - width, None, axis=dim), axis, forward
        )
        high = lax.ppermute(lax.slice_in_dim(block, 0, width, axis=dim), axis, backward)
        block = jnp.concatenate([low, block, high], axis=dim)
    return block


def fluid_update(
    fluid, stream_velocity, pitch_velocity, wall_flux, pitch_extended, stream_extended
):
    pitch_prev = pitch_extended[:, :-2]
    pitch_next = pitch_extended[:, 2:]
    stream_prev = stream_extended[:, :, :-2]
    stream_next = stream_extended[:, :, 2:]
    span_prev = jnp.concatenate([fluid[:1], fluid[:-1]], 0)
    span_next = jnp.concatenate([fluid[1:], fluid[-1:]], 0)
    spread = SPREAD * (
        pitch_prev + pitch_next + stream_prev + stream_next + span_prev + span_next - 6.0 * fluid
    )
    carried = (
        -ADVECT * stream_velocity * (fluid - stream_prev)
        - ADVECT * jnp.maximum(pitch_velocity, 0.0) * (fluid - pitch_prev)
        + ADVECT * jnp.maximum(-pitch_velocity, 0.0) * (pitch_next - fluid)
    )
    updated = fluid + spread + carried
    return updated.at[0].add(-WALL * wall_flux)


def solid_update(solid, conduct, inflow, solid_extended, conduct_extended):
    stream_prev = solid_extended[..., :-2]
    stream_next = solid_extended[..., 2:]
    conduct_prev = conduct_extended[..., :-2]
    conduct_next = conduct_extended[..., 2:]
    depth_prev = jnp.concatenate([solid[:, :1], solid[:, :-1]], 1)
    depth_next = jnp.concatenate([solid[:, 1:], solid[:, -1:]], 1)
    kdepth_prev = jnp.concatenate([conduct[:, :1], conduct[:, :-1]], 1)
    kdepth_next = jnp.concatenate([conduct[:, 1:], conduct[:, -1:]], 1)
    flow = (
        0.5 * (conduct + conduct_prev) * (stream_prev - solid)
        + 0.5 * (conduct + conduct_next) * (stream_next - solid)
        + 0.5 * (conduct + kdepth_prev) * (depth_prev - solid)
        + 0.5 * (conduct + kdepth_next) * (depth_next - solid)
    )
    updated = solid + SOLID_STEP * flow
    updated = updated.at[:, 0].add(SOLID_STEP * inflow)
    updated = updated.at[:, -1].add(SOLID_STEP * COOLING * (COOLANT - solid[:, -1]))
    return updated


def local(
    fluid_temp, stream_velocity, pitch_velocity, film_coeff, solid_temp, conductivity, face_owner
):
    span_cells, pitch_cells, stream_cells = fluid_temp.shape
    depth_cells = solid_temp.shape[1]
    block_count = lax.axis_size("blk")
    capacity = max(2, (pitch_cells + block_count - 1) // block_count)
    owners = face_owner.reshape(-1)
    onehot = (owners[:, None] == jnp.arange(block_count, dtype=jnp.int32)[None, :]).astype(
        jnp.float32
    )
    same_owner = owners[:, None] == owners[None, :]
    earlier = lax.broadcasted_iota(jnp.int32, (pitch_cells, pitch_cells), 0) < lax.broadcasted_iota(
        jnp.int32, (pitch_cells, pitch_cells), 1
    )
    slot_rank = jnp.sum((same_owner & earlier).astype(jnp.int32), axis=0)
    slot_table = (slot_rank[None, :] == jnp.arange(capacity, dtype=jnp.int32)[:, None]).astype(
        jnp.float32
    )
    placing = onehot.T[:, None, :] * slot_table[None, :, :]
    fluid = fluid_temp
    solid = solid_temp
    gas_rows = span_cells * pitch_cells
    for subiter in range(SUB):
        wall_row = solid[0, 0:1, :]
        wall_temp = jnp.dot(
            onehot,
            lax.all_gather(wall_row, "blk", axis=0, tiled=True),
            precision=lax.Precision.HIGHEST,
            preferred_element_type=jnp.float32,
        )
        flux = film_coeff * (fluid[0] - wall_temp)
        outgoing = jnp.einsum("ocb,bf->ocf", placing, flux, precision=lax.Precision.HIGHEST)
        received = lax.all_to_all(outgoing, "blk", split_axis=0, concat_axis=0, tiled=True)
        inflow = jnp.sum(received, axis=(0, 1))
        conduct = conductivity * (1.0 + 0.25 * jnp.tanh(solid))
        stacked = jnp.concatenate([fluid.reshape(gas_rows, stream_cells), solid[0], conduct[0]], 0)
        stream_ext = padded(stacked, (("blk", 1),), 1, False)
        pitch_extended = padded(fluid, (("sec", 1),), 1, True)
        fluid_stream = stream_ext[:gas_rows].reshape(span_cells, pitch_cells, stream_cells + 2)
        solid_stream = stream_ext[gas_rows : gas_rows + depth_cells][None]
        conduct_stream = stream_ext[gas_rows + depth_cells :][None]
        fluid = fluid_update(
            fluid, stream_velocity, pitch_velocity, flux, pitch_extended, fluid_stream
        )
        solid = solid_update(solid, conduct, inflow[None, :], solid_stream, conduct_stream)
    return (fluid, solid)


def solution(mesh):
    placed = (
        P(None, "sec", "blk"),
        P(None, "sec", "blk"),
        P(None, "sec", "blk"),
        P("sec", "blk"),
        P("sec", None, "blk"),
        P("sec", None, "blk"),
        P("sec", "blk", None, None),
    )
    sizes = dict(mesh.shape)

    def chosen(*args):
        fits = args[0].shape == (FZ, FP, FS) and args[4].shape == (1, SD, FS)
        fits = fits and sizes["blk"] == NB and sizes["sec"] % 2 == 0
        return two_exchanges(*args) if fits else local(*args)

    return jax.shard_map(
        chosen,
        mesh=mesh,
        in_specs=placed,
        out_specs=(P(None, "sec", "blk"), P("sec", None, "blk")),
        check_vma=False,
    )
```

```python
import jax
import jax.numpy as jnp
from jax import lax
from jax.experimental import pallas as pl
from jax.experimental.pallas import tpu as pltpu
from jax.sharding import PartitionSpec as P

SUB = 4


ADVECT = 0.4
SPREAD = 0.04
WALL = 0.4
SOLID_STEP = 0.04
COOLING = 0.5
COOLANT = -1.0

F32 = jnp.float32
NB = 8
FZ = 8
FP = 64
FS = 128
SD = 32
R0 = 40
R1 = 32
ROWS = 48
OPEN_ROOM = 56 * 1024
PREPARE_ROOM = 1400 * 1024
ORDER = (5, 0, 1, 2, 6, 3, 4, 7)
PLACE = tuple(ORDER.index(peer) for peer in range(NB))


def lanes(rows):
    return lax.broadcasted_iota(jnp.int32, (rows, FS), 1)


def subs(rows):
    return lax.broadcasted_iota(jnp.int32, (rows, FS), 0)


def turn(x, shift, axis=1):
    return pltpu.roll(x, shift % x.shape[axis], axis)


def by_owner(owner, values):
    sub = subs(NB)
    outs = [jnp.zeros((NB, FS), F32) for _ in values]
    for o in range(NB):
        mine = owner == o
        for i, value in enumerate(values):
            total = jnp.sum(jnp.where(mine, value, 0.0), axis=0, keepdims=True)
            outs[i] = jnp.where(sub == o, total, outs[i])
    return outs


def pick(owner, table):
    out = jnp.zeros(owner.shape, F32)
    for o in range(NB):
        out = jnp.where(owner == o, table[o : o + 1], out)
    return out


def pick_lane(owner_row, table, lane):
    column = jnp.broadcast_to(table[:, lane : lane + 1], (NB, FS))
    named = jnp.broadcast_to(owner_row, (NB, FS)) == subs(NB).astype(F32)
    return jnp.sum(jnp.where(named, column, 0.0), axis=0, keepdims=True)


def stencil(x, low, high, left, right, below, above, sv, pv):
    spread = SPREAD * (low + high + left + right + below + above - 6.0 * x)
    carried = (
        -ADVECT * sv * (x - left)
        - ADVECT * jnp.maximum(pv, 0.0) * (x - low)
        + ADVECT * jnp.maximum(-pv, 0.0) * (high - x)
    )
    return x + spread + carried


def factored(x, low, high, left, right, below, above, toward, up, down):
    new = (1.0 - 3.0 * SPREAD) * x + SPREAD * (right + below + above)
    return new + toward * (left - x) + up * (low - x) + down * (high - x)


def span(x):
    sub = subs(FZ)
    below = jnp.where(sub == 0, x, turn(x, 1, 0))
    above = jnp.where(sub == FZ - 1, x, turn(x, FZ - 1, 0))
    return below, above


def halo_row(x, low, high, left_corner, right_corner, sv, pv, flux):
    lane = lanes(FZ)
    left = jnp.where(lane == 0, left_corner, turn(x, 1))
    right = jnp.where(lane == FS - 1, right_corner, turn(x, -1))
    below, above = span(x)
    new = stencil(x, low, high, left, right, below, above, sv, pv)
    return new - jnp.where(subs(FZ) == 0, WALL * flux, 0.0)


def edge_part(x, low_end, high_end, left, right, sv, pv, film):
    lane = lanes(FZ)
    low = jnp.where(lane == 0, low_end, turn(x, 1))
    high = jnp.where(lane == FP - 1, high_end, turn(x, -1))
    below, above = span(x)
    new = stencil(x, low, high, left, right, below, above, sv, pv)
    return new - jnp.where(subs(FZ) == 0, WALL * film * x, 0.0)


def set_row(x, row, at):
    if at == 0:
        return jnp.concatenate([jnp.where(subs(8) == 0, row, x[:8]), x[8:]], axis=0)
    return jnp.concatenate([x[:-8], jnp.where(subs(8) == 7, row, x[-8:])], axis=0)


def advance(src, dst, low_row, high_row, columns, base, factors, film, wall):
    lane = lanes(FP)
    toward, up, down = factors
    for z in range(FZ):
        x = src[z]
        low = set_row(turn(x, 1, 0), low_row[z : z + 1], 0)
        high = set_row(turn(x, -1, 0), high_row[z : z + 1], 1)
        edge = turn(columns, -(base + 2 * z + 1))
        left = jnp.where(lane == 0, edge, turn(x, 1))
        right = jnp.where(lane == FS - 1, edge, turn(x, -1))
        below, above = src[max(z - 1, 0)], src[min(z + 1, FZ - 1)]
        new = factored(x, low, high, left, right, below, above, toward[z], up[z], down[z])
        if z == 0:
            new = new - WALL * film * (x - wall)
        dst[z] = new


def prepare_kernel(fluid_in, sv_in, pv_in, film, toward, up, down, partial, fluid, sv, pv, sems):
    started = fetch([(fluid_in, fluid), (sv_in, sv), (pv_in, pv)], sems)
    for copy in started:
        copy.wait()
    for z in range(FZ):
        toward[z] = SPREAD + ADVECT * sv[z]
        up[z] = up_factor(pv[z])
        down[z] = down_factor(pv[z])
    none = jnp.zeros((FZ, FS), F32)
    columns = jnp.zeros((FP, FS), F32)
    advance(fluid, partial, none, none, columns, 0, (toward, up, down), film[...], 0.0)


def complete(partial, dst, low_row, high_row, columns, factors, film, wall):
    lane = lanes(FP)
    toward, up, down = factors
    for z in range(FZ):
        edge = turn(columns, -(2 * z + 1))
        gain = jnp.where(lane == 0, toward[z], jnp.where(lane == FS - 1, SPREAD, 0.0))
        new = partial[z] + gain * edge
        if z == 0:
            new = new + WALL * film * wall
        first = new[:8] + jnp.where(subs(8) == 0, up[z, :8, :] * low_row[z : z + 1], 0.0)
        last = new[-8:] + jnp.where(subs(8) == 7, down[z, FP - 8 :, :] * high_row[z : z + 1], 0.0)
        dst[z] = jnp.concatenate([first, new[8:-8], last], axis=0)


def strip_row(here, k_here, under, k_under):
    sub, lane = subs(NB), lanes(NB)

    def prev(x):
        moved = turn(x, 1)
        carried = jnp.where(sub == 0, 0.0, turn(moved, 1, 0))
        return jnp.where(lane == 0, carried, moved)

    def following(x):
        moved = turn(x, -1)
        carried = jnp.where(sub == NB - 1, 0.0, turn(moved, -1, 0))
        return jnp.where(lane == FS - 1, carried, moved)

    flow = (
        0.5 * (k_here + prev(k_here)) * (prev(here) - here)
        + 0.5 * (k_here + following(k_here)) * (following(here) - here)
        + 0.5 * (k_here + k_under) * (under - here)
    )
    return here + SOLID_STEP * flow


def conduct_of(conductivity, solid):
    return conductivity * (1.0 + 0.25 * jnp.tanh(solid))


def metal_step(own, halo, c_own, c_halo, keep):
    depth_cells = own.shape[0]
    k_own, k_halo = conduct_of(c_own, own), conduct_of(c_halo, halo)
    lane, sub = lanes(depth_cells), subs(depth_cells)

    def depth(x):
        up = jnp.where(sub == 0, x, turn(x, 1, 0))
        down = jnp.where(sub == depth_cells - 1, x, turn(x, -1, 0))
        return up, down

    def stream(x, other):
        prev = jnp.where(lane == 0, turn(other, 1), turn(x, 1))
        following = jnp.where(lane == FS - 1, turn(other, -1), turn(x, -1))
        return prev, following

    def update(x, k, other, k_other):
        flow = jnp.zeros_like(x)
        for a, ka in zip(stream(x, other) + depth(x), stream(k, k_other) + depth(k)):
            flow = flow + 0.5 * (k + ka) * (a - x)
        new = x + SOLID_STEP * flow
        return new + jnp.where(sub == SD - 1, SOLID_STEP * COOLING * (COOLANT - x), 0.0)

    return update(own, k_own, halo, k_halo), update(halo, k_halo, own, k_own) * keep


def row_of(table, index):
    return jnp.sum(jnp.where(subs(NB) == index, table, 0.0), axis=0, keepdims=True)


def set_walls(own, halo, walls, me, keep):
    sub, lane = subs(own.shape[0]), lanes(own.shape[0])
    beside = jnp.where(lane >= FS // 2, row_of(walls, me - 1), row_of(walls, me + 1)) * keep
    return jnp.where(sub == 0, row_of(walls, me), own), jnp.where(sub == 0, beside, halo)


def metal_halo(turned, rows):
    deep = turned[FP : FP + rows]
    lane = lanes(rows)

    def placed(left, right):
        return jnp.where(
            lane >= 124, turn(deep, left), jnp.where(lane < 4, turn(deep, right), 0.0)
        )

    return placed(108, 104), placed(104, 100)


def place_of(peer):
    return sum(jnp.where(peer == k, PLACE[k], 0) for k in range(NB))


def rows_of(recv, row):
    return jnp.concatenate([recv[PLACE[k], row : row + 1, :] for k in range(NB)], axis=0)


def keeps(me):
    return (me > 0).astype(F32), (me < NB - 1).astype(F32)


def block_of(recv, me, start):
    keep_l, keep_r = keeps(me)
    before = place_of(jnp.maximum(me - 1, 0))
    after = place_of(jnp.minimum(me + 1, NB - 1))
    part = slice(start, start + 8)
    return recv[before, part, :] * keep_l, recv[after, part, :] * keep_r


def column_blocks(mt):
    right = mt[pl.ds(1, FZ, stride=4), :], mt[pl.ds(0, FZ, stride=4), :]
    left = mt[pl.ds(2, FZ, stride=4), :], mt[pl.ds(3, FZ, stride=4), :]
    return right, left


def flows(mt):
    right, left = mt[pl.ds(32, FZ, stride=2), :], mt[pl.ds(33, FZ, stride=2), :]
    return (turn(right, 64), right, mt[48:49, :]), (turn(left, 64), left, mt[49:50, :])


def gather_columns(fluid, lane):
    acc = jnp.zeros((FP, FS), F32)
    for z in range(FZ):
        acc = jnp.where(lane // 4 == z, turn(fluid[z], 4 * z + 2), acc)
    return acc


def sorted_rows(first, second):
    even = lax.axis_index("sec") % 2 == 0
    return (
        lambda a, b: jnp.where(even, second[a:b, :], first[a:b, :]),
        lambda a, b: jnp.where(even, first[a:b, :], second[a:b, :]),
    )


def send_rows(first, second, start, up, down):
    even = lax.axis_index("sec") % 2 == 0
    part = slice(start, start + up.shape[0])
    first[part, :] = jnp.where(even, up, down)
    second[part, :] = jnp.where(even, down, up)


def up_factor(pv):
    return SPREAD + ADVECT * jnp.maximum(pv, 0.0)


def down_factor(pv):
    return SPREAD + ADVECT * jnp.maximum(-pv, 0.0)


def fetch(copies, sems):
    started = [
        pltpu.make_async_copy(src, dst, sems.at[i]) for i, (src, dst) in enumerate(copies)
    ]
    for copy in started:
        copy.start()
    return started


def open_kernel(
    fluid_in, sv_in, pv_in, film_in, solid_in, cond_in, owner,
    out, first, second, mt, names, fluid, sv, pv, film, solid, cond, ids, sems,
):
    me = lax.axis_index("blk")
    half = FZ // 2
    copies = [(owner, ids), (film_in, film), (solid_in, solid), (cond_in, cond)]
    for src, dst in ((fluid_in, fluid), (pv_in, pv), (sv_in, sv)):
        for part in range(2):
            copies.append((src.at[pl.ds(half * part, half)], dst.at[pl.ds(half * part, half)]))
    started = fetch(copies, sems)
    lane = lanes(FP)
    for copy in started[:4]:
        copy.wait()
    ids_row = jnp.concatenate([ids[...].astype(F32), jnp.zeros((1, FS - FP), F32)], axis=1)
    named = jnp.broadcast_to(ids_row, (FS, FS)).T[:FP]
    names[...] = named
    metal = jnp.zeros((SD, FS), F32)
    thin = lanes(SD)
    s, c = solid[...], cond[...]
    for k in range(4):
        metal = jnp.where(thin == 4 * k + 1, turn(s, 3 * k + 5), metal)
        metal = jnp.where(thin == 4 * k + 2, turn(s, 3 * k + 2), metal)
        metal = jnp.where(thin == 4 * k + 17, turn(c, 3 * k + 21), metal)
        metal = jnp.where(thin == 4 * k + 18, turn(c, 3 * k + 18), metal)
    started[4].wait()
    a0, h = by_owner(named, [film[...] * fluid[0], film[...]])
    started[5].wait()
    top = gather_columns(fluid, lane)
    send_rows(first, second, 0, fluid[:, FP - 1, :], fluid[:, 0, :])
    blank = jnp.zeros((7, FS), F32)
    send_rows(
        first, second, 40,
        jnp.concatenate([film[FP - 1 : FP, :], blank], axis=0),
        jnp.concatenate([film[0:1, :], blank], axis=0),
    )
    for copy in started[6:]:
        copy.wait()
    bottom = jnp.zeros((FP, FS), F32)
    pair = (lane - 32) // 2
    for z in range(FZ):
        here = (pair == z) & (lane >= 32)
        top = jnp.where(here, turn(pv[z], 33 + 2 * z), top)
        bottom = jnp.where(here, turn(sv[z], 33 + 2 * z), bottom)
    send_rows(first, second, 8, sv[:, FP - 2, :], sv[:, 1, :])
    send_rows(first, second, 16, sv[:, FP - 1, :], sv[:, 0, :])
    send_rows(first, second, 24, pv[:, FP - 2, :], pv[:, 1, :])
    send_rows(first, second, 32, pv[:, FP - 1, :], pv[:, 0, :])
    top = jnp.where(lane // 2 == 24, turn(film[...], 49), top)
    top = jnp.where(lane == 50, named, top)
    metal = jnp.where(thin < 32, metal, bottom[:SD])
    mt[...] = jnp.concatenate([top, metal, bottom[SD:]], axis=0).T

    (r0, r1), (l0, l1) = column_blocks(mt)
    (sv_r, pv_r, film_r), (sv_l, pv_l, film_l) = flows(mt)
    wide = lanes(FZ)
    right_part = edge_part(r0, 0.0, 0.0, r1, 0.0, sv_r, pv_r, film_r)
    left_part = edge_part(l0, 0.0, 0.0, 0.0, l1, sv_l, pv_l, film_l)
    right_part = jnp.where(wide < FP, right_part, SPREAD)
    left_part = jnp.where(wide < FP, left_part, turn(SPREAD + ADVECT * sv_l, 64))

    def with_factors(block, p):
        block = jnp.where(wide == 96, turn(up_factor(p), 96), block)
        return jnp.where(wide == 97, turn(down_factor(p), 97 - (FP - 1)), block)

    r0, l0 = with_factors(r0, pv_r), with_factors(l0, pv_l)
    owner_row = turn(mt[50:51, :], 64)
    inside = lanes(1) < FP
    right_row, left_row = (jnp.where(inside, f, owner_row) for f in (film_r, film_l))
    head = jnp.concatenate([s[0:2], c[0:2], named[FP - 1 : FP], named[0:1]], axis=0)
    for peer in range(NB):
        ahead = (me + 1 == peer).astype(F32)
        behind = (me - 1 == peer).astype(F32)
        special = right_row * ahead + left_row * behind
        out[PLACE[peer], 0:8, :] = jnp.concatenate([head, special, special], axis=0)
        out[PLACE[peer], 8:16, :] = a0
        out[PLACE[peer], 16:24, :] = h
        same = (me == peer).astype(F32)
        out[PLACE[peer], 24:32, :] = r0 * ahead + l0 * behind + r0 * same
        out[PLACE[peer], 32:40, :] = right_part * ahead + left_part * behind + l0 * same


def halo_columns(known_l, known_r, factor_l, factor_r, rows, mine_right, mine_left, walls, me):
    keep_l, keep_r = keeps(me)
    (film_l, own_l), (film_r, own_r) = rows
    top = subs(FZ) == 0
    wall_l, wall_r = pick_lane(own_l, walls, FS - 1), pick_lane(own_r, walls, 0)
    new_l = known_l + factor_l * mine_left + jnp.where(top, WALL * film_l * wall_l, 0.0)
    new_r = known_r + factor_r * mine_right + jnp.where(top, WALL * film_r * wall_r, 0.0)
    return new_l * keep_l, new_r * keep_r


def edge_rows(recv, me):
    return [(block[6:7], turn(block[6:7], 64)) for block in block_of(recv, me, 0)]


def first_kernel(
    recv, partial, toward, up, down, film, solid, cond, owner, first, second,
    fluid1, first_out, second_out, turned, side, tm,
):
    me = lax.axis_index("blk")
    lo, hi = sorted_rows(first, second)
    left, right = block_of(recv, me, 24)
    part_l, part_r = block_of(recv, me, 32)
    wall0, under0 = rows_of(recv, 0), rows_of(recv, 1)
    c0, c1 = rows_of(recv, 2), rows_of(recv, 3)
    a0, h = recv[0, 8:16, :], recv[0, 16:24, :]
    for j in range(1, NB):
        a0, h = a0 + recv[j, 8:16, :], h + recv[j, 16:24, :]
    wall1 = strip_row(wall0, conduct_of(c0, wall0), under0, conduct_of(c1, under0))
    wall1 = wall1 + SOLID_STEP * (a0 - h * wall0)

    mine_right, mine_left = recv[place_of(me), 24:32, :], recv[place_of(me), 32:40, :]
    new_l, new_r = halo_columns(
        part_l, part_r, turn(part_l, 64), turn(part_r, 64), edge_rows(recv, me),
        mine_right, mine_left, wall0, me,
    )
    tm[...] = jnp.zeros((FS, FS), F32)
    tm[pl.ds(0, FZ, stride=2), :] = right
    tm[pl.ds(1, FZ, stride=2), :] = left
    tm[16:24, :] = left
    tm[24:32, :] = right
    tm[pl.ds(32, FZ, stride=2), :] = new_r
    tm[pl.ds(33, FZ, stride=2), :] = new_l
    turned[...] = tm[...].T
    named = owner[...]
    walls0, walls1 = pick(named, wall0), pick(named, wall1)
    factors = (toward, up, down)
    columns = turned[:FP, :]
    complete(partial, fluid1, lo(0, 8), hi(0, 8), columns, factors, film[...], walls0)
    flux = film[...] * (fluid1[0] - walls1)
    (shares,) = by_owner(named, [flux])

    keep_l, keep_r = keeps(me)
    keep = jnp.where(lanes(8) >= FS // 2, keep_l, keep_r)
    halo, c_halo = metal_halo(turned, 8)
    own, halo = metal_step(solid[0:8, :], halo, cond[0:8, :], c_halo, keep)
    own, halo = set_walls(own, halo, wall1, me, keep)
    own, _ = metal_step(own, halo, cond[0:8, :], c_halo, keep)
    shares = SOLID_STEP * shares + jnp.where(subs(NB) == me, own[0:1], 0.0)
    side[0:8, :], side[8:16, :], side[16:24, :] = wall1, shares, h

    lane = lanes(FZ)

    def corners(at, beside, factor):
        out = jnp.zeros((FZ, FS), F32)
        for i, (old, new) in enumerate(((left, new_l), (right, new_r))):
            for k, (source, lane_of) in enumerate(
                ((old, at), (new, at), (old, factor), (new, beside))
            ):
                out = jnp.where(lane == 4 * i + k, turn(source, 4 * i + k - lane_of), out)
        return out

    blank = jnp.zeros((6, FS), F32)
    for i in range(3):
        send_rows(first_out, second_out, 8 * i, fluid1[:, FP - 3 + i, :], fluid1[:, 2 - i, :])
    send_rows(first_out, second_out, 24, corners(FP - 1, FP - 2, 97), corners(0, 1, 96))
    send_rows(first_out, second_out, 32, pick(rows_of(recv, 4), shares), pick(rows_of(recv, 5), shares))
    send_rows(
        first_out, second_out, 40,
        jnp.concatenate([flux[FP - 2 : FP], blank], axis=0),
        jnp.concatenate([flux[1:2], flux[0:1], blank], axis=0),
    )


def sums_kernel(
    fluid1, turned, side, toward, up, down, film, solid, cond, owner,
    fluid2, mt, sums, metal,
):
    me = lax.axis_index("blk")
    lane, sub = lanes(FP), subs(FP)
    named, f = owner[...], film[...]
    wall1 = side[0:8, :]
    none = jnp.zeros((FZ, FS), F32)
    factors = (toward, up, down)
    advance(fluid1, fluid2, none, none, turned[:FP, :], 32, factors, f, pick(named, wall1))
    x = fluid2[0]
    low, high = turn(x, 1, 0), turn(x, -1, 0)
    before = jnp.where(lane == 0, 0.0, turn(x, 1))
    after = jnp.where(lane == FS - 1, 0.0, turn(x, -1))
    moved = factored(
        x, low, high, before, after, x, fluid2[1], toward[0], up[0], down[0]
    ) - WALL * f * x
    within = jnp.where((sub == 0) | (sub == FP - 1), 0.0, f)
    deep = jnp.where((sub < 2) | (sub >= FP - 2), 0.0, f)
    sums[0:8, :], sums[8:16, :], sums[16:24, :] = by_owner(
        named, [within * x, deep * moved, f * f]
    )
    whole = jnp.concatenate([gather_columns(fluid2, lane), jnp.zeros((FP, FS), F32)], axis=0)
    mt[...] = whole.T
    keep_l, keep_r = keeps(me)
    keep = jnp.where(lanes(SD) >= FS // 2, keep_l, keep_r)
    halo, c_halo = metal_halo(turned, SD)
    own, halo = metal_step(solid[...], halo, cond[...], c_halo, keep)
    own, halo = set_walls(own, halo, wall1, me, keep)
    own, halo = metal_step(own, halo, cond[...], c_halo, keep)
    metal[0:SD, :], metal[SD : 2 * SD, :], metal[2 * SD : 3 * SD, :] = own, halo, c_halo


def pack_kernel(
    recv, mt_old, mt, sums, metal, side, fluid1, fluid2, toward, up, down, film, owner,
    first, second, first1, second1, sent, out, edge,
):
    me = lax.axis_index("blk")
    lane, sub = lanes(FZ), subs(FZ)
    keep_l, keep_r = keeps(me)
    lo, hi = sorted_rows(first, second)
    lo1, hi1 = sorted_rows(first1, second1)
    left, right = block_of(recv, me, 24)

    def outside(rows, rows1, inner, near_l, near_r):
        far, mid, near = rows1(0, 8), rows1(8, 16), rows1(16, 24)
        corner = rows1(24, 32)

        def at(k, to):
            return turn(corner, to - k)

        def lane_at(x, of, to):
            return turn(x, to - of)

        old_l, old_r = at(0, 0), at(4, FS - 1)
        side_l = at(1, 0) + at(2, 0) * lane_at(left, near_l, 0)
        side_r = at(5, FS - 1) + at(6, FS - 1) * lane_at(right, near_r, FS - 1)
        return far, mid, near, (old_l, old_r), (side_l, side_r), (at(3, 0), at(7, FS - 1))

    def finish(rows, rows1, inner, own_partial, factor, near_lane, factor_lane, upward):
        far, mid, near, old, beside, beside2 = outside(rows, rows1, inner, near_lane, near_lane)
        sv2, sv1, pv2, pv1 = rows(8, 16), rows(16, 24), rows(24, 32), rows(32, 40)
        flux = rows1(40, 42)
        order = (mid, inner) if upward else (inner, mid)
        new1 = halo_row(near, *order, *beside, sv1, pv1, flux[1:2])
        order = (far, near) if upward else (near, far)
        new2 = halo_row(mid, *order, *beside2, sv2, pv2, flux[0:1])
        through_l = turn(left, -factor_lane) * old[0]
        through_r = turn(right, FS - 1 - factor_lane) * old[1]
        own = own_partial + factor * near
        toward_here = toward[:, 0 if upward else FP - 1, :]
        own = own + jnp.where(lane == 0, toward_here * through_l, 0.0)
        own = own + jnp.where(lane == FS - 1, SPREAD * through_r, 0.0)
        return new1, new2, own

    low1, low2, x_first = finish(
        lo, lo1, fluid1[:, 0, :], fluid2[:, 0, :], up[:, 0, :], 0, 96, True
    )
    high1, high2, x_last = finish(
        hi, hi1, fluid1[:, FP - 1, :], fluid2[:, FP - 1, :], down[:, FP - 1, :],
        FP - 1, 97, False,
    )

    (r0, r1), (l0, l1) = column_blocks(mt)

    def patched(block, column):
        block = jnp.where(lane == 0, turn(x_first, -column), block)
        return jnp.where(lane == FP - 1, turn(x_last, FP - 1 - column), block)

    r0, r1 = patched(r0, FS - 1), patched(r1, FS - 2)
    l0, l1 = patched(l0, 0), patched(l1, 1)
    (sv_r, pv_r, film_r), (sv_l, pv_l, film_l) = flows(mt_old)

    def ends(column):
        return turn(low1, -column), turn(high1, FP - 1 - column)

    right_part = edge_part(r0, *ends(FS - 1), r1, 0.0, sv_r, pv_r, film_r)
    left_part = edge_part(l0, *ends(0), 0.0, l1, sv_l, pv_l, film_l)

    def corner_row(column):
        rows = []
        for i, x in enumerate((low1, high1)):
            spread = jnp.broadcast_to(x[:, column : column + 1], (FZ, FS))
            rows.append(
                jnp.sum(jnp.where(lane == sub + 8 * i, spread, 0.0), axis=0, keepdims=True)
            )
        return rows[0] + rows[1]

    rows = (0, 1, FP - 2, FP - 1)

    def stack(parts):
        return jnp.concatenate(list(parts) + [jnp.zeros((4, FS), F32)], axis=0)

    layer = {r: fluid2[0, r : r + 1, :] for r in (1, 2, FP - 3, FP - 2)}
    layer[-1], layer[0], layer[FP - 1], layer[FP] = (
        low1[0:1], x_first[0:1], x_last[0:1], high1[0:1],
    )
    here = stack(layer[r] for r in rows)
    above = stack([x_first[1:2], fluid2[1, 1:2, :], fluid2[1, FP - 2 : FP - 1, :], x_last[1:2]])
    f4 = stack(film[r : r + 1, :] for r in rows)
    factors = [stack(part[0, r : r + 1, :] for r in rows) for part in (toward, up, down)]
    before = jnp.where(lane == 0, 0.0, turn(here, 1))
    after = jnp.where(lane == FS - 1, 0.0, turn(here, -1))
    moved = f4 * (
        factored(
            here, stack(layer[r - 1] for r in rows), stack(layer[r + 1] for r in rows),
            before, after, here, above, *factors,
        )
        - WALL * f4 * here
    )
    direct = f4 * here
    a2, b3, h2 = sums[0:8, :], sums[8:16, :], sums[16:24, :]
    for i, r in enumerate(rows):
        hit = owner[r : r + 1, :] == sub.astype(F32)
        b3 = b3 + jnp.where(hit, moved[i : i + 1], 0.0)
        if r in (0, FP - 1):
            a2 = a2 + jnp.where(hit, direct[i : i + 1], 0.0)
    (film_bl, own_bl), (film_br, own_br) = edge_rows(recv, me)
    _, part_r = block_of(recv, me, 32)
    inside = lane < FP

    def shared(own_row, term):
        hit = (jnp.broadcast_to(own_row, (NB, FS)) == sub.astype(F32)) & inside
        return jnp.sum(jnp.where(hit, term, 0.0), axis=1, keepdims=True)

    right_term = film_br * turn(part_r, 64)[0:1] * r0[0:1] * keep_r
    left_term = film_bl * SPREAD * l0[0:1] * keep_l
    b3 = b3 + jnp.where(lane == 0, shared(own_br, right_term), 0.0)
    b3 = b3 + jnp.where(lane == FS - 1, shared(own_bl, left_term), 0.0)

    right_corner, left_corner = corner_row(FS - 1), corner_row(0)
    to_right = jnp.where(inside, r0, turn(right_part, 64))
    to_left = jnp.where(inside, l0, turn(left_part, 64))
    relay_lo, relay_hi = lo1(32, 40), hi1(32, 40)
    blank = jnp.zeros((2, FS), F32)
    for peer in range(NB):
        ahead = (me + 1 == peer).astype(F32)
        behind = (me - 1 == peer).astype(F32)
        out[PLACE[peer], 0:8, :] = jnp.concatenate(
            [
                metal[1:2, :],
                b3[peer : peer + 1],
                h2[peer : peer + 1],
                relay_lo[peer : peer + 1],
                relay_hi[peer : peer + 1],
                right_corner * ahead + left_corner * behind,
                blank,
            ],
            axis=0,
        )
        out[PLACE[peer], 8:16, :] = side[8:16, :]
        out[PLACE[peer], 16:24, :] = a2
        out[PLACE[peer], 24:32, :] = to_right * ahead + to_left * behind
    kept = (
        low1, low2, high1, high2, r0, l0, x_first, x_last,
        lo(16, 24), lo(32, 40), hi(16, 24), hi(32, 40), lo(40, 48), hi(40, 48),
    )
    for i, value in enumerate(kept):
        edge[8 * i : 8 * i + 8, :] = value


def last_kernel(
    recv1, recv, edge, side, metal, fluid2, toward, up, down, film, cond, owner,
    fluid_out, solid_out,
    tm, fluid3,
):
    me = lax.axis_index("blk")
    lane, sub = lanes(FZ), subs(FZ)
    (
        low1, low2, high1, high2, mine_right, mine_left, x_first, x_last,
        sv_lo, pv_lo, sv_hi, pv_hi, film_lo, film_hi,
    ) = [edge[8 * i : 8 * i + 8, :] for i in range(14)]
    left, right = block_of(recv1, me, 24)
    corner_l, corner_r = (block[5:6] for block in block_of(recv1, me, 0))
    part_l, part_r = block_of(recv, me, 32)
    c0, c1, h = rows_of(recv, 2), rows_of(recv, 3), side[16:24, :]
    tail, wall2, a2 = recv1[0, 0:8, :], recv1[0, 8:16, :], recv1[0, 16:24, :]
    for j in range(1, NB):
        tail = tail + recv1[j, 0:8, :]
        wall2 = wall2 + recv1[j, 8:16, :]
        a2 = a2 + recv1[j, 16:24, :]
    under2 = rows_of(recv1, 0)
    wall3 = strip_row(wall2, conduct_of(c0, wall2), under2, conduct_of(c1, under2))
    wall3 = wall3 + SOLID_STEP * (a2 - h * wall2)
    inflow3 = tail[1:2] + WALL * tail[2:3] * row_of(wall2, me) - row_of(h * wall3, me)

    new_l, new_r = halo_columns(
        turn(left, 64), turn(right, 64), turn(part_l, 64), turn(part_r, 64),
        edge_rows(recv, me), mine_right, mine_left, wall2, me,
    )
    tm[...] = jnp.zeros((FS, FS), F32)
    tm[pl.ds(0, FZ, stride=2), :] = right
    tm[pl.ds(1, FZ, stride=2), :] = left
    tm[pl.ds(32, FZ, stride=2), :] = new_r
    tm[pl.ds(33, FZ, stride=2), :] = new_l
    columns = tm[...].T[:FP]

    def corner(row, which):
        spread = jnp.broadcast_to(row, (FZ, FS))
        return jnp.sum(jnp.where(lane == sub + 8 * which, spread, 0.0), axis=1, keepdims=True)

    new_low = halo_row(
        low1, low2, x_first, corner(corner_l, 0), corner(corner_r, 0), sv_lo, pv_lo,
        film_lo[0:1] * (low1[0:1] - tail[3:4]),
    )
    new_high = halo_row(
        high1, x_last, high2, corner(corner_l, 1), corner(corner_r, 1), sv_hi, pv_hi,
        film_hi[0:1] * (high1[0:1] - tail[4:5]),
    )
    named, f = owner[...], film[...]
    source = [
        set_row(set_row(fluid2[z], x_first[z : z + 1], 0), x_last[z : z + 1], 1)
        for z in range(FZ)
    ]
    factors = (toward, up, down)
    advance(source, fluid3, low1, high1, columns, 0, factors, f, pick(named, wall2))
    walls3 = pick(named, wall3)
    advance(fluid3, fluid_out, new_low, new_high, columns, 32, factors, f, walls3)

    keep_l, keep_r = keeps(me)
    keep = jnp.where(lanes(SD) >= FS // 2, keep_l, keep_r)
    own, halo, c_halo = metal[0:SD, :], metal[SD : 2 * SD, :], metal[2 * SD : 3 * SD, :]
    own, halo = set_walls(own, halo, wall2, me, keep)
    own, halo = metal_step(own, halo, cond[...], c_halo, keep)
    own, halo = set_walls(own, halo, wall3, me, keep)
    own, _ = metal_step(own, halo, cond[...], c_halo, keep)
    solid_out[...] = own + jnp.where(subs(SD) == 0, SOLID_STEP * inflow3, 0.0)


def shape(*dims):
    return jax.ShapeDtypeStruct(dims, F32)


VMEM = pl.BlockSpec(memory_space=pltpu.VMEM)
GRANT = 54 * 1024 * 1024
HBM = pl.BlockSpec(memory_space=pltpu.HBM)


def call(kernel, outs, args, name, scratch=(), far=0, limit=32 * 1024 * 1024):
    return pl.pallas_call(
        kernel,
        out_shape=outs,
        in_specs=[HBM] * far + [VMEM] * (len(args) - far),
        out_specs=jax.tree.map(lambda _: VMEM, outs),
        scratch_shapes=scratch,
        name=name,
        compiler_params=pltpu.CompilerParams(vmem_limit_bytes=limit),
    )(*args)


def both_ways(first, second):
    count = lax.axis_size("sec")
    near = [(i, i ^ 1) for i in range(count)]
    far = [(i, (i + 1 if i % 2 else i - 1) % count) for i in range(count)]
    second = lax.ppermute(second, "sec", far)
    return lax.ppermute(first, "sec", near), second


def swap(message):
    return lax.all_to_all(
        message, "blk", split_axis=0, concat_axis=0, tiled=True, axis_index_groups=[list(ORDER)]
    )


def two_exchanges(fluid, sv, pv, film, solid, cond, face_owner):
    owner = face_owner.reshape(1, FP)
    solid, cond = solid.reshape(SD, FS), cond.reshape(SD, FS)
    field, rows = shape(FZ, FP, FS), shape(ROWS, FS)
    held = [pltpu.VMEM((FZ, FP, FS), F32)] * 3
    held += [pltpu.VMEM((n, FS), F32) for n in (FP, SD, SD)]
    message, first, second, mt, owner = call(
        open_kernel,
        (shape(NB, R0, FS), rows, rows, shape(FS, FS), shape(FP, FS)),
        (fluid, sv, pv, film, solid, cond, owner),
        "open",
        held + [pltpu.VMEM((1, FP), jnp.int32), pltpu.SemaphoreType.DMA((10,))],
        far=7,
        limit=GRANT - OPEN_ROOM,
    )
    first, second = both_ways(first, second)
    recv = swap(message)
    *factors, partial = call(
        prepare_kernel,
        (field,) * 4,
        (fluid, sv, pv, film),
        "prepare",
        [pltpu.VMEM((FZ, FP, FS), F32)] * 3 + [pltpu.SemaphoreType.DMA((3,))],
        far=3,
        limit=GRANT - PREPARE_ROOM,
    )
    fluid1, first_sent, second_sent, turned, side = call(
        first_kernel,
        (field, rows, rows, shape(FS, FS), shape(24, FS)),
        (recv, partial, *factors, film, solid, cond, owner, first, second),
        "first",
        [pltpu.VMEM((FS, FS), F32)],
    )
    first1, second1 = both_ways(first_sent, second_sent)
    fluid2, mt2, sums, metal = call(
        sums_kernel,
        (field, shape(FS, FS), shape(24, FS), shape(3 * SD, FS)),
        (fluid1, turned, side, *factors, film, solid, cond, owner),
        "sums",
    )
    message, edge = call(
        pack_kernel,
        (shape(NB, R1, FS), shape(14 * 8, FS)),
        (
            recv, mt, mt2, sums, metal, side, fluid1, fluid2, *factors, film, owner,
            first, second, first1, second1, first_sent,
        ),
        "pack",
    )
    recv1 = swap(message)
    fluid, solid = call(
        last_kernel,
        (field, shape(SD, FS)),
        (recv1, recv, edge, side, metal, fluid2, *factors, film, cond, owner),
        "last",
        [pltpu.VMEM((FS, FS), F32), pltpu.VMEM((FZ, FP, FS), F32)],
    )
    return fluid, solid.reshape(1, SD, FS)


def padded(block, sides, width, periodic):
    for axis, dim in sides:
        count = lax.axis_size(axis)
        forward = [(i, i + 1) for i in range(count - 1)]
        if periodic:
            forward.append((count - 1, 0))
        backward = [(target, source) for source, target in forward]
        low = lax.ppermute(
            lax.slice_in_dim(block, block.shape[dim] - width, None, axis=dim), axis, forward
        )
        high = lax.ppermute(lax.slice_in_dim(block, 0, width, axis=dim), axis, backward)
        block = jnp.concatenate([low, block, high], axis=dim)
    return block


def fluid_update(
    fluid, stream_velocity, pitch_velocity, wall_flux, pitch_extended, stream_extended
):
    pitch_prev = pitch_extended[:, :-2]
    pitch_next = pitch_extended[:, 2:]
    stream_prev = stream_extended[:, :, :-2]
    stream_next = stream_extended[:, :, 2:]
    span_prev = jnp.concatenate([fluid[:1], fluid[:-1]], 0)
    span_next = jnp.concatenate([fluid[1:], fluid[-1:]], 0)
    spread = SPREAD * (
        pitch_prev + pitch_next + stream_prev + stream_next + span_prev + span_next - 6.0 * fluid
    )
    carried = (
        -ADVECT * stream_velocity * (fluid - stream_prev)
        - ADVECT * jnp.maximum(pitch_velocity, 0.0) * (fluid - pitch_prev)
        + ADVECT * jnp.maximum(-pitch_velocity, 0.0) * (pitch_next - fluid)
    )
    updated = fluid + spread + carried
    return updated.at[0].add(-WALL * wall_flux)


def solid_update(solid, conduct, inflow, solid_extended, conduct_extended):
    stream_prev = solid_extended[..., :-2]
    stream_next = solid_extended[..., 2:]
    conduct_prev = conduct_extended[..., :-2]
    conduct_next = conduct_extended[..., 2:]
    depth_prev = jnp.concatenate([solid[:, :1], solid[:, :-1]], 1)
    depth_next = jnp.concatenate([solid[:, 1:], solid[:, -1:]], 1)
    kdepth_prev = jnp.concatenate([conduct[:, :1], conduct[:, :-1]], 1)
    kdepth_next = jnp.concatenate([conduct[:, 1:], conduct[:, -1:]], 1)
    flow = (
        0.5 * (conduct + conduct_prev) * (stream_prev - solid)
        + 0.5 * (conduct + conduct_next) * (stream_next - solid)
        + 0.5 * (conduct + kdepth_prev) * (depth_prev - solid)
        + 0.5 * (conduct + kdepth_next) * (depth_next - solid)
    )
    updated = solid + SOLID_STEP * flow
    updated = updated.at[:, 0].add(SOLID_STEP * inflow)
    updated = updated.at[:, -1].add(SOLID_STEP * COOLING * (COOLANT - solid[:, -1]))
    return updated


def local(
    fluid_temp, stream_velocity, pitch_velocity, film_coeff, solid_temp, conductivity, face_owner
):
    span_cells, pitch_cells, stream_cells = fluid_temp.shape
    depth_cells = solid_temp.shape[1]
    block_count = lax.axis_size("blk")
    capacity = max(2, (pitch_cells + block_count - 1) // block_count)
    owners = face_owner.reshape(-1)
    onehot = (owners[:, None] == jnp.arange(block_count, dtype=jnp.int32)[None, :]).astype(
        jnp.float32
    )
    same_owner = owners[:, None] == owners[None, :]
    earlier = lax.broadcasted_iota(jnp.int32, (pitch_cells, pitch_cells), 0) < lax.broadcasted_iota(
        jnp.int32, (pitch_cells, pitch_cells), 1
    )
    slot_rank = jnp.sum((same_owner & earlier).astype(jnp.int32), axis=0)
    slot_table = (slot_rank[None, :] == jnp.arange(capacity, dtype=jnp.int32)[:, None]).astype(
        jnp.float32
    )
    placing = onehot.T[:, None, :] * slot_table[None, :, :]
    fluid = fluid_temp
    solid = solid_temp
    gas_rows = span_cells * pitch_cells
    for subiter in range(SUB):
        wall_row = solid[0, 0:1, :]
        wall_temp = jnp.dot(
            onehot,
            lax.all_gather(wall_row, "blk", axis=0, tiled=True),
            precision=lax.Precision.HIGHEST,
            preferred_element_type=jnp.float32,
        )
        flux = film_coeff * (fluid[0] - wall_temp)
        outgoing = jnp.einsum("ocb,bf->ocf", placing, flux, precision=lax.Precision.HIGHEST)
        received = lax.all_to_all(outgoing, "blk", split_axis=0, concat_axis=0, tiled=True)
        inflow = jnp.sum(received, axis=(0, 1))
        conduct = conductivity * (1.0 + 0.25 * jnp.tanh(solid))
        stacked = jnp.concatenate([fluid.reshape(gas_rows, stream_cells), solid[0], conduct[0]], 0)
        stream_ext = padded(stacked, (("blk", 1),), 1, False)
        pitch_extended = padded(fluid, (("sec", 1),), 1, True)
        fluid_stream = stream_ext[:gas_rows].reshape(span_cells, pitch_cells, stream_cells + 2)
        solid_stream = stream_ext[gas_rows : gas_rows + depth_cells][None]
        conduct_stream = stream_ext[gas_rows + depth_cells :][None]
        fluid = fluid_update(
            fluid, stream_velocity, pitch_velocity, flux, pitch_extended, fluid_stream
        )
        solid = solid_update(solid, conduct, inflow[None, :], solid_stream, conduct_stream)
    return (fluid, solid)


def solution(mesh):
    placed = (
        P(None, "sec", "blk"),
        P(None, "sec", "blk"),
        P(None, "sec", "blk"),
        P("sec", "blk"),
        P("sec", None, "blk"),
        P("sec", None, "blk"),
        P("sec", "blk", None, None),
    )
    sizes = dict(mesh.shape)

    def chosen(*args):
        fits = args[0].shape == (FZ, FP, FS) and args[4].shape == (1, SD, FS)
        fits = fits and sizes["blk"] == NB and sizes["sec"] % 2 == 0
        return two_exchanges(*args) if fits else local(*args)

    return jax.shard_map(
        chosen,
        mesh=mesh,
        in_specs=placed,
        out_specs=(P(None, "sec", "blk"), P("sec", None, "blk")),
        check_vma=False,
    )
```

```python
import jax
import jax.numpy as jnp
from jax import lax
from jax.experimental import pallas as pl
from jax.experimental.pallas import tpu as pltpu
from jax.sharding import PartitionSpec as P

SUB = 4


ADVECT = 0.4
SPREAD = 0.04
WALL = 0.4
SOLID_STEP = 0.04
COOLING = 0.5
COOLANT = -1.0

F32 = jnp.float32
NB = 8
FZ = 8
FP = 64
FS = 128
SD = 32
R0 = 40
R1 = 32
ROWS = 48
OPEN_ROOM = 56 * 1024
PREPARE_ROOM = 1400 * 1024
ORDER0 = (5, 0, 1, 2, 6, 3, 4, 7)
ORDER1 = (5, 2, 6, 4, 1, 0, 7, 3)


def lanes(rows):
    return lax.broadcasted_iota(jnp.int32, (rows, FS), 1)


def subs(rows):
    return lax.broadcasted_iota(jnp.int32, (rows, FS), 0)


def turn(x, shift, axis=1):
    return pltpu.roll(x, shift % x.shape[axis], axis)


def by_owner(owner, values):
    sub = subs(NB)
    outs = [jnp.zeros((NB, FS), F32) for _ in values]
    for o in range(NB):
        mine = owner == o
        for i, value in enumerate(values):
            total = jnp.sum(jnp.where(mine, value, 0.0), axis=0, keepdims=True)
            outs[i] = jnp.where(sub == o, total, outs[i])
    return outs


def pick(owner, table):
    out = jnp.zeros(owner.shape, F32)
    for o in range(NB):
        out = jnp.where(owner == o, table[o : o + 1], out)
    return out


def pick_lane(owner_row, table, lane):
    column = jnp.broadcast_to(table[:, lane : lane + 1], (NB, FS))
    named = jnp.broadcast_to(owner_row, (NB, FS)) == subs(NB).astype(F32)
    return jnp.sum(jnp.where(named, column, 0.0), axis=0, keepdims=True)


def stencil(x, low, high, left, right, below, above, sv, pv):
    spread = SPREAD * (low + high + left + right + below + above - 6.0 * x)
    carried = (
        -ADVECT * sv * (x - left)
        - ADVECT * jnp.maximum(pv, 0.0) * (x - low)
        + ADVECT * jnp.maximum(-pv, 0.0) * (high - x)
    )
    return x + spread + carried


def factored(x, low, high, left, right, below, above, toward, up, down):
    new = (1.0 - 3.0 * SPREAD) * x + SPREAD * (right + below + above)
    return new + toward * (left - x) + up * (low - x) + down * (high - x)


def span(x):
    sub = subs(FZ)
    below = jnp.where(sub == 0, x, turn(x, 1, 0))
    above = jnp.where(sub == FZ - 1, x, turn(x, FZ - 1, 0))
    return below, above


def halo_row(x, low, high, left_corner, right_corner, sv, pv, flux):
    lane = lanes(FZ)
    left = jnp.where(lane == 0, left_corner, turn(x, 1))
    right = jnp.where(lane == FS - 1, right_corner, turn(x, -1))
    below, above = span(x)
    new = stencil(x, low, high, left, right, below, above, sv, pv)
    return new - jnp.where(subs(FZ) == 0, WALL * flux, 0.0)


def edge_part(x, low_end, high_end, left, right, sv, pv, film):
    lane = lanes(FZ)
    low = jnp.where(lane == 0, low_end, turn(x, 1))
    high = jnp.where(lane == FP - 1, high_end, turn(x, -1))
    below, above = span(x)
    new = stencil(x, low, high, left, right, below, above, sv, pv)
    return new - jnp.where(subs(FZ) == 0, WALL * film * x, 0.0)


def set_row(x, row, at):
    if at == 0:
        return jnp.concatenate([jnp.where(subs(8) == 0, row, x[:8]), x[8:]], axis=0)
    return jnp.concatenate([x[:-8], jnp.where(subs(8) == 7, row, x[-8:])], axis=0)


def advance(src, dst, low_row, high_row, columns, base, factors, film, wall):
    lane = lanes(FP)
    toward, up, down = factors
    for z in range(FZ):
        x = src[z]
        low = set_row(turn(x, 1, 0), low_row[z : z + 1], 0)
        high = set_row(turn(x, -1, 0), high_row[z : z + 1], 1)
        edge = turn(columns, -(base + 2 * z + 1))
        left = jnp.where(lane == 0, edge, turn(x, 1))
        right = jnp.where(lane == FS - 1, edge, turn(x, -1))
        below, above = src[max(z - 1, 0)], src[min(z + 1, FZ - 1)]
        new = factored(x, low, high, left, right, below, above, toward[z], up[z], down[z])
        if z == 0:
            new = new - WALL * film * (x - wall)
        dst[z] = new


def prepare_kernel(fluid_in, sv_in, pv_in, film, toward, up, down, partial, fluid, sv, pv, sems):
    started = fetch([(fluid_in, fluid), (sv_in, sv), (pv_in, pv)], sems)
    for copy in started:
        copy.wait()
    for z in range(FZ):
        toward[z] = SPREAD + ADVECT * sv[z]
        up[z] = up_factor(pv[z])
        down[z] = down_factor(pv[z])
    none = jnp.zeros((FZ, FS), F32)
    columns = jnp.zeros((FP, FS), F32)
    advance(fluid, partial, none, none, columns, 0, (toward, up, down), film[...], 0.0)


def complete(partial, dst, low_row, high_row, columns, factors, film, wall):
    lane = lanes(FP)
    toward, up, down = factors
    for z in range(FZ):
        edge = turn(columns, -(2 * z + 1))
        gain = jnp.where(lane == 0, toward[z], jnp.where(lane == FS - 1, SPREAD, 0.0))
        new = partial[z] + gain * edge
        if z == 0:
            new = new + WALL * film * wall
        first = new[:8] + jnp.where(subs(8) == 0, up[z, :8, :] * low_row[z : z + 1], 0.0)
        last = new[-8:] + jnp.where(subs(8) == 7, down[z, FP - 8 :, :] * high_row[z : z + 1], 0.0)
        dst[z] = jnp.concatenate([first, new[8:-8], last], axis=0)


def strip_row(here, k_here, under, k_under):
    sub, lane = subs(NB), lanes(NB)

    def prev(x):
        moved = turn(x, 1)
        carried = jnp.where(sub == 0, 0.0, turn(moved, 1, 0))
        return jnp.where(lane == 0, carried, moved)

    def following(x):
        moved = turn(x, -1)
        carried = jnp.where(sub == NB - 1, 0.0, turn(moved, -1, 0))
        return jnp.where(lane == FS - 1, carried, moved)

    flow = (
        0.5 * (k_here + prev(k_here)) * (prev(here) - here)
        + 0.5 * (k_here + following(k_here)) * (following(here) - here)
        + 0.5 * (k_here + k_under) * (under - here)
    )
    return here + SOLID_STEP * flow


def conduct_of(conductivity, solid):
    return conductivity * (1.0 + 0.25 * jnp.tanh(solid))


def metal_step(own, halo, c_own, c_halo, keep):
    depth_cells = own.shape[0]
    k_own, k_halo = conduct_of(c_own, own), conduct_of(c_halo, halo)
    lane, sub = lanes(depth_cells), subs(depth_cells)

    def depth(x):
        up = jnp.where(sub == 0, x, turn(x, 1, 0))
        down = jnp.where(sub == depth_cells - 1, x, turn(x, -1, 0))
        return up, down

    def stream(x, other):
        prev = jnp.where(lane == 0, turn(other, 1), turn(x, 1))
        following = jnp.where(lane == FS - 1, turn(other, -1), turn(x, -1))
        return prev, following

    def update(x, k, other, k_other):
        flow = jnp.zeros_like(x)
        for a, ka in zip(stream(x, other) + depth(x), stream(k, k_other) + depth(k)):
            flow = flow + 0.5 * (k + ka) * (a - x)
        new = x + SOLID_STEP * flow
        return new + jnp.where(sub == SD - 1, SOLID_STEP * COOLING * (COOLANT - x), 0.0)

    return update(own, k_own, halo, k_halo), update(halo, k_halo, own, k_own) * keep


def row_of(table, index):
    return jnp.sum(jnp.where(subs(NB) == index, table, 0.0), axis=0, keepdims=True)


def set_walls(own, halo, walls, me, keep):
    sub, lane = subs(own.shape[0]), lanes(own.shape[0])
    beside = jnp.where(lane >= FS // 2, row_of(walls, me - 1), row_of(walls, me + 1)) * keep
    return jnp.where(sub == 0, row_of(walls, me), own), jnp.where(sub == 0, beside, halo)


def metal_halo(turned, rows):
    deep = turned[FP : FP + rows]
    lane = lanes(rows)

    def placed(left, right):
        return jnp.where(
            lane >= 124, turn(deep, left), jnp.where(lane < 4, turn(deep, right), 0.0)
        )

    return placed(108, 104), placed(104, 100)


def place_of(peer, order):
    return sum(jnp.where(peer == k, order.index(k), 0) for k in range(NB))


def rows_of(recv, row, order):
    return jnp.concatenate([recv[order.index(k), row : row + 1, :] for k in range(NB)], axis=0)


def keeps(me):
    return (me > 0).astype(F32), (me < NB - 1).astype(F32)


def block_of(recv, me, start, order=ORDER0):
    keep_l, keep_r = keeps(me)
    before = place_of(jnp.maximum(me - 1, 0), order)
    after = place_of(jnp.minimum(me + 1, NB - 1), order)
    part = slice(start, start + 8)
    return recv[before, part, :] * keep_l, recv[after, part, :] * keep_r


def column_blocks(mt):
    right = mt[pl.ds(1, FZ, stride=4), :], mt[pl.ds(0, FZ, stride=4), :]
    left = mt[pl.ds(2, FZ, stride=4), :], mt[pl.ds(3, FZ, stride=4), :]
    return right, left


def flows(mt):
    right, left = mt[pl.ds(32, FZ, stride=2), :], mt[pl.ds(33, FZ, stride=2), :]
    return (turn(right, 64), right, mt[48:49, :]), (turn(left, 64), left, mt[49:50, :])


def gather_columns(fluid, lane):
    acc = jnp.zeros((FP, FS), F32)
    for z in range(FZ):
        acc = jnp.where(lane // 4 == z, turn(fluid[z], 4 * z + 2), acc)
    return acc


def sorted_rows(first, second):
    even = lax.axis_index("sec") % 2 == 0
    return (
        lambda a, b: jnp.where(even, second[a:b, :], first[a:b, :]),
        lambda a, b: jnp.where(even, first[a:b, :], second[a:b, :]),
    )


def send_rows(first, second, start, up, down):
    even = lax.axis_index("sec") % 2 == 0
    part = slice(start, start + up.shape[0])
    first[part, :] = jnp.where(even, up, down)
    second[part, :] = jnp.where(even, down, up)


def up_factor(pv):
    return SPREAD + ADVECT * jnp.maximum(pv, 0.0)


def down_factor(pv):
    return SPREAD + ADVECT * jnp.maximum(-pv, 0.0)


def fetch(copies, sems):
    started = [
        pltpu.make_async_copy(src, dst, sems.at[i]) for i, (src, dst) in enumerate(copies)
    ]
    for copy in started:
        copy.start()
    return started


def open_kernel(
    fluid_in, sv_in, pv_in, film_in, solid_in, cond_in, owner,
    out, first, second, mt, names, fluid, sv, pv, film, solid, cond, ids, sems,
):
    me = lax.axis_index("blk")
    half = FZ // 2
    copies = [(owner, ids), (film_in, film), (solid_in, solid), (cond_in, cond)]
    copies += [(fluid_in, fluid), (pv_in, pv), (sv_in, sv)]
    started = fetch(copies, sems)
    lane = lanes(FP)
    for copy in started[:4]:
        copy.wait()
    ids_row = jnp.concatenate([ids[...].astype(F32), jnp.zeros((1, FS - FP), F32)], axis=1)
    named = jnp.broadcast_to(ids_row, (FS, FS)).T[:FP]
    names[...] = named
    metal = jnp.zeros((SD, FS), F32)
    thin = lanes(SD)
    s, c = solid[...], cond[...]
    for k in range(4):
        metal = jnp.where(thin == 4 * k + 1, turn(s, 3 * k + 5), metal)
        metal = jnp.where(thin == 4 * k + 2, turn(s, 3 * k + 2), metal)
        metal = jnp.where(thin == 4 * k + 17, turn(c, 3 * k + 21), metal)
        metal = jnp.where(thin == 4 * k + 18, turn(c, 3 * k + 18), metal)
    started[4].wait()
    a0, h = by_owner(named, [film[...] * fluid[0], film[...]])
    top = gather_columns(fluid, lane)
    send_rows(first, second, 0, fluid[:, FP - 1, :], fluid[:, 0, :])
    blank = jnp.zeros((7, FS), F32)
    send_rows(
        first, second, 40,
        jnp.concatenate([film[FP - 1 : FP, :], blank], axis=0),
        jnp.concatenate([film[0:1, :], blank], axis=0),
    )
    for copy in started[5:]:
        copy.wait()
    bottom = jnp.zeros((FP, FS), F32)
    pair = (lane - 32) // 2
    for z in range(FZ):
        here = (pair == z) & (lane >= 32)
        top = jnp.where(here, turn(pv[z], 33 + 2 * z), top)
        bottom = jnp.where(here, turn(sv[z], 33 + 2 * z), bottom)
    send_rows(first, second, 8, sv[:, FP - 2, :], sv[:, 1, :])
    send_rows(first, second, 16, sv[:, FP - 1, :], sv[:, 0, :])
    send_rows(first, second, 24, pv[:, FP - 2, :], pv[:, 1, :])
    send_rows(first, second, 32, pv[:, FP - 1, :], pv[:, 0, :])
    top = jnp.where(lane // 2 == 24, turn(film[...], 49), top)
    top = jnp.where(lane == 50, named, top)
    metal = jnp.where(thin < 32, metal, bottom[:SD])
    mt[...] = jnp.concatenate([top, metal, bottom[SD:]], axis=0).T

    (r0, r1), (l0, l1) = column_blocks(mt)
    (sv_r, pv_r, film_r), (sv_l, pv_l, film_l) = flows(mt)
    wide = lanes(FZ)
    right_part = edge_part(r0, 0.0, 0.0, r1, 0.0, sv_r, pv_r, film_r)
    left_part = edge_part(l0, 0.0, 0.0, 0.0, l1, sv_l, pv_l, film_l)
    right_part = jnp.where(wide < FP, right_part, SPREAD)
    left_part = jnp.where(wide < FP, left_part, turn(SPREAD + ADVECT * sv_l, 64))

    def with_factors(block, p):
        block = jnp.where(wide == 96, turn(up_factor(p), 96), block)
        return jnp.where(wide == 97, turn(down_factor(p), 97 - (FP - 1)), block)

    r0, l0 = with_factors(r0, pv_r), with_factors(l0, pv_l)
    owner_row = turn(mt[50:51, :], 64)
    inside = lanes(1) < FP
    right_row, left_row = (jnp.where(inside, f, owner_row) for f in (film_r, film_l))
    head = jnp.concatenate([s[0:2], c[0:2], named[FP - 1 : FP], named[0:1]], axis=0)
    for peer in range(NB):
        ahead = (me + 1 == peer).astype(F32)
        behind = (me - 1 == peer).astype(F32)
        special = right_row * ahead + left_row * behind
        out[ORDER0.index(peer), 0:8, :] = jnp.concatenate([head, special, special], axis=0)
        out[ORDER0.index(peer), 8:16, :] = a0
        out[ORDER0.index(peer), 16:24, :] = h
        same = (me == peer).astype(F32)
        out[ORDER0.index(peer), 24:32, :] = r0 * ahead + l0 * behind + r0 * same
        out[ORDER0.index(peer), 32:40, :] = right_part * ahead + left_part * behind + l0 * same


def halo_columns(known_l, known_r, factor_l, factor_r, rows, mine_right, mine_left, walls, me):
    keep_l, keep_r = keeps(me)
    (film_l, own_l), (film_r, own_r) = rows
    top = subs(FZ) == 0
    wall_l, wall_r = pick_lane(own_l, walls, FS - 1), pick_lane(own_r, walls, 0)
    new_l = known_l + factor_l * mine_left + jnp.where(top, WALL * film_l * wall_l, 0.0)
    new_r = known_r + factor_r * mine_right + jnp.where(top, WALL * film_r * wall_r, 0.0)
    return new_l * keep_l, new_r * keep_r


def edge_rows(recv, me):
    return [(block[6:7], turn(block[6:7], 64)) for block in block_of(recv, me, 0)]


def first_kernel(
    recv, partial, toward, up, down, film, solid, cond, owner, first, second,
    fluid1, first_out, second_out, turned, side, tm,
):
    me = lax.axis_index("blk")
    lo, hi = sorted_rows(first, second)
    left, right = block_of(recv, me, 24)
    part_l, part_r = block_of(recv, me, 32)
    wall0, under0 = rows_of(recv, 0, ORDER0), rows_of(recv, 1, ORDER0)
    c0, c1 = rows_of(recv, 2, ORDER0), rows_of(recv, 3, ORDER0)
    a0, h = recv[0, 8:16, :], recv[0, 16:24, :]
    for j in range(1, NB):
        a0, h = a0 + recv[j, 8:16, :], h + recv[j, 16:24, :]
    wall1 = strip_row(wall0, conduct_of(c0, wall0), under0, conduct_of(c1, under0))
    wall1 = wall1 + SOLID_STEP * (a0 - h * wall0)

    here = place_of(me, ORDER0)
    mine_right, mine_left = recv[here, 24:32, :], recv[here, 32:40, :]
    new_l, new_r = halo_columns(
        part_l, part_r, turn(part_l, 64), turn(part_r, 64), edge_rows(recv, me),
        mine_right, mine_left, wall0, me,
    )
    tm[...] = jnp.zeros((FS, FS), F32)
    tm[pl.ds(0, FZ, stride=2), :] = right
    tm[pl.ds(1, FZ, stride=2), :] = left
    tm[16:24, :] = left
    tm[24:32, :] = right
    tm[pl.ds(32, FZ, stride=2), :] = new_r
    tm[pl.ds(33, FZ, stride=2), :] = new_l
    turned[...] = tm[...].T
    named = owner[...]
    walls0, walls1 = pick(named, wall0), pick(named, wall1)
    factors = (toward, up, down)
    columns = turned[:FP, :]
    complete(partial, fluid1, lo(0, 8), hi(0, 8), columns, factors, film[...], walls0)
    flux = film[...] * (fluid1[0] - walls1)
    (shares,) = by_owner(named, [flux])

    keep_l, keep_r = keeps(me)
    keep = jnp.where(lanes(8) >= FS // 2, keep_l, keep_r)
    halo, c_halo = metal_halo(turned, 8)
    own, halo = metal_step(solid[0:8, :], halo, cond[0:8, :], c_halo, keep)
    own, halo = set_walls(own, halo, wall1, me, keep)
    own, _ = metal_step(own, halo, cond[0:8, :], c_halo, keep)
    shares = SOLID_STEP * shares + jnp.where(subs(NB) == me, own[0:1], 0.0)
    side[0:8, :], side[8:16, :], side[16:24, :] = wall1, shares, h

    lane = lanes(FZ)

    def corners(at, beside, factor):
        out = jnp.zeros((FZ, FS), F32)
        for i, (old, new) in enumerate(((left, new_l), (right, new_r))):
            for k, (source, lane_of) in enumerate(
                ((old, at), (new, at), (old, factor), (new, beside))
            ):
                out = jnp.where(lane == 4 * i + k, turn(source, 4 * i + k - lane_of), out)
        return out

    blank = jnp.zeros((6, FS), F32)
    for i in range(3):
        send_rows(first_out, second_out, 8 * i, fluid1[:, FP - 3 + i, :], fluid1[:, 2 - i, :])
    send_rows(first_out, second_out, 24, corners(FP - 1, FP - 2, 97), corners(0, 1, 96))
    ids_last, ids_first = rows_of(recv, 4, ORDER0), rows_of(recv, 5, ORDER0)
    send_rows(first_out, second_out, 32, pick(ids_last, shares), pick(ids_first, shares))
    send_rows(
        first_out, second_out, 40,
        jnp.concatenate([flux[FP - 2 : FP], blank], axis=0),
        jnp.concatenate([flux[1:2], flux[0:1], blank], axis=0),
    )


def sums_kernel(
    fluid1, turned, side, toward, up, down, film, solid, cond, owner,
    fluid2, mt, sums, metal,
):
    me = lax.axis_index("blk")
    lane, sub = lanes(FP), subs(FP)
    named, f = owner[...], film[...]
    wall1 = side[0:8, :]
    none = jnp.zeros((FZ, FS), F32)
    factors = (toward, up, down)
    advance(fluid1, fluid2, none, none, turned[:FP, :], 32, factors, f, pick(named, wall1))
    x = fluid2[0]
    low, high = turn(x, 1, 0), turn(x, -1, 0)
    before = jnp.where(lane == 0, 0.0, turn(x, 1))
    after = jnp.where(lane == FS - 1, 0.0, turn(x, -1))
    moved = factored(
        x, low, high, before, after, x, fluid2[1], toward[0], up[0], down[0]
    ) - WALL * f * x
    within = jnp.where((sub == 0) | (sub == FP - 1), 0.0, f)
    deep = jnp.where((sub < 2) | (sub >= FP - 2), 0.0, f)
    sums[0:8, :], sums[8:16, :], sums[16:24, :] = by_owner(
        named, [within * x, deep * moved, f * f]
    )
    whole = jnp.concatenate([gather_columns(fluid2, lane), jnp.zeros((FP, FS), F32)], axis=0)
    mt[...] = whole.T
    keep_l, keep_r = keeps(me)
    keep = jnp.where(lanes(SD) >= FS // 2, keep_l, keep_r)
    halo, c_halo = metal_halo(turned, SD)
    own, halo = metal_step(solid[...], halo, cond[...], c_halo, keep)
    own, halo = set_walls(own, halo, wall1, me, keep)
    own, halo = metal_step(own, halo, cond[...], c_halo, keep)
    metal[0:SD, :], metal[SD : 2 * SD, :], metal[2 * SD : 3 * SD, :] = own, halo, c_halo


def pack_kernel(
    recv, mt_old, mt, sums, metal, side, fluid1, fluid2, toward, up, down, film, owner,
    first, second, first1, second1, sent, out, edge,
):
    me = lax.axis_index("blk")
    lane, sub = lanes(FZ), subs(FZ)
    keep_l, keep_r = keeps(me)
    lo, hi = sorted_rows(first, second)
    lo1, hi1 = sorted_rows(first1, second1)
    left, right = block_of(recv, me, 24)

    def outside(rows, rows1, inner, near_l, near_r):
        far, mid, near = rows1(0, 8), rows1(8, 16), rows1(16, 24)
        corner = rows1(24, 32)

        def at(k, to):
            return turn(corner, to - k)

        def lane_at(x, of, to):
            return turn(x, to - of)

        old_l, old_r = at(0, 0), at(4, FS - 1)
        side_l = at(1, 0) + at(2, 0) * lane_at(left, near_l, 0)
        side_r = at(5, FS - 1) + at(6, FS - 1) * lane_at(right, near_r, FS - 1)
        return far, mid, near, (old_l, old_r), (side_l, side_r), (at(3, 0), at(7, FS - 1))

    def finish(rows, rows1, inner, own_partial, factor, near_lane, factor_lane, upward):
        far, mid, near, old, beside, beside2 = outside(rows, rows1, inner, near_lane, near_lane)
        sv2, sv1, pv2, pv1 = rows(8, 16), rows(16, 24), rows(24, 32), rows(32, 40)
        flux = rows1(40, 42)
        order = (mid, inner) if upward else (inner, mid)
        new1 = halo_row(near, *order, *beside, sv1, pv1, flux[1:2])
        order = (far, near) if upward else (near, far)
        new2 = halo_row(mid, *order, *beside2, sv2, pv2, flux[0:1])
        through_l = turn(left, -factor_lane) * old[0]
        through_r = turn(right, FS - 1 - factor_lane) * old[1]
        own = own_partial + factor * near
        toward_here = toward[:, 0 if upward else FP - 1, :]
        own = own + jnp.where(lane == 0, toward_here * through_l, 0.0)
        own = own + jnp.where(lane == FS - 1, SPREAD * through_r, 0.0)
        return new1, new2, own

    low1, low2, x_first = finish(
        lo, lo1, fluid1[:, 0, :], fluid2[:, 0, :], up[:, 0, :], 0, 96, True
    )
    high1, high2, x_last = finish(
        hi, hi1, fluid1[:, FP - 1, :], fluid2[:, FP - 1, :], down[:, FP - 1, :],
        FP - 1, 97, False,
    )

    (r0, r1), (l0, l1) = column_blocks(mt)

    def patched(block, column):
        block = jnp.where(lane == 0, turn(x_first, -column), block)
        return jnp.where(lane == FP - 1, turn(x_last, FP - 1 - column), block)

    r0, r1 = patched(r0, FS - 1), patched(r1, FS - 2)
    l0, l1 = patched(l0, 0), patched(l1, 1)
    (sv_r, pv_r, film_r), (sv_l, pv_l, film_l) = flows(mt_old)

    def ends(column):
        return turn(low1, -column), turn(high1, FP - 1 - column)

    right_part = edge_part(r0, *ends(FS - 1), r1, 0.0, sv_r, pv_r, film_r)
    left_part = edge_part(l0, *ends(0), 0.0, l1, sv_l, pv_l, film_l)

    def corner_row(column):
        rows = []
        for i, x in enumerate((low1, high1)):
            spread = jnp.broadcast_to(x[:, column : column + 1], (FZ, FS))
            rows.append(
                jnp.sum(jnp.where(lane == sub + 8 * i, spread, 0.0), axis=0, keepdims=True)
            )
        return rows[0] + rows[1]

    rows = (0, 1, FP - 2, FP - 1)

    def stack(parts):
        return jnp.concatenate(list(parts) + [jnp.zeros((4, FS), F32)], axis=0)

    layer = {r: fluid2[0, r : r + 1, :] for r in (1, 2, FP - 3, FP - 2)}
    layer[-1], layer[0], layer[FP - 1], layer[FP] = (
        low1[0:1], x_first[0:1], x_last[0:1], high1[0:1],
    )
    here = stack(layer[r] for r in rows)
    above = stack([x_first[1:2], fluid2[1, 1:2, :], fluid2[1, FP - 2 : FP - 1, :], x_last[1:2]])
    f4 = stack(film[r : r + 1, :] for r in rows)
    factors = [stack(part[0, r : r + 1, :] for r in rows) for part in (toward, up, down)]
    before = jnp.where(lane == 0, 0.0, turn(here, 1))
    after = jnp.where(lane == FS - 1, 0.0, turn(here, -1))
    moved = f4 * (
        factored(
            here, stack(layer[r - 1] for r in rows), stack(layer[r + 1] for r in rows),
            before, after, here, above, *factors,
        )
        - WALL * f4 * here
    )
    direct = f4 * here
    a2, b3, h2 = sums[0:8, :], sums[8:16, :], sums[16:24, :]
    for i, r in enumerate(rows):
        hit = owner[r : r + 1, :] == sub.astype(F32)
        b3 = b3 + jnp.where(hit, moved[i : i + 1], 0.0)
        if r in (0, FP - 1):
            a2 = a2 + jnp.where(hit, direct[i : i + 1], 0.0)
    (film_bl, own_bl), (film_br, own_br) = edge_rows(recv, me)
    _, part_r = block_of(recv, me, 32)
    inside = lane < FP

    def shared(own_row, term):
        hit = (jnp.broadcast_to(own_row, (NB, FS)) == sub.astype(F32)) & inside
        return jnp.sum(jnp.where(hit, term, 0.0), axis=1, keepdims=True)

    right_term = film_br * turn(part_r, 64)[0:1] * r0[0:1] * keep_r
    left_term = film_bl * SPREAD * l0[0:1] * keep_l
    b3 = b3 + jnp.where(lane == 0, shared(own_br, right_term), 0.0)
    b3 = b3 + jnp.where(lane == FS - 1, shared(own_bl, left_term), 0.0)

    right_corner, left_corner = corner_row(FS - 1), corner_row(0)
    to_right = jnp.where(inside, r0, turn(right_part, 64))
    to_left = jnp.where(inside, l0, turn(left_part, 64))
    relay_lo, relay_hi = lo1(32, 40), hi1(32, 40)
    blank = jnp.zeros((2, FS), F32)
    for peer in range(NB):
        ahead = (me + 1 == peer).astype(F32)
        behind = (me - 1 == peer).astype(F32)
        out[ORDER1.index(peer), 0:8, :] = jnp.concatenate(
            [
                metal[1:2, :],
                b3[peer : peer + 1],
                h2[peer : peer + 1],
                relay_lo[peer : peer + 1],
                relay_hi[peer : peer + 1],
                right_corner * ahead + left_corner * behind,
                blank,
            ],
            axis=0,
        )
        out[ORDER1.index(peer), 8:16, :] = side[8:16, :]
        out[ORDER1.index(peer), 16:24, :] = a2
        out[ORDER1.index(peer), 24:32, :] = to_right * ahead + to_left * behind
    kept = (
        low1, low2, high1, high2, r0, l0, x_first, x_last,
        lo(16, 24), lo(32, 40), hi(16, 24), hi(32, 40), lo(40, 48), hi(40, 48),
    )
    for i, value in enumerate(kept):
        edge[8 * i : 8 * i + 8, :] = value


def last_kernel(
    recv1, recv, edge, side, metal, fluid2, toward, up, down, film, cond, owner,
    fluid_out, solid_out,
    tm, fluid3,
):
    me = lax.axis_index("blk")
    lane, sub = lanes(FZ), subs(FZ)
    (
        low1, low2, high1, high2, mine_right, mine_left, x_first, x_last,
        sv_lo, pv_lo, sv_hi, pv_hi, film_lo, film_hi,
    ) = [edge[8 * i : 8 * i + 8, :] for i in range(14)]
    left, right = block_of(recv1, me, 24, ORDER1)
    corner_l, corner_r = (block[5:6] for block in block_of(recv1, me, 0, ORDER1))
    part_l, part_r = block_of(recv, me, 32)
    c0, c1, h = rows_of(recv, 2, ORDER0), rows_of(recv, 3, ORDER0), side[16:24, :]
    tail, wall2, a2 = recv1[0, 0:8, :], recv1[0, 8:16, :], recv1[0, 16:24, :]
    for j in range(1, NB):
        tail = tail + recv1[j, 0:8, :]
        wall2 = wall2 + recv1[j, 8:16, :]
        a2 = a2 + recv1[j, 16:24, :]
    under2 = rows_of(recv1, 0, ORDER1)
    wall3 = strip_row(wall2, conduct_of(c0, wall2), under2, conduct_of(c1, under2))
    wall3 = wall3 + SOLID_STEP * (a2 - h * wall2)
    inflow3 = tail[1:2] + WALL * tail[2:3] * row_of(wall2, me) - row_of(h * wall3, me)

    new_l, new_r = halo_columns(
        turn(left, 64), turn(right, 64), turn(part_l, 64), turn(part_r, 64),
        edge_rows(recv, me), mine_right, mine_left, wall2, me,
    )
    tm[...] = jnp.zeros((FS, FS), F32)
    tm[pl.ds(0, FZ, stride=2), :] = right
    tm[pl.ds(1, FZ, stride=2), :] = left
    tm[pl.ds(32, FZ, stride=2), :] = new_r
    tm[pl.ds(33, FZ, stride=2), :] = new_l
    columns = tm[...].T[:FP]

    def corner(row, which):
        spread = jnp.broadcast_to(row, (FZ, FS))
        return jnp.sum(jnp.where(lane == sub + 8 * which, spread, 0.0), axis=1, keepdims=True)

    new_low = halo_row(
        low1, low2, x_first, corner(corner_l, 0), corner(corner_r, 0), sv_lo, pv_lo,
        film_lo[0:1] * (low1[0:1] - tail[3:4]),
    )
    new_high = halo_row(
        high1, x_last, high2, corner(corner_l, 1), corner(corner_r, 1), sv_hi, pv_hi,
        film_hi[0:1] * (high1[0:1] - tail[4:5]),
    )
    named, f = owner[...], film[...]
    source = [
        set_row(set_row(fluid2[z], x_first[z : z + 1], 0), x_last[z : z + 1], 1)
        for z in range(FZ)
    ]
    factors = (toward, up, down)
    advance(source, fluid3, low1, high1, columns, 0, factors, f, pick(named, wall2))
    walls3 = pick(named, wall3)
    advance(fluid3, fluid_out, new_low, new_high, columns, 32, factors, f, walls3)

    keep_l, keep_r = keeps(me)
    keep = jnp.where(lanes(SD) >= FS // 2, keep_l, keep_r)
    own, halo, c_halo = metal[0:SD, :], metal[SD : 2 * SD, :], metal[2 * SD : 3 * SD, :]
    own, halo = set_walls(own, halo, wall2, me, keep)
    own, halo = metal_step(own, halo, cond[...], c_halo, keep)
    own, halo = set_walls(own, halo, wall3, me, keep)
    own, _ = metal_step(own, halo, cond[...], c_halo, keep)
    solid_out[...] = own + jnp.where(subs(SD) == 0, SOLID_STEP * inflow3, 0.0)


def shape(*dims):
    return jax.ShapeDtypeStruct(dims, F32)


VMEM = pl.BlockSpec(memory_space=pltpu.VMEM)
GRANT = 54 * 1024 * 1024
HBM = pl.BlockSpec(memory_space=pltpu.HBM)


def call(kernel, outs, args, name, scratch=(), far=0, limit=32 * 1024 * 1024):
    return pl.pallas_call(
        kernel,
        out_shape=outs,
        in_specs=[HBM] * far + [VMEM] * (len(args) - far),
        out_specs=jax.tree.map(lambda _: VMEM, outs),
        scratch_shapes=scratch,
        name=name,
        compiler_params=pltpu.CompilerParams(vmem_limit_bytes=limit),
    )(*args)


def both_ways(first, second):
    count = lax.axis_size("sec")
    near = [(i, i ^ 1) for i in range(count)]
    far = [(i, (i + 1 if i % 2 else i - 1) % count) for i in range(count)]
    second = lax.ppermute(second, "sec", far)
    return lax.ppermute(first, "sec", near), second


def swap(message, order):
    return lax.all_to_all(
        message, "blk", split_axis=0, concat_axis=0, tiled=True, axis_index_groups=[list(order)]
    )


def two_exchanges(fluid, sv, pv, film, solid, cond, face_owner):
    owner = face_owner.reshape(1, FP)
    solid, cond = solid.reshape(SD, FS), cond.reshape(SD, FS)
    field, rows = shape(FZ, FP, FS), shape(ROWS, FS)
    held = [pltpu.VMEM((FZ, FP, FS), F32)] * 3
    held += [pltpu.VMEM((n, FS), F32) for n in (FP, SD, SD)]
    message, first, second, mt, owner = call(
        open_kernel,
        (shape(NB, R0, FS), rows, rows, shape(FS, FS), shape(FP, FS)),
        (fluid, sv, pv, film, solid, cond, owner),
        "open",
        held + [pltpu.VMEM((1, FP), jnp.int32), pltpu.SemaphoreType.DMA((10,))],
        far=7,
        limit=GRANT - OPEN_ROOM,
    )
    first, second = both_ways(first, second)
    recv = swap(message, ORDER0)
    *factors, partial = call(
        prepare_kernel,
        (field,) * 4,
        (fluid, sv, pv, film),
        "prepare",
        [pltpu.VMEM((FZ, FP, FS), F32)] * 3 + [pltpu.SemaphoreType.DMA((3,))],
        far=3,
        limit=GRANT - PREPARE_ROOM,
    )
    fluid1, first_sent, second_sent, turned, side = call(
        first_kernel,
        (field, rows, rows, shape(FS, FS), shape(24, FS)),
        (recv, partial, *factors, film, solid, cond, owner, first, second),
        "first",
        [pltpu.VMEM((FS, FS), F32)],
    )
    first1, second1 = both_ways(first_sent, second_sent)
    fluid2, mt2, sums, metal = call(
        sums_kernel,
        (field, shape(FS, FS), shape(24, FS), shape(3 * SD, FS)),
        (fluid1, turned, side, *factors, film, solid, cond, owner),
        "sums",
    )
    message, edge = call(
        pack_kernel,
        (shape(NB, R1, FS), shape(14 * 8, FS)),
        (
            recv, mt, mt2, sums, metal, side, fluid1, fluid2, *factors, film, owner,
            first, second, first1, second1, first_sent,
        ),
        "pack",
    )
    recv1 = swap(message, ORDER1)
    fluid, solid = call(
        last_kernel,
        (field, shape(SD, FS)),
        (recv1, recv, edge, side, metal, fluid2, *factors, film, cond, owner),
        "last",
        [pltpu.VMEM((FS, FS), F32), pltpu.VMEM((FZ, FP, FS), F32)],
    )
    return fluid, solid.reshape(1, SD, FS)


def padded(block, sides, width, periodic):
    for axis, dim in sides:
        count = lax.axis_size(axis)
        forward = [(i, i + 1) for i in range(count - 1)]
        if periodic:
            forward.append((count - 1, 0))
        backward = [(target, source) for source, target in forward]
        low = lax.ppermute(
            lax.slice_in_dim(block, block.shape[dim] - width, None, axis=dim), axis, forward
        )
        high = lax.ppermute(lax.slice_in_dim(block, 0, width, axis=dim), axis, backward)
        block = jnp.concatenate([low, block, high], axis=dim)
    return block


def fluid_update(
    fluid, stream_velocity, pitch_velocity, wall_flux, pitch_extended, stream_extended
):
    pitch_prev = pitch_extended[:, :-2]
    pitch_next = pitch_extended[:, 2:]
    stream_prev = stream_extended[:, :, :-2]
    stream_next = stream_extended[:, :, 2:]
    span_prev = jnp.concatenate([fluid[:1], fluid[:-1]], 0)
    span_next = jnp.concatenate([fluid[1:], fluid[-1:]], 0)
    spread = SPREAD * (
        pitch_prev + pitch_next + stream_prev + stream_next + span_prev + span_next - 6.0 * fluid
    )
    carried = (
        -ADVECT * stream_velocity * (fluid - stream_prev)
        - ADVECT * jnp.maximum(pitch_velocity, 0.0) * (fluid - pitch_prev)
        + ADVECT * jnp.maximum(-pitch_velocity, 0.0) * (pitch_next - fluid)
    )
    updated = fluid + spread + carried
    return updated.at[0].add(-WALL * wall_flux)


def solid_update(solid, conduct, inflow, solid_extended, conduct_extended):
    stream_prev = solid_extended[..., :-2]
    stream_next = solid_extended[..., 2:]
    conduct_prev = conduct_extended[..., :-2]
    conduct_next = conduct_extended[..., 2:]
    depth_prev = jnp.concatenate([solid[:, :1], solid[:, :-1]], 1)
    depth_next = jnp.concatenate([solid[:, 1:], solid[:, -1:]], 1)
    kdepth_prev = jnp.concatenate([conduct[:, :1], conduct[:, :-1]], 1)
    kdepth_next = jnp.concatenate([conduct[:, 1:], conduct[:, -1:]], 1)
    flow = (
        0.5 * (conduct + conduct_prev) * (stream_prev - solid)
        + 0.5 * (conduct + conduct_next) * (stream_next - solid)
        + 0.5 * (conduct + kdepth_prev) * (depth_prev - solid)
        + 0.5 * (conduct + kdepth_next) * (depth_next - solid)
    )
    updated = solid + SOLID_STEP * flow
    updated = updated.at[:, 0].add(SOLID_STEP * inflow)
    updated = updated.at[:, -1].add(SOLID_STEP * COOLING * (COOLANT - solid[:, -1]))
    return updated


def local(
    fluid_temp, stream_velocity, pitch_velocity, film_coeff, solid_temp, conductivity, face_owner
):
    span_cells, pitch_cells, stream_cells = fluid_temp.shape
    depth_cells = solid_temp.shape[1]
    block_count = lax.axis_size("blk")
    capacity = max(2, (pitch_cells + block_count - 1) // block_count)
    owners = face_owner.reshape(-1)
    onehot = (owners[:, None] == jnp.arange(block_count, dtype=jnp.int32)[None, :]).astype(
        jnp.float32
    )
    same_owner = owners[:, None] == owners[None, :]
    earlier = lax.broadcasted_iota(jnp.int32, (pitch_cells, pitch_cells), 0) < lax.broadcasted_iota(
        jnp.int32, (pitch_cells, pitch_cells), 1
    )
    slot_rank = jnp.sum((same_owner & earlier).astype(jnp.int32), axis=0)
    slot_table = (slot_rank[None, :] == jnp.arange(capacity, dtype=jnp.int32)[:, None]).astype(
        jnp.float32
    )
    placing = onehot.T[:, None, :] * slot_table[None, :, :]
    fluid = fluid_temp
    solid = solid_temp
    gas_rows = span_cells * pitch_cells
    for subiter in range(SUB):
        wall_row = solid[0, 0:1, :]
        wall_temp = jnp.dot(
            onehot,
            lax.all_gather(wall_row, "blk", axis=0, tiled=True),
            precision=lax.Precision.HIGHEST,
            preferred_element_type=jnp.float32,
        )
        flux = film_coeff * (fluid[0] - wall_temp)
        outgoing = jnp.einsum("ocb,bf->ocf", placing, flux, precision=lax.Precision.HIGHEST)
        received = lax.all_to_all(outgoing, "blk", split_axis=0, concat_axis=0, tiled=True)
        inflow = jnp.sum(received, axis=(0, 1))
        conduct = conductivity * (1.0 + 0.25 * jnp.tanh(solid))
        stacked = jnp.concatenate([fluid.reshape(gas_rows, stream_cells), solid[0], conduct[0]], 0)
        stream_ext = padded(stacked, (("blk", 1),), 1, False)
        pitch_extended = padded(fluid, (("sec", 1),), 1, True)
        fluid_stream = stream_ext[:gas_rows].reshape(span_cells, pitch_cells, stream_cells + 2)
        solid_stream = stream_ext[gas_rows : gas_rows + depth_cells][None]
        conduct_stream = stream_ext[gas_rows + depth_cells :][None]
        fluid = fluid_update(
            fluid, stream_velocity, pitch_velocity, flux, pitch_extended, fluid_stream
        )
        solid = solid_update(solid, conduct, inflow[None, :], solid_stream, conduct_stream)
    return (fluid, solid)


def solution(mesh):
    placed = (
        P(None, "sec", "blk"),
        P(None, "sec", "blk"),
        P(None, "sec", "blk"),
        P("sec", "blk"),
        P("sec", None, "blk"),
        P("sec", None, "blk"),
        P("sec", "blk", None, None),
    )
    sizes = dict(mesh.shape)

    def chosen(*args):
        fits = args[0].shape == (FZ, FP, FS) and args[4].shape == (1, SD, FS)
        fits = fits and sizes["blk"] == NB and sizes["sec"] % 2 == 0
        return two_exchanges(*args) if fits else local(*args)

    return jax.shard_map(
        chosen,
        mesh=mesh,
        in_specs=placed,
        out_specs=(P(None, "sec", "blk"), P("sec", None, "blk")),
        check_vma=False,
    )
```

```python
import jax
import jax.numpy as jnp
from jax import lax
from jax.experimental import pallas as pl
from jax.experimental.pallas import tpu as pltpu
from jax.sharding import PartitionSpec as P

SUB = 4


ADVECT = 0.4
SPREAD = 0.04
WALL = 0.4
SOLID_STEP = 0.04
COOLING = 0.5
COOLANT = -1.0

F32 = jnp.float32
NB = 8
FZ = 8
FP = 64
FS = 128
SD = 32
R0 = 40
R1 = 32
ROWS = 48
OPEN_ROOM = 56 * 1024
PREPARE_ROOM = 1400 * 1024
ORDER0 = ((5, 0, 1, 2, 6, 3, 4, 7), (4, 1, 0, 3, 7, 2, 5, 6))
ORDER1 = ((5, 2, 6, 4, 1, 0, 7, 3),) * 2


def lanes(rows):
    return lax.broadcasted_iota(jnp.int32, (rows, FS), 1)


def subs(rows):
    return lax.broadcasted_iota(jnp.int32, (rows, FS), 0)


def turn(x, shift, axis=1):
    return pltpu.roll(x, shift % x.shape[axis], axis)


def by_owner(owner, values):
    sub = subs(NB)
    outs = [jnp.zeros((NB, FS), F32) for _ in values]
    for o in range(NB):
        mine = owner == o
        for i, value in enumerate(values):
            total = jnp.sum(jnp.where(mine, value, 0.0), axis=0, keepdims=True)
            outs[i] = jnp.where(sub == o, total, outs[i])
    return outs


def pick(owner, table):
    out = jnp.zeros(owner.shape, F32)
    for o in range(NB):
        out = jnp.where(owner == o, table[o : o + 1], out)
    return out


def pick_lane(owner_row, table, lane):
    column = jnp.broadcast_to(table[:, lane : lane + 1], (NB, FS))
    named = jnp.broadcast_to(owner_row, (NB, FS)) == subs(NB).astype(F32)
    return jnp.sum(jnp.where(named, column, 0.0), axis=0, keepdims=True)


def stencil(x, low, high, left, right, below, above, sv, pv):
    spread = SPREAD * (low + high + left + right + below + above - 6.0 * x)
    carried = (
        -ADVECT * sv * (x - left)
        - ADVECT * jnp.maximum(pv, 0.0) * (x - low)
        + ADVECT * jnp.maximum(-pv, 0.0) * (high - x)
    )
    return x + spread + carried


def factored(x, low, high, left, right, below, above, toward, up, down):
    new = (1.0 - 3.0 * SPREAD) * x + SPREAD * (right + below + above)
    return new + toward * (left - x) + up * (low - x) + down * (high - x)


def span(x):
    sub = subs(FZ)
    below = jnp.where(sub == 0, x, turn(x, 1, 0))
    above = jnp.where(sub == FZ - 1, x, turn(x, FZ - 1, 0))
    return below, above


def halo_row(x, low, high, left_corner, right_corner, sv, pv, flux):
    lane = lanes(FZ)
    left = jnp.where(lane == 0, left_corner, turn(x, 1))
    right = jnp.where(lane == FS - 1, right_corner, turn(x, -1))
    below, above = span(x)
    new = stencil(x, low, high, left, right, below, above, sv, pv)
    return new - jnp.where(subs(FZ) == 0, WALL * flux, 0.0)


def edge_part(x, low_end, high_end, left, right, sv, pv, film):
    lane = lanes(FZ)
    low = jnp.where(lane == 0, low_end, turn(x, 1))
    high = jnp.where(lane == FP - 1, high_end, turn(x, -1))
    below, above = span(x)
    new = stencil(x, low, high, left, right, below, above, sv, pv)
    return new - jnp.where(subs(FZ) == 0, WALL * film * x, 0.0)


def set_row(x, row, at):
    if at == 0:
        return jnp.concatenate([jnp.where(subs(8) == 0, row, x[:8]), x[8:]], axis=0)
    return jnp.concatenate([x[:-8], jnp.where(subs(8) == 7, row, x[-8:])], axis=0)


def advance(src, dst, low_row, high_row, columns, base, factors, film, wall):
    lane = lanes(FP)
    toward, up, down = factors
    for z in range(FZ):
        x = src[z]
        low = set_row(turn(x, 1, 0), low_row[z : z + 1], 0)
        high = set_row(turn(x, -1, 0), high_row[z : z + 1], 1)
        edge = turn(columns, -(base + 2 * z + 1))
        left = jnp.where(lane == 0, edge, turn(x, 1))
        right = jnp.where(lane == FS - 1, edge, turn(x, -1))
        below, above = src[max(z - 1, 0)], src[min(z + 1, FZ - 1)]
        new = factored(x, low, high, left, right, below, above, toward[z], up[z], down[z])
        if z == 0:
            new = new - WALL * film * (x - wall)
        dst[z] = new


def prepare_kernel(fluid_in, sv_in, pv_in, film, toward, up, down, partial, fluid, sv, pv, sems):
    started = fetch([(fluid_in, fluid), (sv_in, sv), (pv_in, pv)], sems)
    for copy in started:
        copy.wait()
    for z in range(FZ):
        toward[z] = SPREAD + ADVECT * sv[z]
        up[z] = up_factor(pv[z])
        down[z] = down_factor(pv[z])
    none = jnp.zeros((FZ, FS), F32)
    columns = jnp.zeros((FP, FS), F32)
    advance(fluid, partial, none, none, columns, 0, (toward, up, down), film[...], 0.0)


def complete(partial, dst, low_row, high_row, columns, factors, film, wall):
    lane = lanes(FP)
    toward, up, down = factors
    for z in range(FZ):
        edge = turn(columns, -(2 * z + 1))
        gain = jnp.where(lane == 0, toward[z], jnp.where(lane == FS - 1, SPREAD, 0.0))
        new = partial[z] + gain * edge
        if z == 0:
            new = new + WALL * film * wall
        first = new[:8] + jnp.where(subs(8) == 0, up[z, :8, :] * low_row[z : z + 1], 0.0)
        last = new[-8:] + jnp.where(subs(8) == 7, down[z, FP - 8 :, :] * high_row[z : z + 1], 0.0)
        dst[z] = jnp.concatenate([first, new[8:-8], last], axis=0)


def strip_row(here, k_here, under, k_under):
    sub, lane = subs(NB), lanes(NB)

    def prev(x):
        moved = turn(x, 1)
        carried = jnp.where(sub == 0, 0.0, turn(moved, 1, 0))
        return jnp.where(lane == 0, carried, moved)

    def following(x):
        moved = turn(x, -1)
        carried = jnp.where(sub == NB - 1, 0.0, turn(moved, -1, 0))
        return jnp.where(lane == FS - 1, carried, moved)

    flow = (
        0.5 * (k_here + prev(k_here)) * (prev(here) - here)
        + 0.5 * (k_here + following(k_here)) * (following(here) - here)
        + 0.5 * (k_here + k_under) * (under - here)
    )
    return here + SOLID_STEP * flow


def conduct_of(conductivity, solid):
    return conductivity * (1.0 + 0.25 * jnp.tanh(solid))


def metal_step(own, halo, c_own, c_halo, keep):
    depth_cells = own.shape[0]
    k_own, k_halo = conduct_of(c_own, own), conduct_of(c_halo, halo)
    lane, sub = lanes(depth_cells), subs(depth_cells)

    def depth(x):
        up = jnp.where(sub == 0, x, turn(x, 1, 0))
        down = jnp.where(sub == depth_cells - 1, x, turn(x, -1, 0))
        return up, down

    def stream(x, other):
        prev = jnp.where(lane == 0, turn(other, 1), turn(x, 1))
        following = jnp.where(lane == FS - 1, turn(other, -1), turn(x, -1))
        return prev, following

    def update(x, k, other, k_other):
        flow = jnp.zeros_like(x)
        for a, ka in zip(stream(x, other) + depth(x), stream(k, k_other) + depth(k)):
            flow = flow + 0.5 * (k + ka) * (a - x)
        new = x + SOLID_STEP * flow
        return new + jnp.where(sub == SD - 1, SOLID_STEP * COOLING * (COOLANT - x), 0.0)

    return update(own, k_own, halo, k_halo), update(halo, k_halo, own, k_own) * keep


def row_of(table, index):
    return jnp.sum(jnp.where(subs(NB) == index, table, 0.0), axis=0, keepdims=True)


def set_walls(own, halo, walls, me, keep):
    sub, lane = subs(own.shape[0]), lanes(own.shape[0])
    beside = jnp.where(lane >= FS // 2, row_of(walls, me - 1), row_of(walls, me + 1)) * keep
    return jnp.where(sub == 0, row_of(walls, me), own), jnp.where(sub == 0, beside, halo)


def metal_halo(turned, rows):
    deep = turned[FP : FP + rows]
    lane = lanes(rows)

    def placed(left, right):
        return jnp.where(
            lane >= 124, turn(deep, left), jnp.where(lane < 4, turn(deep, right), 0.0)
        )

    return placed(108, 104), placed(104, 100)


def place(peer, order):
    lower, upper = order[0].index(peer), order[1].index(peer)
    if lower == upper:
        return lower
    return jnp.where(2 * lax.axis_index("sec") >= lax.axis_size("sec"), upper, lower)


def place_of(peer, order):
    return sum(jnp.where(peer == k, place(k, order), 0) for k in range(NB))


def rows_of(recv, row, order):
    return jnp.concatenate([recv[place(k, order), row : row + 1, :] for k in range(NB)], axis=0)


def keeps(me):
    return (me > 0).astype(F32), (me < NB - 1).astype(F32)


def block_of(recv, me, start, order=ORDER0):
    keep_l, keep_r = keeps(me)
    before = place_of(jnp.maximum(me - 1, 0), order)
    after = place_of(jnp.minimum(me + 1, NB - 1), order)
    part = slice(start, start + 8)
    return recv[before, part, :] * keep_l, recv[after, part, :] * keep_r


def column_blocks(mt):
    right = mt[pl.ds(1, FZ, stride=4), :], mt[pl.ds(0, FZ, stride=4), :]
    left = mt[pl.ds(2, FZ, stride=4), :], mt[pl.ds(3, FZ, stride=4), :]
    return right, left


def flows(mt):
    right, left = mt[pl.ds(32, FZ, stride=2), :], mt[pl.ds(33, FZ, stride=2), :]
    return (turn(right, 64), right, mt[48:49, :]), (turn(left, 64), left, mt[49:50, :])


def gather_columns(fluid, lane):
    acc = jnp.zeros((FP, FS), F32)
    for z in range(FZ):
        acc = jnp.where(lane // 4 == z, turn(fluid[z], 4 * z + 2), acc)
    return acc


def sorted_rows(first, second):
    even = lax.axis_index("sec") % 2 == 0
    return (
        lambda a, b: jnp.where(even, second[a:b, :], first[a:b, :]),
        lambda a, b: jnp.where(even, first[a:b, :], second[a:b, :]),
    )


def send_rows(first, second, start, up, down):
    even = lax.axis_index("sec") % 2 == 0
    part = slice(start, start + up.shape[0])
    first[part, :] = jnp.where(even, up, down)
    second[part, :] = jnp.where(even, down, up)


def up_factor(pv):
    return SPREAD + ADVECT * jnp.maximum(pv, 0.0)


def down_factor(pv):
    return SPREAD + ADVECT * jnp.maximum(-pv, 0.0)


def fetch(copies, sems):
    started = [
        pltpu.make_async_copy(src, dst, sems.at[i]) for i, (src, dst) in enumerate(copies)
    ]
    for copy in started:
        copy.start()
    return started


def open_kernel(
    fluid_in, sv_in, pv_in, film_in, solid_in, cond_in, owner,
    out, first, second, mt, names, fluid, sv, pv, film, solid, cond, ids, sems,
):
    me = lax.axis_index("blk")
    half = FZ // 2
    copies = [(owner, ids), (film_in, film), (solid_in, solid), (cond_in, cond)]
    copies += [(fluid_in, fluid), (pv_in, pv), (sv_in, sv)]
    started = fetch(copies, sems)
    lane = lanes(FP)
    for copy in started[:4]:
        copy.wait()
    ids_row = jnp.concatenate([ids[...].astype(F32), jnp.zeros((1, FS - FP), F32)], axis=1)
    named = jnp.broadcast_to(ids_row, (FS, FS)).T[:FP]
    names[...] = named
    metal = jnp.zeros((SD, FS), F32)
    thin = lanes(SD)
    s, c = solid[...], cond[...]
    for k in range(4):
        metal = jnp.where(thin == 4 * k + 1, turn(s, 3 * k + 5), metal)
        metal = jnp.where(thin == 4 * k + 2, turn(s, 3 * k + 2), metal)
        metal = jnp.where(thin == 4 * k + 17, turn(c, 3 * k + 21), metal)
        metal = jnp.where(thin == 4 * k + 18, turn(c, 3 * k + 18), metal)
    started[4].wait()
    a0, h = by_owner(named, [film[...] * fluid[0], film[...]])
    top = gather_columns(fluid, lane)
    send_rows(first, second, 0, fluid[:, FP - 1, :], fluid[:, 0, :])
    blank = jnp.zeros((7, FS), F32)
    send_rows(
        first, second, 40,
        jnp.concatenate([film[FP - 1 : FP, :], blank], axis=0),
        jnp.concatenate([film[0:1, :], blank], axis=0),
    )
    for copy in started[5:]:
        copy.wait()
    bottom = jnp.zeros((FP, FS), F32)
    pair = (lane - 32) // 2
    for z in range(FZ):
        here = (pair == z) & (lane >= 32)
        top = jnp.where(here, turn(pv[z], 33 + 2 * z), top)
        bottom = jnp.where(here, turn(sv[z], 33 + 2 * z), bottom)
    send_rows(first, second, 8, sv[:, FP - 2, :], sv[:, 1, :])
    send_rows(first, second, 16, sv[:, FP - 1, :], sv[:, 0, :])
    send_rows(first, second, 24, pv[:, FP - 2, :], pv[:, 1, :])
    send_rows(first, second, 32, pv[:, FP - 1, :], pv[:, 0, :])
    top = jnp.where(lane // 2 == 24, turn(film[...], 49), top)
    top = jnp.where(lane == 50, named, top)
    metal = jnp.where(thin < 32, metal, bottom[:SD])
    mt[...] = jnp.concatenate([top, metal, bottom[SD:]], axis=0).T

    (r0, r1), (l0, l1) = column_blocks(mt)
    (sv_r, pv_r, film_r), (sv_l, pv_l, film_l) = flows(mt)
    wide = lanes(FZ)
    right_part = edge_part(r0, 0.0, 0.0, r1, 0.0, sv_r, pv_r, film_r)
    left_part = edge_part(l0, 0.0, 0.0, 0.0, l1, sv_l, pv_l, film_l)
    right_part = jnp.where(wide < FP, right_part, SPREAD)
    left_part = jnp.where(wide < FP, left_part, turn(SPREAD + ADVECT * sv_l, 64))

    def with_factors(block, p):
        block = jnp.where(wide == 96, turn(up_factor(p), 96), block)
        return jnp.where(wide == 97, turn(down_factor(p), 97 - (FP - 1)), block)

    r0, l0 = with_factors(r0, pv_r), with_factors(l0, pv_l)
    owner_row = turn(mt[50:51, :], 64)
    inside = lanes(1) < FP
    right_row, left_row = (jnp.where(inside, f, owner_row) for f in (film_r, film_l))
    head = jnp.concatenate([s[0:2], c[0:2], named[FP - 1 : FP], named[0:1]], axis=0)
    for peer in range(NB):
        ahead = (me + 1 == peer).astype(F32)
        behind = (me - 1 == peer).astype(F32)
        special = right_row * ahead + left_row * behind
        out[place(peer, ORDER0), 0:8, :] = jnp.concatenate([head, special, special], axis=0)
        out[place(peer, ORDER0), 8:16, :] = a0
        out[place(peer, ORDER0), 16:24, :] = h
        same = (me == peer).astype(F32)
        out[place(peer, ORDER0), 24:32, :] = r0 * ahead + l0 * behind + r0 * same
        out[place(peer, ORDER0), 32:40, :] = right_part * ahead + left_part * behind + l0 * same


def halo_columns(known_l, known_r, factor_l, factor_r, rows, mine_right, mine_left, walls, me):
    keep_l, keep_r = keeps(me)
    (film_l, own_l), (film_r, own_r) = rows
    top = subs(FZ) == 0
    wall_l, wall_r = pick_lane(own_l, walls, FS - 1), pick_lane(own_r, walls, 0)
    new_l = known_l + factor_l * mine_left + jnp.where(top, WALL * film_l * wall_l, 0.0)
    new_r = known_r + factor_r * mine_right + jnp.where(top, WALL * film_r * wall_r, 0.0)
    return new_l * keep_l, new_r * keep_r


def edge_rows(recv, me):
    return [(block[6:7], turn(block[6:7], 64)) for block in block_of(recv, me, 0)]


def first_kernel(
    recv, partial, toward, up, down, film, solid, cond, owner, first, second,
    fluid1, first_out, second_out, turned, side, tm,
):
    me = lax.axis_index("blk")
    lo, hi = sorted_rows(first, second)
    left, right = block_of(recv, me, 24)
    part_l, part_r = block_of(recv, me, 32)
    wall0, under0 = rows_of(recv, 0, ORDER0), rows_of(recv, 1, ORDER0)
    c0, c1 = rows_of(recv, 2, ORDER0), rows_of(recv, 3, ORDER0)
    a0, h = recv[0, 8:16, :], recv[0, 16:24, :]
    for j in range(1, NB):
        a0, h = a0 + recv[j, 8:16, :], h + recv[j, 16:24, :]
    wall1 = strip_row(wall0, conduct_of(c0, wall0), under0, conduct_of(c1, under0))
    wall1 = wall1 + SOLID_STEP * (a0 - h * wall0)

    here = place_of(me, ORDER0)
    mine_right, mine_left = recv[here, 24:32, :], recv[here, 32:40, :]
    new_l, new_r = halo_columns(
        part_l, part_r, turn(part_l, 64), turn(part_r, 64), edge_rows(recv, me),
        mine_right, mine_left, wall0, me,
    )
    tm[...] = jnp.zeros((FS, FS), F32)
    tm[pl.ds(0, FZ, stride=2), :] = right
    tm[pl.ds(1, FZ, stride=2), :] = left
    tm[16:24, :] = left
    tm[24:32, :] = right
    tm[pl.ds(32, FZ, stride=2), :] = new_r
    tm[pl.ds(33, FZ, stride=2), :] = new_l
    turned[...] = tm[...].T
    named = owner[...]
    walls0, walls1 = pick(named, wall0), pick(named, wall1)
    factors = (toward, up, down)
    columns = turned[:FP, :]
    complete(partial, fluid1, lo(0, 8), hi(0, 8), columns, factors, film[...], walls0)
    flux = film[...] * (fluid1[0] - walls1)
    (shares,) = by_owner(named, [flux])

    keep_l, keep_r = keeps(me)
    keep = jnp.where(lanes(8) >= FS // 2, keep_l, keep_r)
    halo, c_halo = metal_halo(turned, 8)
    own, halo = metal_step(solid[0:8, :], halo, cond[0:8, :], c_halo, keep)
    own, halo = set_walls(own, halo, wall1, me, keep)
    own, _ = metal_step(own, halo, cond[0:8, :], c_halo, keep)
    shares = SOLID_STEP * shares + jnp.where(subs(NB) == me, own[0:1], 0.0)
    side[0:8, :], side[8:16, :], side[16:24, :] = wall1, shares, h

    lane = lanes(FZ)

    def corners(at, beside, factor):
        out = jnp.zeros((FZ, FS), F32)
        for i, (old, new) in enumerate(((left, new_l), (right, new_r))):
            for k, (source, lane_of) in enumerate(
                ((old, at), (new, at), (old, factor), (new, beside))
            ):
                out = jnp.where(lane == 4 * i + k, turn(source, 4 * i + k - lane_of), out)
        return out

    blank = jnp.zeros((6, FS), F32)
    for i in range(3):
        send_rows(first_out, second_out, 8 * i, fluid1[:, FP - 3 + i, :], fluid1[:, 2 - i, :])
    send_rows(first_out, second_out, 24, corners(FP - 1, FP - 2, 97), corners(0, 1, 96))
    ids_last, ids_first = rows_of(recv, 4, ORDER0), rows_of(recv, 5, ORDER0)
    send_rows(first_out, second_out, 32, pick(ids_last, shares), pick(ids_first, shares))
    send_rows(
        first_out, second_out, 40,
        jnp.concatenate([flux[FP - 2 : FP], blank], axis=0),
        jnp.concatenate([flux[1:2], flux[0:1], blank], axis=0),
    )


def sums_kernel(
    fluid1, turned, side, toward, up, down, film, solid, cond, owner,
    fluid2, mt, sums, metal,
):
    me = lax.axis_index("blk")
    lane, sub = lanes(FP), subs(FP)
    named, f = owner[...], film[...]
    wall1 = side[0:8, :]
    none = jnp.zeros((FZ, FS), F32)
    factors = (toward, up, down)
    advance(fluid1, fluid2, none, none, turned[:FP, :], 32, factors, f, pick(named, wall1))
    x = fluid2[0]
    low, high = turn(x, 1, 0), turn(x, -1, 0)
    before = jnp.where(lane == 0, 0.0, turn(x, 1))
    after = jnp.where(lane == FS - 1, 0.0, turn(x, -1))
    moved = factored(
        x, low, high, before, after, x, fluid2[1], toward[0], up[0], down[0]
    ) - WALL * f * x
    within = jnp.where((sub == 0) | (sub == FP - 1), 0.0, f)
    deep = jnp.where((sub < 2) | (sub >= FP - 2), 0.0, f)
    sums[0:8, :], sums[8:16, :], sums[16:24, :] = by_owner(
        named, [within * x, deep * moved, f * f]
    )
    whole = jnp.concatenate([gather_columns(fluid2, lane), jnp.zeros((FP, FS), F32)], axis=0)
    mt[...] = whole.T
    keep_l, keep_r = keeps(me)
    keep = jnp.where(lanes(SD) >= FS // 2, keep_l, keep_r)
    halo, c_halo = metal_halo(turned, SD)
    own, halo = metal_step(solid[...], halo, cond[...], c_halo, keep)
    own, halo = set_walls(own, halo, wall1, me, keep)
    own, halo = metal_step(own, halo, cond[...], c_halo, keep)
    metal[0:SD, :], metal[SD : 2 * SD, :], metal[2 * SD : 3 * SD, :] = own, halo, c_halo


def pack_kernel(
    recv, mt_old, mt, sums, metal, side, fluid1, fluid2, toward, up, down, film, owner,
    first, second, first1, second1, sent, out, edge,
):
    me = lax.axis_index("blk")
    lane, sub = lanes(FZ), subs(FZ)
    keep_l, keep_r = keeps(me)
    lo, hi = sorted_rows(first, second)
    lo1, hi1 = sorted_rows(first1, second1)
    left, right = block_of(recv, me, 24)

    def outside(rows, rows1, inner, near_l, near_r):
        far, mid, near = rows1(0, 8), rows1(8, 16), rows1(16, 24)
        corner = rows1(24, 32)

        def at(k, to):
            return turn(corner, to - k)

        def lane_at(x, of, to):
            return turn(x, to - of)

        old_l, old_r = at(0, 0), at(4, FS - 1)
        side_l = at(1, 0) + at(2, 0) * lane_at(left, near_l, 0)
        side_r = at(5, FS - 1) + at(6, FS - 1) * lane_at(right, near_r, FS - 1)
        return far, mid, near, (old_l, old_r), (side_l, side_r), (at(3, 0), at(7, FS - 1))

    def finish(rows, rows1, inner, own_partial, factor, near_lane, factor_lane, upward):
        far, mid, near, old, beside, beside2 = outside(rows, rows1, inner, near_lane, near_lane)
        sv2, sv1, pv2, pv1 = rows(8, 16), rows(16, 24), rows(24, 32), rows(32, 40)
        flux = rows1(40, 42)
        order = (mid, inner) if upward else (inner, mid)
        new1 = halo_row(near, *order, *beside, sv1, pv1, flux[1:2])
        order = (far, near) if upward else (near, far)
        new2 = halo_row(mid, *order, *beside2, sv2, pv2, flux[0:1])
        through_l = turn(left, -factor_lane) * old[0]
        through_r = turn(right, FS - 1 - factor_lane) * old[1]
        own = own_partial + factor * near
        toward_here = toward[:, 0 if upward else FP - 1, :]
        own = own + jnp.where(lane == 0, toward_here * through_l, 0.0)
        own = own + jnp.where(lane == FS - 1, SPREAD * through_r, 0.0)
        return new1, new2, own

    low1, low2, x_first = finish(
        lo, lo1, fluid1[:, 0, :], fluid2[:, 0, :], up[:, 0, :], 0, 96, True
    )
    high1, high2, x_last = finish(
        hi, hi1, fluid1[:, FP - 1, :], fluid2[:, FP - 1, :], down[:, FP - 1, :],
        FP - 1, 97, False,
    )

    (r0, r1), (l0, l1) = column_blocks(mt)

    def patched(block, column):
        block = jnp.where(lane == 0, turn(x_first, -column), block)
        return jnp.where(lane == FP - 1, turn(x_last, FP - 1 - column), block)

    r0, r1 = patched(r0, FS - 1), patched(r1, FS - 2)
    l0, l1 = patched(l0, 0), patched(l1, 1)
    (sv_r, pv_r, film_r), (sv_l, pv_l, film_l) = flows(mt_old)

    def ends(column):
        return turn(low1, -column), turn(high1, FP - 1 - column)

    right_part = edge_part(r0, *ends(FS - 1), r1, 0.0, sv_r, pv_r, film_r)
    left_part = edge_part(l0, *ends(0), 0.0, l1, sv_l, pv_l, film_l)

    def corner_row(column):
        rows = []
        for i, x in enumerate((low1, high1)):
            spread = jnp.broadcast_to(x[:, column : column + 1], (FZ, FS))
            rows.append(
                jnp.sum(jnp.where(lane == sub + 8 * i, spread, 0.0), axis=0, keepdims=True)
            )
        return rows[0] + rows[1]

    rows = (0, 1, FP - 2, FP - 1)

    def stack(parts):
        return jnp.concatenate(list(parts) + [jnp.zeros((4, FS), F32)], axis=0)

    layer = {r: fluid2[0, r : r + 1, :] for r in (1, 2, FP - 3, FP - 2)}
    layer[-1], layer[0], layer[FP - 1], layer[FP] = (
        low1[0:1], x_first[0:1], x_last[0:1], high1[0:1],
    )
    here = stack(layer[r] for r in rows)
    above = stack([x_first[1:2], fluid2[1, 1:2, :], fluid2[1, FP - 2 : FP - 1, :], x_last[1:2]])
    f4 = stack(film[r : r + 1, :] for r in rows)
    factors = [stack(part[0, r : r + 1, :] for r in rows) for part in (toward, up, down)]
    before = jnp.where(lane == 0, 0.0, turn(here, 1))
    after = jnp.where(lane == FS - 1, 0.0, turn(here, -1))
    moved = f4 * (
        factored(
            here, stack(layer[r - 1] for r in rows), stack(layer[r + 1] for r in rows),
            before, after, here, above, *factors,
        )
        - WALL * f4 * here
    )
    direct = f4 * here
    a2, b3, h2 = sums[0:8, :], sums[8:16, :], sums[16:24, :]
    for i, r in enumerate(rows):
        hit = owner[r : r + 1, :] == sub.astype(F32)
        b3 = b3 + jnp.where(hit, moved[i : i + 1], 0.0)
        if r in (0, FP - 1):
            a2 = a2 + jnp.where(hit, direct[i : i + 1], 0.0)
    (film_bl, own_bl), (film_br, own_br) = edge_rows(recv, me)
    _, part_r = block_of(recv, me, 32)
    inside = lane < FP

    def shared(own_row, term):
        hit = (jnp.broadcast_to(own_row, (NB, FS)) == sub.astype(F32)) & inside
        return jnp.sum(jnp.where(hit, term, 0.0), axis=1, keepdims=True)

    right_term = film_br * turn(part_r, 64)[0:1] * r0[0:1] * keep_r
    left_term = film_bl * SPREAD * l0[0:1] * keep_l
    b3 = b3 + jnp.where(lane == 0, shared(own_br, right_term), 0.0)
    b3 = b3 + jnp.where(lane == FS - 1, shared(own_bl, left_term), 0.0)

    right_corner, left_corner = corner_row(FS - 1), corner_row(0)
    to_right = jnp.where(inside, r0, turn(right_part, 64))
    to_left = jnp.where(inside, l0, turn(left_part, 64))
    relay_lo, relay_hi = lo1(32, 40), hi1(32, 40)
    blank = jnp.zeros((2, FS), F32)
    for peer in range(NB):
        ahead = (me + 1 == peer).astype(F32)
        behind = (me - 1 == peer).astype(F32)
        out[place(peer, ORDER1), 0:8, :] = jnp.concatenate(
            [
                metal[1:2, :],
                b3[peer : peer + 1],
                h2[peer : peer + 1],
                relay_lo[peer : peer + 1],
                relay_hi[peer : peer + 1],
                right_corner * ahead + left_corner * behind,
                blank,
            ],
            axis=0,
        )
        out[place(peer, ORDER1), 8:16, :] = side[8:16, :]
        out[place(peer, ORDER1), 16:24, :] = a2
        out[place(peer, ORDER1), 24:32, :] = to_right * ahead + to_left * behind
    kept = (
        low1, low2, high1, high2, r0, l0, x_first, x_last,
        lo(16, 24), lo(32, 40), hi(16, 24), hi(32, 40), lo(40, 48), hi(40, 48),
    )
    for i, value in enumerate(kept):
        edge[8 * i : 8 * i + 8, :] = value


def last_kernel(
    recv1, recv, edge, side, metal, fluid2, toward, up, down, film, cond, owner,
    fluid_out, solid_out,
    tm, fluid3,
):
    me = lax.axis_index("blk")
    lane, sub = lanes(FZ), subs(FZ)
    (
        low1, low2, high1, high2, mine_right, mine_left, x_first, x_last,
        sv_lo, pv_lo, sv_hi, pv_hi, film_lo, film_hi,
    ) = [edge[8 * i : 8 * i + 8, :] for i in range(14)]
    left, right = block_of(recv1, me, 24, ORDER1)
    corner_l, corner_r = (block[5:6] for block in block_of(recv1, me, 0, ORDER1))
    part_l, part_r = block_of(recv, me, 32)
    c0, c1, h = rows_of(recv, 2, ORDER0), rows_of(recv, 3, ORDER0), side[16:24, :]
    tail, wall2, a2 = recv1[0, 0:8, :], recv1[0, 8:16, :], recv1[0, 16:24, :]
    for j in range(1, NB):
        tail = tail + recv1[j, 0:8, :]
        wall2 = wall2 + recv1[j, 8:16, :]
        a2 = a2 + recv1[j, 16:24, :]
    under2 = rows_of(recv1, 0, ORDER1)
    wall3 = strip_row(wall2, conduct_of(c0, wall2), under2, conduct_of(c1, under2))
    wall3 = wall3 + SOLID_STEP * (a2 - h * wall2)
    inflow3 = tail[1:2] + WALL * tail[2:3] * row_of(wall2, me) - row_of(h * wall3, me)

    new_l, new_r = halo_columns(
        turn(left, 64), turn(right, 64), turn(part_l, 64), turn(part_r, 64),
        edge_rows(recv, me), mine_right, mine_left, wall2, me,
    )
    tm[...] = jnp.zeros((FS, FS), F32)
    tm[pl.ds(0, FZ, stride=2), :] = right
    tm[pl.ds(1, FZ, stride=2), :] = left
    tm[pl.ds(32, FZ, stride=2), :] = new_r
    tm[pl.ds(33, FZ, stride=2), :] = new_l
    columns = tm[...].T[:FP]

    def corner(row, which):
        spread = jnp.broadcast_to(row, (FZ, FS))
        return jnp.sum(jnp.where(lane == sub + 8 * which, spread, 0.0), axis=1, keepdims=True)

    new_low = halo_row(
        low1, low2, x_first, corner(corner_l, 0), corner(corner_r, 0), sv_lo, pv_lo,
        film_lo[0:1] * (low1[0:1] - tail[3:4]),
    )
    new_high = halo_row(
        high1, x_last, high2, corner(corner_l, 1), corner(corner_r, 1), sv_hi, pv_hi,
        film_hi[0:1] * (high1[0:1] - tail[4:5]),
    )
    named, f = owner[...], film[...]
    source = [
        set_row(set_row(fluid2[z], x_first[z : z + 1], 0), x_last[z : z + 1], 1)
        for z in range(FZ)
    ]
    factors = (toward, up, down)
    advance(source, fluid3, low1, high1, columns, 0, factors, f, pick(named, wall2))
    walls3 = pick(named, wall3)
    advance(fluid3, fluid_out, new_low, new_high, columns, 32, factors, f, walls3)

    keep_l, keep_r = keeps(me)
    keep = jnp.where(lanes(SD) >= FS // 2, keep_l, keep_r)
    own, halo, c_halo = metal[0:SD, :], metal[SD : 2 * SD, :], metal[2 * SD : 3 * SD, :]
    own, halo = set_walls(own, halo, wall2, me, keep)
    own, halo = metal_step(own, halo, cond[...], c_halo, keep)
    own, halo = set_walls(own, halo, wall3, me, keep)
    own, _ = metal_step(own, halo, cond[...], c_halo, keep)
    solid_out[...] = own + jnp.where(subs(SD) == 0, SOLID_STEP * inflow3, 0.0)


def shape(*dims):
    return jax.ShapeDtypeStruct(dims, F32)


VMEM = pl.BlockSpec(memory_space=pltpu.VMEM)
GRANT = 54 * 1024 * 1024
HBM = pl.BlockSpec(memory_space=pltpu.HBM)


def call(kernel, outs, args, name, scratch=(), far=0, limit=32 * 1024 * 1024):
    return pl.pallas_call(
        kernel,
        out_shape=outs,
        in_specs=[HBM] * far + [VMEM] * (len(args) - far),
        out_specs=jax.tree.map(lambda _: VMEM, outs),
        scratch_shapes=scratch,
        name=name,
        compiler_params=pltpu.CompilerParams(vmem_limit_bytes=limit),
    )(*args)


def both_ways(first, second):
    count = lax.axis_size("sec")
    near = [(i, i ^ 1) for i in range(count)]
    far = [(i, (i + 1 if i % 2 else i - 1) % count) for i in range(count)]
    second = lax.ppermute(second, "sec", far)
    return lax.ppermute(first, "sec", near), second


def swap(message, order):
    count = lax.axis_size("sec")
    groups = [[NB * s + k for k in order[2 * s >= count]] for s in range(count)]
    return lax.all_to_all(
        message, ("sec", "blk"), split_axis=0, concat_axis=0, tiled=True, axis_index_groups=groups
    )


def two_exchanges(fluid, sv, pv, film, solid, cond, face_owner):
    owner = face_owner.reshape(1, FP)
    solid, cond = solid.reshape(SD, FS), cond.reshape(SD, FS)
    field, rows = shape(FZ, FP, FS), shape(ROWS, FS)
    held = [pltpu.VMEM((FZ, FP, FS), F32)] * 3
    held += [pltpu.VMEM((n, FS), F32) for n in (FP, SD, SD)]
    message, first, second, mt, owner = call(
        open_kernel,
        (shape(NB, R0, FS), rows, rows, shape(FS, FS), shape(FP, FS)),
        (fluid, sv, pv, film, solid, cond, owner),
        "open",
        held + [pltpu.VMEM((1, FP), jnp.int32), pltpu.SemaphoreType.DMA((10,))],
        far=7,
        limit=GRANT - OPEN_ROOM,
    )
    first, second = both_ways(first, second)
    recv = swap(message, ORDER0)
    *factors, partial = call(
        prepare_kernel,
        (field,) * 4,
        (fluid, sv, pv, film),
        "prepare",
        [pltpu.VMEM((FZ, FP, FS), F32)] * 3 + [pltpu.SemaphoreType.DMA((3,))],
        far=3,
        limit=GRANT - PREPARE_ROOM,
    )
    fluid1, first_sent, second_sent, turned, side = call(
        first_kernel,
        (field, rows, rows, shape(FS, FS), shape(24, FS)),
        (recv, partial, *factors, film, solid, cond, owner, first, second),
        "first",
        [pltpu.VMEM((FS, FS), F32)],
    )
    first1, second1 = both_ways(first_sent, second_sent)
    fluid2, mt2, sums, metal = call(
        sums_kernel,
        (field, shape(FS, FS), shape(24, FS), shape(3 * SD, FS)),
        (fluid1, turned, side, *factors, film, solid, cond, owner),
        "sums",
    )
    message, edge = call(
        pack_kernel,
        (shape(NB, R1, FS), shape(14 * 8, FS)),
        (
            recv, mt, mt2, sums, metal, side, fluid1, fluid2, *factors, film, owner,
            first, second, first1, second1, first_sent,
        ),
        "pack",
    )
    recv1 = swap(message, ORDER1)
    fluid, solid = call(
        last_kernel,
        (field, shape(SD, FS)),
        (recv1, recv, edge, side, metal, fluid2, *factors, film, cond, owner),
        "last",
        [pltpu.VMEM((FS, FS), F32), pltpu.VMEM((FZ, FP, FS), F32)],
    )
    return fluid, solid.reshape(1, SD, FS)


def padded(block, sides, width, periodic):
    for axis, dim in sides:
        count = lax.axis_size(axis)
        forward = [(i, i + 1) for i in range(count - 1)]
        if periodic:
            forward.append((count - 1, 0))
        backward = [(target, source) for source, target in forward]
        low = lax.ppermute(
            lax.slice_in_dim(block, block.shape[dim] - width, None, axis=dim), axis, forward
        )
        high = lax.ppermute(lax.slice_in_dim(block, 0, width, axis=dim), axis, backward)
        block = jnp.concatenate([low, block, high], axis=dim)
    return block


def fluid_update(
    fluid, stream_velocity, pitch_velocity, wall_flux, pitch_extended, stream_extended
):
    pitch_prev = pitch_extended[:, :-2]
    pitch_next = pitch_extended[:, 2:]
    stream_prev = stream_extended[:, :, :-2]
    stream_next = stream_extended[:, :, 2:]
    span_prev = jnp.concatenate([fluid[:1], fluid[:-1]], 0)
    span_next = jnp.concatenate([fluid[1:], fluid[-1:]], 0)
    spread = SPREAD * (
        pitch_prev + pitch_next + stream_prev + stream_next + span_prev + span_next - 6.0 * fluid
    )
    carried = (
        -ADVECT * stream_velocity * (fluid - stream_prev)
        - ADVECT * jnp.maximum(pitch_velocity, 0.0) * (fluid - pitch_prev)
        + ADVECT * jnp.maximum(-pitch_velocity, 0.0) * (pitch_next - fluid)
    )
    updated = fluid + spread + carried
    return updated.at[0].add(-WALL * wall_flux)


def solid_update(solid, conduct, inflow, solid_extended, conduct_extended):
    stream_prev = solid_extended[..., :-2]
    stream_next = solid_extended[..., 2:]
    conduct_prev = conduct_extended[..., :-2]
    conduct_next = conduct_extended[..., 2:]
    depth_prev = jnp.concatenate([solid[:, :1], solid[:, :-1]], 1)
    depth_next = jnp.concatenate([solid[:, 1:], solid[:, -1:]], 1)
    kdepth_prev = jnp.concatenate([conduct[:, :1], conduct[:, :-1]], 1)
    kdepth_next = jnp.concatenate([conduct[:, 1:], conduct[:, -1:]], 1)
    flow = (
        0.5 * (conduct + conduct_prev) * (stream_prev - solid)
        + 0.5 * (conduct + conduct_next) * (stream_next - solid)
        + 0.5 * (conduct + kdepth_prev) * (depth_prev - solid)
        + 0.5 * (conduct + kdepth_next) * (depth_next - solid)
    )
    updated = solid + SOLID_STEP * flow
    updated = updated.at[:, 0].add(SOLID_STEP * inflow)
    updated = updated.at[:, -1].add(SOLID_STEP * COOLING * (COOLANT - solid[:, -1]))
    return updated


def local(
    fluid_temp, stream_velocity, pitch_velocity, film_coeff, solid_temp, conductivity, face_owner
):
    span_cells, pitch_cells, stream_cells = fluid_temp.shape
    depth_cells = solid_temp.shape[1]
    block_count = lax.axis_size("blk")
    capacity = max(2, (pitch_cells + block_count - 1) // block_count)
    owners = face_owner.reshape(-1)
    onehot = (owners[:, None] == jnp.arange(block_count, dtype=jnp.int32)[None, :]).astype(
        jnp.float32
    )
    same_owner = owners[:, None] == owners[None, :]
    earlier = lax.broadcasted_iota(jnp.int32, (pitch_cells, pitch_cells), 0) < lax.broadcasted_iota(
        jnp.int32, (pitch_cells, pitch_cells), 1
    )
    slot_rank = jnp.sum((same_owner & earlier).astype(jnp.int32), axis=0)
    slot_table = (slot_rank[None, :] == jnp.arange(capacity, dtype=jnp.int32)[:, None]).astype(
        jnp.float32
    )
    placing = onehot.T[:, None, :] * slot_table[None, :, :]
    fluid = fluid_temp
    solid = solid_temp
    gas_rows = span_cells * pitch_cells
    for subiter in range(SUB):
        wall_row = solid[0, 0:1, :]
        wall_temp = jnp.dot(
            onehot,
            lax.all_gather(wall_row, "blk", axis=0, tiled=True),
            precision=lax.Precision.HIGHEST,
            preferred_element_type=jnp.float32,
        )
        flux = film_coeff * (fluid[0] - wall_temp)
        outgoing = jnp.einsum("ocb,bf->ocf", placing, flux, precision=lax.Precision.HIGHEST)
        received = lax.all_to_all(outgoing, "blk", split_axis=0, concat_axis=0, tiled=True)
        inflow = jnp.sum(received, axis=(0, 1))
        conduct = conductivity * (1.0 + 0.25 * jnp.tanh(solid))
        stacked = jnp.concatenate([fluid.reshape(gas_rows, stream_cells), solid[0], conduct[0]], 0)
        stream_ext = padded(stacked, (("blk", 1),), 1, False)
        pitch_extended = padded(fluid, (("sec", 1),), 1, True)
        fluid_stream = stream_ext[:gas_rows].reshape(span_cells, pitch_cells, stream_cells + 2)
        solid_stream = stream_ext[gas_rows : gas_rows + depth_cells][None]
        conduct_stream = stream_ext[gas_rows + depth_cells :][None]
        fluid = fluid_update(
            fluid, stream_velocity, pitch_velocity, flux, pitch_extended, fluid_stream
        )
        solid = solid_update(solid, conduct, inflow[None, :], solid_stream, conduct_stream)
    return (fluid, solid)


def solution(mesh):
    placed = (
        P(None, "sec", "blk"),
        P(None, "sec", "blk"),
        P(None, "sec", "blk"),
        P("sec", "blk"),
        P("sec", None, "blk"),
        P("sec", None, "blk"),
        P("sec", "blk", None, None),
    )
    sizes = dict(mesh.shape)

    def chosen(*args):
        fits = args[0].shape == (FZ, FP, FS) and args[4].shape == (1, SD, FS)
        fits = fits and sizes["blk"] == NB and sizes["sec"] % 2 == 0
        return two_exchanges(*args) if fits else local(*args)

    return jax.shard_map(
        chosen,
        mesh=mesh,
        in_specs=placed,
        out_specs=(P(None, "sec", "blk"), P("sec", None, "blk")),
        check_vma=False,
    )
```

```python
import jax
import jax.numpy as jnp
from jax import lax
from jax.experimental import pallas as pl
from jax.experimental.pallas import tpu as pltpu
from jax.sharding import PartitionSpec as P

SUB = 4


ADVECT = 0.4
SPREAD = 0.04
WALL = 0.4
SOLID_STEP = 0.04
COOLING = 0.5
COOLANT = -1.0

F32 = jnp.float32
NB = 8
FZ = 8
FP = 64
FS = 128
SD = 32
R0 = 40
R1 = 32
ROWS = 48
OPEN_ROOM = 56 * 1024
PREPARE_ROOM = 1400 * 1024
ORDER0 = ((5, 0, 1, 2, 6, 3, 4, 7), (4, 1, 0, 3, 7, 2, 5, 6))
ORDER1 = ((5, 2, 6, 4, 1, 0, 7, 3),) * 2


def lanes(rows):
    return lax.broadcasted_iota(jnp.int32, (rows, FS), 1)


def subs(rows):
    return lax.broadcasted_iota(jnp.int32, (rows, FS), 0)


def turn(x, shift, axis=1):
    return pltpu.roll(x, shift % x.shape[axis], axis)


def by_owner(owner, values):
    sub = subs(NB)
    outs = [jnp.zeros((NB, FS), F32) for _ in values]
    for o in range(NB):
        mine = owner == o
        for i, value in enumerate(values):
            total = jnp.sum(jnp.where(mine, value, 0.0), axis=0, keepdims=True)
            outs[i] = jnp.where(sub == o, total, outs[i])
    return outs


def pick(owner, table):
    out = jnp.zeros(owner.shape, F32)
    for o in range(NB):
        out = jnp.where(owner == o, table[o : o + 1], out)
    return out


def pick_lane(owner_row, table, lane):
    column = jnp.broadcast_to(table[:, lane : lane + 1], (NB, FS))
    named = jnp.broadcast_to(owner_row, (NB, FS)) == subs(NB).astype(F32)
    return jnp.sum(jnp.where(named, column, 0.0), axis=0, keepdims=True)


def stencil(x, low, high, left, right, below, above, sv, pv):
    spread = SPREAD * (low + high + left + right + below + above - 6.0 * x)
    carried = (
        -ADVECT * sv * (x - left)
        - ADVECT * jnp.maximum(pv, 0.0) * (x - low)
        + ADVECT * jnp.maximum(-pv, 0.0) * (high - x)
    )
    return x + spread + carried


def factored(x, low, high, left, right, below, above, toward, up, down):
    new = (1.0 - 3.0 * SPREAD) * x + SPREAD * (right + below + above)
    return new + toward * (left - x) + up * (low - x) + down * (high - x)


def span(x):
    sub = subs(FZ)
    below = jnp.where(sub == 0, x, turn(x, 1, 0))
    above = jnp.where(sub == FZ - 1, x, turn(x, FZ - 1, 0))
    return below, above


def halo_row(x, low, high, left_corner, right_corner, sv, pv, flux):
    lane = lanes(FZ)
    left = jnp.where(lane == 0, left_corner, turn(x, 1))
    right = jnp.where(lane == FS - 1, right_corner, turn(x, -1))
    below, above = span(x)
    new = stencil(x, low, high, left, right, below, above, sv, pv)
    return new - jnp.where(subs(FZ) == 0, WALL * flux, 0.0)


def edge_part(x, low_end, high_end, left, right, sv, pv, film):
    lane = lanes(FZ)
    low = jnp.where(lane == 0, low_end, turn(x, 1))
    high = jnp.where(lane == FP - 1, high_end, turn(x, -1))
    below, above = span(x)
    new = stencil(x, low, high, left, right, below, above, sv, pv)
    return new - jnp.where(subs(FZ) == 0, WALL * film * x, 0.0)


def set_row(x, row, at):
    if at == 0:
        return jnp.concatenate([jnp.where(subs(8) == 0, row, x[:8]), x[8:]], axis=0)
    return jnp.concatenate([x[:-8], jnp.where(subs(8) == 7, row, x[-8:])], axis=0)


def advance(src, dst, low_row, high_row, columns, base, factors, film, wall):
    lane = lanes(FP)
    toward, up, down = factors
    for z in range(FZ):
        x = src[z]
        low = set_row(turn(x, 1, 0), low_row[z : z + 1], 0)
        high = set_row(turn(x, -1, 0), high_row[z : z + 1], 1)
        edge = turn(columns, -(base + 2 * z + 1))
        left = jnp.where(lane == 0, edge, turn(x, 1))
        right = jnp.where(lane == FS - 1, edge, turn(x, -1))
        below, above = src[max(z - 1, 0)], src[min(z + 1, FZ - 1)]
        new = factored(x, low, high, left, right, below, above, toward[z], up[z], down[z])
        if z == 0:
            new = new - WALL * film * (x - wall)
        dst[z] = new


def prepare_kernel(fluid_in, sv_in, pv_in, film, toward, up, down, partial, fluid, sv, pv, sems):
    started = fetch([(fluid_in, fluid), (sv_in, sv), (pv_in, pv)], sems)
    for copy in started:
        copy.wait()
    for z in range(FZ):
        toward[z] = SPREAD + ADVECT * sv[z]
        up[z] = up_factor(pv[z])
        down[z] = down_factor(pv[z])
    none = jnp.zeros((FZ, FS), F32)
    columns = jnp.zeros((FP, FS), F32)
    advance(fluid, partial, none, none, columns, 0, (toward, up, down), film[...], 0.0)


def complete(partial, dst, low_row, high_row, columns, factors, film, wall):
    lane = lanes(FP)
    toward, up, down = factors
    for z in range(FZ):
        edge = turn(columns, -(2 * z + 1))
        gain = jnp.where(lane == 0, toward[z], jnp.where(lane == FS - 1, SPREAD, 0.0))
        new = partial[z] + gain * edge
        if z == 0:
            new = new + WALL * film * wall
        first = new[:8] + jnp.where(subs(8) == 0, up[z, :8, :] * low_row[z : z + 1], 0.0)
        last = new[-8:] + jnp.where(subs(8) == 7, down[z, FP - 8 :, :] * high_row[z : z + 1], 0.0)
        dst[z] = jnp.concatenate([first, new[8:-8], last], axis=0)


def strip_row(here, k_here, under, k_under):
    sub, lane = subs(NB), lanes(NB)

    def prev(x):
        moved = turn(x, 1)
        carried = jnp.where(sub == 0, 0.0, turn(moved, 1, 0))
        return jnp.where(lane == 0, carried, moved)

    def following(x):
        moved = turn(x, -1)
        carried = jnp.where(sub == NB - 1, 0.0, turn(moved, -1, 0))
        return jnp.where(lane == FS - 1, carried, moved)

    flow = (
        0.5 * (k_here + prev(k_here)) * (prev(here) - here)
        + 0.5 * (k_here + following(k_here)) * (following(here) - here)
        + 0.5 * (k_here + k_under) * (under - here)
    )
    return here + SOLID_STEP * flow


def conduct_of(conductivity, solid):
    return conductivity * (1.0 + 0.25 * jnp.tanh(solid))


def metal_step(own, halo, c_own, c_halo, keep):
    depth_cells = own.shape[0]
    k_own, k_halo = conduct_of(c_own, own), conduct_of(c_halo, halo)
    lane, sub = lanes(depth_cells), subs(depth_cells)

    def depth(x):
        up = jnp.where(sub == 0, x, turn(x, 1, 0))
        down = jnp.where(sub == depth_cells - 1, x, turn(x, -1, 0))
        return up, down

    def stream(x, other):
        prev = jnp.where(lane == 0, turn(other, 1), turn(x, 1))
        following = jnp.where(lane == FS - 1, turn(other, -1), turn(x, -1))
        return prev, following

    def update(x, k, other, k_other):
        flow = jnp.zeros_like(x)
        for a, ka in zip(stream(x, other) + depth(x), stream(k, k_other) + depth(k)):
            flow = flow + 0.5 * (k + ka) * (a - x)
        new = x + SOLID_STEP * flow
        return new + jnp.where(sub == SD - 1, SOLID_STEP * COOLING * (COOLANT - x), 0.0)

    return update(own, k_own, halo, k_halo), update(halo, k_halo, own, k_own) * keep


def row_of(table, index):
    return jnp.sum(jnp.where(subs(NB) == index, table, 0.0), axis=0, keepdims=True)


def set_walls(own, halo, walls, me, keep):
    sub, lane = subs(own.shape[0]), lanes(own.shape[0])
    beside = jnp.where(lane >= FS // 2, row_of(walls, me - 1), row_of(walls, me + 1)) * keep
    return jnp.where(sub == 0, row_of(walls, me), own), jnp.where(sub == 0, beside, halo)


def metal_halo(turned, rows):
    deep = turned[FP : FP + rows]
    lane = lanes(rows)

    def placed(left, right):
        return jnp.where(
            lane >= 124, turn(deep, left), jnp.where(lane < 4, turn(deep, right), 0.0)
        )

    return placed(108, 104), placed(104, 100)


def place(peer, order):
    lower, upper = order[0].index(peer), order[1].index(peer)
    if lower == upper:
        return lower
    return jnp.where(2 * lax.axis_index("sec") >= lax.axis_size("sec"), upper, lower)


def place_of(peer, order):
    return sum(jnp.where(peer == k, place(k, order), 0) for k in range(NB))


def rows_of(recv, row, order):
    return jnp.concatenate([recv[place(k, order), row : row + 1, :] for k in range(NB)], axis=0)


def keeps(me):
    return (me > 0).astype(F32), (me < NB - 1).astype(F32)


def block_of(recv, me, start, order=ORDER0):
    keep_l, keep_r = keeps(me)
    before = place_of(jnp.maximum(me - 1, 0), order)
    after = place_of(jnp.minimum(me + 1, NB - 1), order)
    part = slice(start, start + 8)
    return recv[before, part, :] * keep_l, recv[after, part, :] * keep_r


def column_blocks(mt):
    right = mt[pl.ds(1, FZ, stride=4), :], mt[pl.ds(0, FZ, stride=4), :]
    left = mt[pl.ds(2, FZ, stride=4), :], mt[pl.ds(3, FZ, stride=4), :]
    return right, left


def flows(mt):
    right, left = mt[pl.ds(32, FZ, stride=2), :], mt[pl.ds(33, FZ, stride=2), :]
    return (turn(right, 64), right, mt[48:49, :]), (turn(left, 64), left, mt[49:50, :])


def gather_columns(fluid, lane):
    acc = jnp.zeros((FP, FS), F32)
    for z in range(FZ):
        acc = jnp.where(lane // 4 == z, turn(fluid[z], 4 * z + 2), acc)
    return acc


def sorted_rows(first, second):
    even = lax.axis_index("sec") % 2 == 0
    return (
        lambda a, b: jnp.where(even, second[a:b, :], first[a:b, :]),
        lambda a, b: jnp.where(even, first[a:b, :], second[a:b, :]),
    )


def send_rows(first, second, start, up, down):
    even = lax.axis_index("sec") % 2 == 0
    part = slice(start, start + up.shape[0])
    first[part, :] = jnp.where(even, up, down)
    second[part, :] = jnp.where(even, down, up)


def up_factor(pv):
    return SPREAD + ADVECT * jnp.maximum(pv, 0.0)


def down_factor(pv):
    return SPREAD + ADVECT * jnp.maximum(-pv, 0.0)


def fetch(copies, sems):
    started = [
        pltpu.make_async_copy(src, dst, sems.at[i]) for i, (src, dst) in enumerate(copies)
    ]
    for copy in started:
        copy.start()
    return started


def open_kernel(
    fluid_in, sv_in, pv_in, film_in, solid_in, cond_in, owner,
    out, first, second, mt, names, fluid, sv, pv, film, solid, cond, ids, sems,
):
    me = lax.axis_index("blk")
    half = FZ // 2
    copies = [(owner, ids), (film_in, film), (solid_in, solid), (cond_in, cond)]
    copies += [(fluid_in, fluid), (pv_in, pv), (sv_in, sv)]
    started = fetch(copies, sems)
    lane = lanes(FP)
    for copy in started[:4]:
        copy.wait()
    ids_row = jnp.concatenate([ids[...].astype(F32), jnp.zeros((1, FS - FP), F32)], axis=1)
    named = jnp.broadcast_to(ids_row, (FS, FS)).T[:FP]
    names[...] = named
    metal = jnp.zeros((SD, FS), F32)
    thin = lanes(SD)
    s, c = solid[...], cond[...]
    for k in range(4):
        metal = jnp.where(thin == 4 * k + 1, turn(s, 3 * k + 5), metal)
        metal = jnp.where(thin == 4 * k + 2, turn(s, 3 * k + 2), metal)
        metal = jnp.where(thin == 4 * k + 17, turn(c, 3 * k + 21), metal)
        metal = jnp.where(thin == 4 * k + 18, turn(c, 3 * k + 18), metal)
    started[4].wait()
    a0, h = by_owner(named, [film[...] * fluid[0], film[...]])
    top = gather_columns(fluid, lane)
    send_rows(first, second, 0, fluid[:, FP - 1, :], fluid[:, 0, :])
    blank = jnp.zeros((7, FS), F32)
    send_rows(
        first, second, 40,
        jnp.concatenate([film[FP - 1 : FP, :], blank], axis=0),
        jnp.concatenate([film[0:1, :], blank], axis=0),
    )
    for copy in started[5:]:
        copy.wait()
    bottom = jnp.zeros((FP, FS), F32)
    pair = (lane - 32) // 2
    for z in range(FZ):
        here = (pair == z) & (lane >= 32)
        top = jnp.where(here, turn(pv[z], 33 + 2 * z), top)
        bottom = jnp.where(here, turn(sv[z], 33 + 2 * z), bottom)
    send_rows(first, second, 8, sv[:, FP - 2, :], sv[:, 1, :])
    send_rows(first, second, 16, sv[:, FP - 1, :], sv[:, 0, :])
    send_rows(first, second, 24, pv[:, FP - 2, :], pv[:, 1, :])
    send_rows(first, second, 32, pv[:, FP - 1, :], pv[:, 0, :])
    top = jnp.where(lane // 2 == 24, turn(film[...], 49), top)
    top = jnp.where(lane == 50, named, top)
    metal = jnp.where(thin < 32, metal, bottom[:SD])
    mt[...] = jnp.concatenate([top, metal, bottom[SD:]], axis=0).T

    (r0, r1), (l0, l1) = column_blocks(mt)
    (sv_r, pv_r, film_r), (sv_l, pv_l, film_l) = flows(mt)
    wide = lanes(FZ)
    right_part = edge_part(r0, 0.0, 0.0, r1, 0.0, sv_r, pv_r, film_r)
    left_part = edge_part(l0, 0.0, 0.0, 0.0, l1, sv_l, pv_l, film_l)
    right_part = jnp.where(wide < FP, right_part, SPREAD)
    left_part = jnp.where(wide < FP, left_part, turn(SPREAD + ADVECT * sv_l, 64))

    def with_factors(block, p):
        block = jnp.where(wide == 96, turn(up_factor(p), 96), block)
        return jnp.where(wide == 97, turn(down_factor(p), 97 - (FP - 1)), block)

    r0, l0 = with_factors(r0, pv_r), with_factors(l0, pv_l)
    owner_row = turn(mt[50:51, :], 64)
    inside = lanes(1) < FP
    right_row, left_row = (jnp.where(inside, f, owner_row) for f in (film_r, film_l))
    head = jnp.concatenate([s[0:2], c[0:2], named[FP - 1 : FP], named[0:1]], axis=0)
    for peer in range(NB):
        ahead = (me + 1 == peer).astype(F32)
        behind = (me - 1 == peer).astype(F32)
        special = right_row * ahead + left_row * behind
        out[place(peer, ORDER0), 0:8, :] = jnp.concatenate([head, special, special], axis=0)
        out[place(peer, ORDER0), 8:16, :] = a0
        out[place(peer, ORDER0), 16:24, :] = h
        same = (me == peer).astype(F32)
        out[place(peer, ORDER0), 24:32, :] = r0 * ahead + l0 * behind + r0 * same
        out[place(peer, ORDER0), 32:40, :] = right_part * ahead + left_part * behind + l0 * same


def halo_columns(known_l, known_r, factor_l, factor_r, rows, mine_right, mine_left, walls, me):
    keep_l, keep_r = keeps(me)
    (film_l, own_l), (film_r, own_r) = rows
    top = subs(FZ) == 0
    wall_l, wall_r = pick_lane(own_l, walls, FS - 1), pick_lane(own_r, walls, 0)
    new_l = known_l + factor_l * mine_left + jnp.where(top, WALL * film_l * wall_l, 0.0)
    new_r = known_r + factor_r * mine_right + jnp.where(top, WALL * film_r * wall_r, 0.0)
    return new_l * keep_l, new_r * keep_r


def edge_rows(recv, me):
    return [(block[6:7], turn(block[6:7], 64)) for block in block_of(recv, me, 0)]


def first_kernel(
    recv, partial, toward, up, down, film, solid, cond, owner, first, second, sent,
    fluid1, first_out, second_out, turned, side, tm,
):
    me = lax.axis_index("blk")
    lo, hi = sorted_rows(first, second)
    left, right = block_of(recv, me, 24)
    part_l, part_r = block_of(recv, me, 32)
    wall0, under0 = rows_of(recv, 0, ORDER0), rows_of(recv, 1, ORDER0)
    c0, c1 = rows_of(recv, 2, ORDER0), rows_of(recv, 3, ORDER0)
    a0, h = recv[0, 8:16, :], recv[0, 16:24, :]
    for j in range(1, NB):
        a0, h = a0 + recv[j, 8:16, :], h + recv[j, 16:24, :]
    wall1 = strip_row(wall0, conduct_of(c0, wall0), under0, conduct_of(c1, under0))
    wall1 = wall1 + SOLID_STEP * (a0 - h * wall0)

    here = place_of(me, ORDER0)
    mine_right, mine_left = recv[here, 24:32, :], recv[here, 32:40, :]
    new_l, new_r = halo_columns(
        part_l, part_r, turn(part_l, 64), turn(part_r, 64), edge_rows(recv, me),
        mine_right, mine_left, wall0, me,
    )
    tm[...] = jnp.zeros((FS, FS), F32)
    tm[pl.ds(0, FZ, stride=2), :] = right
    tm[pl.ds(1, FZ, stride=2), :] = left
    tm[16:24, :] = left
    tm[24:32, :] = right
    tm[pl.ds(32, FZ, stride=2), :] = new_r
    tm[pl.ds(33, FZ, stride=2), :] = new_l
    turned[...] = tm[...].T
    named = owner[...]
    walls0, walls1 = pick(named, wall0), pick(named, wall1)
    factors = (toward, up, down)
    columns = turned[:FP, :]
    complete(partial, fluid1, lo(0, 8), hi(0, 8), columns, factors, film[...], walls0)
    flux = film[...] * (fluid1[0] - walls1)
    (shares,) = by_owner(named, [flux])

    keep_l, keep_r = keeps(me)
    keep = jnp.where(lanes(8) >= FS // 2, keep_l, keep_r)
    halo, c_halo = metal_halo(turned, 8)
    own, halo = metal_step(solid[0:8, :], halo, cond[0:8, :], c_halo, keep)
    own, halo = set_walls(own, halo, wall1, me, keep)
    own, _ = metal_step(own, halo, cond[0:8, :], c_halo, keep)
    shares = SOLID_STEP * shares + jnp.where(subs(NB) == me, own[0:1], 0.0)
    side[0:8, :], side[8:16, :], side[16:24, :] = wall1, shares, h

    lane = lanes(FZ)

    def corners(at, beside, factor):
        out = jnp.zeros((FZ, FS), F32)
        for i, (old, new) in enumerate(((left, new_l), (right, new_r))):
            for k, (source, lane_of) in enumerate(
                ((old, at), (new, at), (old, factor), (new, beside))
            ):
                out = jnp.where(lane == 4 * i + k, turn(source, 4 * i + k - lane_of), out)
        return out

    blank = jnp.zeros((6, FS), F32)
    for i in range(3):
        send_rows(first_out, second_out, 8 * i, fluid1[:, FP - 3 + i, :], fluid1[:, 2 - i, :])
    send_rows(first_out, second_out, 24, corners(FP - 1, FP - 2, 97), corners(0, 1, 96))
    ids_last, ids_first = rows_of(recv, 4, ORDER0), rows_of(recv, 5, ORDER0)
    send_rows(first_out, second_out, 32, pick(ids_last, shares), pick(ids_first, shares))
    send_rows(
        first_out, second_out, 40,
        jnp.concatenate([flux[FP - 2 : FP], blank], axis=0),
        jnp.concatenate([flux[1:2], flux[0:1], blank], axis=0),
    )


def sums_kernel(
    fluid1, turned, side, toward, up, down, film, solid, cond, owner,
    fluid2, mt, sums, metal,
):
    me = lax.axis_index("blk")
    lane, sub = lanes(FP), subs(FP)
    named, f = owner[...], film[...]
    wall1 = side[0:8, :]
    none = jnp.zeros((FZ, FS), F32)
    factors = (toward, up, down)
    advance(fluid1, fluid2, none, none, turned[:FP, :], 32, factors, f, pick(named, wall1))
    x = fluid2[0]
    low, high = turn(x, 1, 0), turn(x, -1, 0)
    before = jnp.where(lane == 0, 0.0, turn(x, 1))
    after = jnp.where(lane == FS - 1, 0.0, turn(x, -1))
    moved = factored(
        x, low, high, before, after, x, fluid2[1], toward[0], up[0], down[0]
    ) - WALL * f * x
    within = jnp.where((sub == 0) | (sub == FP - 1), 0.0, f)
    deep = jnp.where((sub < 2) | (sub >= FP - 2), 0.0, f)
    sums[0:8, :], sums[8:16, :], sums[16:24, :] = by_owner(
        named, [within * x, deep * moved, f * f]
    )
    whole = jnp.concatenate([gather_columns(fluid2, lane), jnp.zeros((FP, FS), F32)], axis=0)
    mt[...] = whole.T
    keep_l, keep_r = keeps(me)
    keep = jnp.where(lanes(SD) >= FS // 2, keep_l, keep_r)
    halo, c_halo = metal_halo(turned, SD)
    own, halo = metal_step(solid[...], halo, cond[...], c_halo, keep)
    own, halo = set_walls(own, halo, wall1, me, keep)
    own, halo = metal_step(own, halo, cond[...], c_halo, keep)
    metal[0:SD, :], metal[SD : 2 * SD, :], metal[2 * SD : 3 * SD, :] = own, halo, c_halo


def pack_kernel(
    recv, mt_old, mt, sums, metal, side, fluid1, fluid2, toward, up, down, film, owner,
    first, second, first1, second1, sent, out, edge,
):
    me = lax.axis_index("blk")
    lane, sub = lanes(FZ), subs(FZ)
    keep_l, keep_r = keeps(me)
    lo, hi = sorted_rows(first, second)
    lo1, hi1 = sorted_rows(first1, second1)
    left, right = block_of(recv, me, 24)

    def outside(rows, rows1, inner, near_l, near_r):
        far, mid, near = rows1(0, 8), rows1(8, 16), rows1(16, 24)
        corner = rows1(24, 32)

        def at(k, to):
            return turn(corner, to - k)

        def lane_at(x, of, to):
            return turn(x, to - of)

        old_l, old_r = at(0, 0), at(4, FS - 1)
        side_l = at(1, 0) + at(2, 0) * lane_at(left, near_l, 0)
        side_r = at(5, FS - 1) + at(6, FS - 1) * lane_at(right, near_r, FS - 1)
        return far, mid, near, (old_l, old_r), (side_l, side_r), (at(3, 0), at(7, FS - 1))

    def finish(rows, rows1, inner, own_partial, factor, near_lane, factor_lane, upward):
        far, mid, near, old, beside, beside2 = outside(rows, rows1, inner, near_lane, near_lane)
        sv2, sv1, pv2, pv1 = rows(8, 16), rows(16, 24), rows(24, 32), rows(32, 40)
        flux = rows1(40, 42)
        order = (mid, inner) if upward else (inner, mid)
        new1 = halo_row(near, *order, *beside, sv1, pv1, flux[1:2])
        order = (far, near) if upward else (near, far)
        new2 = halo_row(mid, *order, *beside2, sv2, pv2, flux[0:1])
        through_l = turn(left, -factor_lane) * old[0]
        through_r = turn(right, FS - 1 - factor_lane) * old[1]
        own = own_partial + factor * near
        toward_here = toward[:, 0 if upward else FP - 1, :]
        own = own + jnp.where(lane == 0, toward_here * through_l, 0.0)
        own = own + jnp.where(lane == FS - 1, SPREAD * through_r, 0.0)
        return new1, new2, own

    low1, low2, x_first = finish(
        lo, lo1, fluid1[:, 0, :], fluid2[:, 0, :], up[:, 0, :], 0, 96, True
    )
    high1, high2, x_last = finish(
        hi, hi1, fluid1[:, FP - 1, :], fluid2[:, FP - 1, :], down[:, FP - 1, :],
        FP - 1, 97, False,
    )

    (r0, r1), (l0, l1) = column_blocks(mt)

    def patched(block, column):
        block = jnp.where(lane == 0, turn(x_first, -column), block)
        return jnp.where(lane == FP - 1, turn(x_last, FP - 1 - column), block)

    r0, r1 = patched(r0, FS - 1), patched(r1, FS - 2)
    l0, l1 = patched(l0, 0), patched(l1, 1)
    (sv_r, pv_r, film_r), (sv_l, pv_l, film_l) = flows(mt_old)

    def ends(column):
        return turn(low1, -column), turn(high1, FP - 1 - column)

    right_part = edge_part(r0, *ends(FS - 1), r1, 0.0, sv_r, pv_r, film_r)
    left_part = edge_part(l0, *ends(0), 0.0, l1, sv_l, pv_l, film_l)

    def corner_row(column):
        rows = []
        for i, x in enumerate((low1, high1)):
            spread = jnp.broadcast_to(x[:, column : column + 1], (FZ, FS))
            rows.append(
                jnp.sum(jnp.where(lane == sub + 8 * i, spread, 0.0), axis=0, keepdims=True)
            )
        return rows[0] + rows[1]

    rows = (0, 1, FP - 2, FP - 1)

    def stack(parts):
        return jnp.concatenate(list(parts) + [jnp.zeros((4, FS), F32)], axis=0)

    layer = {r: fluid2[0, r : r + 1, :] for r in (1, 2, FP - 3, FP - 2)}
    layer[-1], layer[0], layer[FP - 1], layer[FP] = (
        low1[0:1], x_first[0:1], x_last[0:1], high1[0:1],
    )
    here = stack(layer[r] for r in rows)
    above = stack([x_first[1:2], fluid2[1, 1:2, :], fluid2[1, FP - 2 : FP - 1, :], x_last[1:2]])
    f4 = stack(film[r : r + 1, :] for r in rows)
    factors = [stack(part[0, r : r + 1, :] for r in rows) for part in (toward, up, down)]
    before = jnp.where(lane == 0, 0.0, turn(here, 1))
    after = jnp.where(lane == FS - 1, 0.0, turn(here, -1))
    moved = f4 * (
        factored(
            here, stack(layer[r - 1] for r in rows), stack(layer[r + 1] for r in rows),
            before, after, here, above, *factors,
        )
        - WALL * f4 * here
    )
    direct = f4 * here
    a2, b3, h2 = sums[0:8, :], sums[8:16, :], sums[16:24, :]
    for i, r in enumerate(rows):
        hit = owner[r : r + 1, :] == sub.astype(F32)
        b3 = b3 + jnp.where(hit, moved[i : i + 1], 0.0)
        if r in (0, FP - 1):
            a2 = a2 + jnp.where(hit, direct[i : i + 1], 0.0)
    (film_bl, own_bl), (film_br, own_br) = edge_rows(recv, me)
    _, part_r = block_of(recv, me, 32)
    inside = lane < FP

    def shared(own_row, term):
        hit = (jnp.broadcast_to(own_row, (NB, FS)) == sub.astype(F32)) & inside
        return jnp.sum(jnp.where(hit, term, 0.0), axis=1, keepdims=True)

    right_term = film_br * turn(part_r, 64)[0:1] * r0[0:1] * keep_r
    left_term = film_bl * SPREAD * l0[0:1] * keep_l
    b3 = b3 + jnp.where(lane == 0, shared(own_br, right_term), 0.0)
    b3 = b3 + jnp.where(lane == FS - 1, shared(own_bl, left_term), 0.0)

    right_corner, left_corner = corner_row(FS - 1), corner_row(0)
    to_right = jnp.where(inside, r0, turn(right_part, 64))
    to_left = jnp.where(inside, l0, turn(left_part, 64))
    relay_lo, relay_hi = lo1(32, 40), hi1(32, 40)
    blank = jnp.zeros((2, FS), F32)
    for peer in range(NB):
        ahead = (me + 1 == peer).astype(F32)
        behind = (me - 1 == peer).astype(F32)
        out[place(peer, ORDER1), 0:8, :] = jnp.concatenate(
            [
                metal[1:2, :],
                b3[peer : peer + 1],
                h2[peer : peer + 1],
                relay_lo[peer : peer + 1],
                relay_hi[peer : peer + 1],
                right_corner * ahead + left_corner * behind,
                blank,
            ],
            axis=0,
        )
        out[place(peer, ORDER1), 8:16, :] = side[8:16, :]
        out[place(peer, ORDER1), 16:24, :] = a2
        out[place(peer, ORDER1), 24:32, :] = to_right * ahead + to_left * behind
    kept = (
        low1, low2, high1, high2, r0, l0, x_first, x_last,
        lo(16, 24), lo(32, 40), hi(16, 24), hi(32, 40), lo(40, 48), hi(40, 48),
    )
    for i, value in enumerate(kept):
        edge[8 * i : 8 * i + 8, :] = value


def last_kernel(
    recv1, recv, edge, side, metal, fluid2, toward, up, down, film, cond, owner,
    fluid_out, solid_out,
    tm, fluid3,
):
    me = lax.axis_index("blk")
    lane, sub = lanes(FZ), subs(FZ)
    (
        low1, low2, high1, high2, mine_right, mine_left, x_first, x_last,
        sv_lo, pv_lo, sv_hi, pv_hi, film_lo, film_hi,
    ) = [edge[8 * i : 8 * i + 8, :] for i in range(14)]
    left, right = block_of(recv1, me, 24, ORDER1)
    corner_l, corner_r = (block[5:6] for block in block_of(recv1, me, 0, ORDER1))
    part_l, part_r = block_of(recv, me, 32)
    c0, c1, h = rows_of(recv, 2, ORDER0), rows_of(recv, 3, ORDER0), side[16:24, :]
    tail, wall2, a2 = recv1[0, 0:8, :], recv1[0, 8:16, :], recv1[0, 16:24, :]
    for j in range(1, NB):
        tail = tail + recv1[j, 0:8, :]
        wall2 = wall2 + recv1[j, 8:16, :]
        a2 = a2 + recv1[j, 16:24, :]
    under2 = rows_of(recv1, 0, ORDER1)
    wall3 = strip_row(wall2, conduct_of(c0, wall2), under2, conduct_of(c1, under2))
    wall3 = wall3 + SOLID_STEP * (a2 - h * wall2)
    inflow3 = tail[1:2] + WALL * tail[2:3] * row_of(wall2, me) - row_of(h * wall3, me)

    new_l, new_r = halo_columns(
        turn(left, 64), turn(right, 64), turn(part_l, 64), turn(part_r, 64),
        edge_rows(recv, me), mine_right, mine_left, wall2, me,
    )
    tm[...] = jnp.zeros((FS, FS), F32)
    tm[pl.ds(0, FZ, stride=2), :] = right
    tm[pl.ds(1, FZ, stride=2), :] = left
    tm[pl.ds(32, FZ, stride=2), :] = new_r
    tm[pl.ds(33, FZ, stride=2), :] = new_l
    columns = tm[...].T[:FP]

    def corner(row, which):
        spread = jnp.broadcast_to(row, (FZ, FS))
        return jnp.sum(jnp.where(lane == sub + 8 * which, spread, 0.0), axis=1, keepdims=True)

    new_low = halo_row(
        low1, low2, x_first, corner(corner_l, 0), corner(corner_r, 0), sv_lo, pv_lo,
        film_lo[0:1] * (low1[0:1] - tail[3:4]),
    )
    new_high = halo_row(
        high1, x_last, high2, corner(corner_l, 1), corner(corner_r, 1), sv_hi, pv_hi,
        film_hi[0:1] * (high1[0:1] - tail[4:5]),
    )
    named, f = owner[...], film[...]
    source = [
        set_row(set_row(fluid2[z], x_first[z : z + 1], 0), x_last[z : z + 1], 1)
        for z in range(FZ)
    ]
    factors = (toward, up, down)
    advance(source, fluid3, low1, high1, columns, 0, factors, f, pick(named, wall2))
    walls3 = pick(named, wall3)
    advance(fluid3, fluid_out, new_low, new_high, columns, 32, factors, f, walls3)

    keep_l, keep_r = keeps(me)
    keep = jnp.where(lanes(SD) >= FS // 2, keep_l, keep_r)
    own, halo, c_halo = metal[0:SD, :], metal[SD : 2 * SD, :], metal[2 * SD : 3 * SD, :]
    own, halo = set_walls(own, halo, wall2, me, keep)
    own, halo = metal_step(own, halo, cond[...], c_halo, keep)
    own, halo = set_walls(own, halo, wall3, me, keep)
    own, _ = metal_step(own, halo, cond[...], c_halo, keep)
    solid_out[...] = own + jnp.where(subs(SD) == 0, SOLID_STEP * inflow3, 0.0)


def shape(*dims):
    return jax.ShapeDtypeStruct(dims, F32)


VMEM = pl.BlockSpec(memory_space=pltpu.VMEM)
GRANT = 54 * 1024 * 1024
HBM = pl.BlockSpec(memory_space=pltpu.HBM)


def call(kernel, outs, args, name, scratch=(), far=0, limit=32 * 1024 * 1024):
    return pl.pallas_call(
        kernel,
        out_shape=outs,
        in_specs=[HBM] * far + [VMEM] * (len(args) - far),
        out_specs=jax.tree.map(lambda _: VMEM, outs),
        scratch_shapes=scratch,
        name=name,
        compiler_params=pltpu.CompilerParams(vmem_limit_bytes=limit),
    )(*args)


def both_ways(first, second):
    count = lax.axis_size("sec")
    near = [(i, i ^ 1) for i in range(count)]
    far = [(i, (i + 1 if i % 2 else i - 1) % count) for i in range(count)]
    second = lax.ppermute(second, "sec", far)
    return lax.ppermute(first, "sec", near), second


def swap(message, order):
    count = lax.axis_size("sec")
    groups = [[NB * s + k for k in order[2 * s >= count]] for s in range(count)]
    return lax.all_to_all(
        message, ("sec", "blk"), split_axis=0, concat_axis=0, tiled=True, axis_index_groups=groups
    )


def two_exchanges(fluid, sv, pv, film, solid, cond, face_owner):
    owner = face_owner.reshape(1, FP)
    solid, cond = solid.reshape(SD, FS), cond.reshape(SD, FS)
    field, rows = shape(FZ, FP, FS), shape(ROWS, FS)
    held = [pltpu.VMEM((FZ, FP, FS), F32)] * 3
    held += [pltpu.VMEM((n, FS), F32) for n in (FP, SD, SD)]
    message, first, second, mt, owner = call(
        open_kernel,
        (shape(NB, R0, FS), rows, rows, shape(FS, FS), shape(FP, FS)),
        (fluid, sv, pv, film, solid, cond, owner),
        "open",
        held + [pltpu.VMEM((1, FP), jnp.int32), pltpu.SemaphoreType.DMA((10,))],
        far=7,
        limit=GRANT - OPEN_ROOM,
    )
    first_out, second_out = first, second
    first, second = both_ways(first, second)
    recv = swap(message, ORDER0)
    *factors, partial = call(
        prepare_kernel,
        (field,) * 4,
        (fluid, sv, pv, film),
        "prepare",
        [pltpu.VMEM((FZ, FP, FS), F32)] * 3 + [pltpu.SemaphoreType.DMA((3,))],
        far=3,
        limit=GRANT - PREPARE_ROOM,
    )
    fluid1, first_sent, second_sent, turned, side = call(
        first_kernel,
        (field, rows, rows, shape(FS, FS), shape(24, FS)),
        (recv, partial, *factors, film, solid, cond, owner, first, second, first_out),
        "first",
        [pltpu.VMEM((FS, FS), F32)],
    )
    first1, second1 = both_ways(first_sent, second_sent)
    fluid2, mt2, sums, metal = call(
        sums_kernel,
        (field, shape(FS, FS), shape(24, FS), shape(3 * SD, FS)),
        (fluid1, turned, side, *factors, film, solid, cond, owner),
        "sums",
    )
    message, edge = call(
        pack_kernel,
        (shape(NB, R1, FS), shape(14 * 8, FS)),
        (
            recv, mt, mt2, sums, metal, side, fluid1, fluid2, *factors, film, owner,
            first, second, first1, second1, first_sent,
        ),
        "pack",
    )
    recv1 = swap(message, ORDER1)
    fluid, solid = call(
        last_kernel,
        (field, shape(SD, FS)),
        (recv1, recv, edge, side, metal, fluid2, *factors, film, cond, owner),
        "last",
        [pltpu.VMEM((FS, FS), F32), pltpu.VMEM((FZ, FP, FS), F32)],
    )
    return fluid, solid.reshape(1, SD, FS)


def padded(block, sides, width, periodic):
    for axis, dim in sides:
        count = lax.axis_size(axis)
        forward = [(i, i + 1) for i in range(count - 1)]
        if periodic:
            forward.append((count - 1, 0))
        backward = [(target, source) for source, target in forward]
        low = lax.ppermute(
            lax.slice_in_dim(block, block.shape[dim] - width, None, axis=dim), axis, forward
        )
        high = lax.ppermute(lax.slice_in_dim(block, 0, width, axis=dim), axis, backward)
        block = jnp.concatenate([low, block, high], axis=dim)
    return block


def fluid_update(
    fluid, stream_velocity, pitch_velocity, wall_flux, pitch_extended, stream_extended
):
    pitch_prev = pitch_extended[:, :-2]
    pitch_next = pitch_extended[:, 2:]
    stream_prev = stream_extended[:, :, :-2]
    stream_next = stream_extended[:, :, 2:]
    span_prev = jnp.concatenate([fluid[:1], fluid[:-1]], 0)
    span_next = jnp.concatenate([fluid[1:], fluid[-1:]], 0)
    spread = SPREAD * (
        pitch_prev + pitch_next + stream_prev + stream_next + span_prev + span_next - 6.0 * fluid
    )
    carried = (
        -ADVECT * stream_velocity * (fluid - stream_prev)
        - ADVECT * jnp.maximum(pitch_velocity, 0.0) * (fluid - pitch_prev)
        + ADVECT * jnp.maximum(-pitch_velocity, 0.0) * (pitch_next - fluid)
    )
    updated = fluid + spread + carried
    return updated.at[0].add(-WALL * wall_flux)


def solid_update(solid, conduct, inflow, solid_extended, conduct_extended):
    stream_prev = solid_extended[..., :-2]
    stream_next = solid_extended[..., 2:]
    conduct_prev = conduct_extended[..., :-2]
    conduct_next = conduct_extended[..., 2:]
    depth_prev = jnp.concatenate([solid[:, :1], solid[:, :-1]], 1)
    depth_next = jnp.concatenate([solid[:, 1:], solid[:, -1:]], 1)
    kdepth_prev = jnp.concatenate([conduct[:, :1], conduct[:, :-1]], 1)
    kdepth_next = jnp.concatenate([conduct[:, 1:], conduct[:, -1:]], 1)
    flow = (
        0.5 * (conduct + conduct_prev) * (stream_prev - solid)
        + 0.5 * (conduct + conduct_next) * (stream_next - solid)
        + 0.5 * (conduct + kdepth_prev) * (depth_prev - solid)
        + 0.5 * (conduct + kdepth_next) * (depth_next - solid)
    )
    updated = solid + SOLID_STEP * flow
    updated = updated.at[:, 0].add(SOLID_STEP * inflow)
    updated = updated.at[:, -1].add(SOLID_STEP * COOLING * (COOLANT - solid[:, -1]))
    return updated


def local(
    fluid_temp, stream_velocity, pitch_velocity, film_coeff, solid_temp, conductivity, face_owner
):
    span_cells, pitch_cells, stream_cells = fluid_temp.shape
    depth_cells = solid_temp.shape[1]
    block_count = lax.axis_size("blk")
    capacity = max(2, (pitch_cells + block_count - 1) // block_count)
    owners = face_owner.reshape(-1)
    onehot = (owners[:, None] == jnp.arange(block_count, dtype=jnp.int32)[None, :]).astype(
        jnp.float32
    )
    same_owner = owners[:, None] == owners[None, :]
    earlier = lax.broadcasted_iota(jnp.int32, (pitch_cells, pitch_cells), 0) < lax.broadcasted_iota(
        jnp.int32, (pitch_cells, pitch_cells), 1
    )
    slot_rank = jnp.sum((same_owner & earlier).astype(jnp.int32), axis=0)
    slot_table = (slot_rank[None, :] == jnp.arange(capacity, dtype=jnp.int32)[:, None]).astype(
        jnp.float32
    )
    placing = onehot.T[:, None, :] * slot_table[None, :, :]
    fluid = fluid_temp
    solid = solid_temp
    gas_rows = span_cells * pitch_cells
    for subiter in range(SUB):
        wall_row = solid[0, 0:1, :]
        wall_temp = jnp.dot(
            onehot,
            lax.all_gather(wall_row, "blk", axis=0, tiled=True),
            precision=lax.Precision.HIGHEST,
            preferred_element_type=jnp.float32,
        )
        flux = film_coeff * (fluid[0] - wall_temp)
        outgoing = jnp.einsum("ocb,bf->ocf", placing, flux, precision=lax.Precision.HIGHEST)
        received = lax.all_to_all(outgoing, "blk", split_axis=0, concat_axis=0, tiled=True)
        inflow = jnp.sum(received, axis=(0, 1))
        conduct = conductivity * (1.0 + 0.25 * jnp.tanh(solid))
        stacked = jnp.concatenate([fluid.reshape(gas_rows, stream_cells), solid[0], conduct[0]], 0)
        stream_ext = padded(stacked, (("blk", 1),), 1, False)
        pitch_extended = padded(fluid, (("sec", 1),), 1, True)
        fluid_stream = stream_ext[:gas_rows].reshape(span_cells, pitch_cells, stream_cells + 2)
        solid_stream = stream_ext[gas_rows : gas_rows + depth_cells][None]
        conduct_stream = stream_ext[gas_rows + depth_cells :][None]
        fluid = fluid_update(
            fluid, stream_velocity, pitch_velocity, flux, pitch_extended, fluid_stream
        )
        solid = solid_update(solid, conduct, inflow[None, :], solid_stream, conduct_stream)
    return (fluid, solid)


def solution(mesh):
    placed = (
        P(None, "sec", "blk"),
        P(None, "sec", "blk"),
        P(None, "sec", "blk"),
        P("sec", "blk"),
        P("sec", None, "blk"),
        P("sec", None, "blk"),
        P("sec", "blk", None, None),
    )
    sizes = dict(mesh.shape)

    def chosen(*args):
        fits = args[0].shape == (FZ, FP, FS) and args[4].shape == (1, SD, FS)
        fits = fits and sizes["blk"] == NB and sizes["sec"] % 2 == 0
        return two_exchanges(*args) if fits else local(*args)

    return jax.shard_map(
        chosen,
        mesh=mesh,
        in_specs=placed,
        out_specs=(P(None, "sec", "blk"), P("sec", None, "blk")),
        check_vma=False,
    )
```
